32 devices in a mesh: dp: 4 (over y, x), blk: 8 (over z, core).
Axes of the slice: x: 2, y: 2, z: 4, core: 2. Of those that a mesh axis runs over, the one named last changes fastest.
Arguments:
- target: bfloat16 [16, 2048, 512], P('dp', 'blk'), may hold values from -6 to 6
- memory: bfloat16 [16, 2048, 512], P('dp', 'blk'), may hold values from -6 to 6
- target_seg: int32 [16, 2048], P('dp', 'blk'), may hold values from 0 to 2, as said below
- target_keep: int32 [16, 2048], P('dp', 'blk'), may hold values from 0 to 1, as said below
- memory_seg: int32 [16, 2048], P('dp', 'blk'), may hold values from 0 to 2, as said below
- memory_keep: int32 [16, 2048], P('dp', 'blk'), may hold values from 0 to 1, as said below
- cotangent: bfloat16 [16, 2048, 512], P('dp', 'blk'), may hold values from -6 to 6
- norm1_gain: float32 [512], replicated, may hold values from 0.5 to 1.5
- norm1_bias: float32 [512], replicated, may hold values from -3 to 3
- w_qkv: bfloat16 [512, 1536], replicated, may hold values from -0.25 to 0.25
- w_out: bfloat16 [512, 512], replicated, may hold values from -3 to 3
- norm2_gain: float32 [512], replicated, may hold values from 0.5 to 1.5
- norm2_bias: float32 [512], replicated, may hold values from -3 to 3
- w_cross_q: bfloat16 [512, 512], replicated, may hold values from -0.25 to 0.25
- w_cross_kv: bfloat16 [512, 1024], replicated, may hold values from -0.25 to 0.25
- w_cross_out: bfloat16 [512, 512], replicated, may hold values from -3 to 3
- norm3_gain: float32 [512], replicated, may hold values from 0.5 to 1.5
- norm3_bias: float32 [512], replicated, may hold values from -3 to 3
- w_up: bfloat16 [512, 2048], replicated, may hold values from -0.25 to 0.25
- b_up: float32 [2048], replicated, may hold values from -3 to 3
- w_down: bfloat16 [2048, 512], replicated, may hold values from -0.125 to 0.125
- b_down: float32 [512], replicated, may hold values from -2 to 2
Outputs:
- block_out: float32 [16, 2048, 512], P('dp', 'blk')
- target_grad: float32 [16, 2048, 512], P('dp', 'blk')
- memory_grad: float32 [16, 2048, 512], P('dp', 'blk')
- grad_norm1_gain: float32 [512], replicated
- grad_norm1_bias: float32 [512], replicated
- grad_w_qkv: float32 [512, 1536], replicated
- grad_w_out: float32 [512, 512], replicated
- grad_norm2_gain: float32 [512], replicated
- grad_norm2_bias: float32 [512], replicated
- grad_w_cross_q: float32 [512, 512], replicated
- grad_w_cross_kv: float32 [512, 1024], replicated
- grad_w_cross_out: float32 [512, 512], replicated
- grad_norm3_gain: float32 [512], replicated
- grad_norm3_bias: float32 [512], replicated
- grad_w_up: float32 [512, 2048], replicated
- grad_b_up: float32 [2048], replicated
- grad_w_down: float32 [2048, 512], replicated
- grad_b_down: float32 [512], replicated
The draws below stay inside these ranges and needn't reach their ends.
Inputs may be any that keep to these rules, and one draw needn't show every extreme that they name: `target_seg`: within a row, pair numbers never fall and every pair 0, 1, 2 is present; pair 1 runs from inside the first 256 tokens to inside the last 256. `target_keep`: padding is a run of one or more tokens at the end of each row, inside its pair 2, which keeps a real token. `memory_seg`: within a row, pair numbers never fall and every pair 0, 1, 2 is present; pair 1 runs from inside the first 256 tokens to inside the last 256. `memory_keep`: padding is a run of one or more tokens at the end of each row, inside its pair 2, which keeps a real token.
All inputs are finite; a program needn't handle non-finite values.
Results may differ from the reference program's by a relative error of at most 0.03.
Values may be sent and summed in bfloat16 or wider, within the bound.
No kernel may reach another device: no remote copies, remote signals or barrier semaphores. Data moves between devices by JAX's collectives and lax.ppermute only.
A program may use at most 256 MiB of HBM per device.

```python
from functools import partial
import jax
import jax.numpy as jnp
from jax import lax

D = 512
FF = 2048
HEADS = 8
ROW_LEN = 2048
MEM_LEN = 2048
TOK_ROW = 256
MEM_ROW = 256
ROWS = 16


def row_split(key, length, shard_len):
    key_first, key_second, key_padding = jax.random.split(key, 3)
    first_end = jax.random.randint(key_first, (ROWS,), 1, shard_len)
    second_end = jax.random.randint(key_second, (ROWS,), length - shard_len + 1, length - 1)
    padding = jax.random.randint(key_padding, (ROWS,), 1, length - second_end)
    position = jnp.arange(length)[None, :]
    segment = (position >= first_end[:, None]).astype(jnp.int32) + (position >= second_end[:, None]).astype(jnp.int32)
    kept_mask = (position < length - padding[:, None]).astype(jnp.int32)
    return (segment, kept_mask)


def draw_target_seg(key, part):
    segment, kept_mask = row_split(jax.random.fold_in(key, 11), ROW_LEN, TOK_ROW)
    return segment


def draw_target_keep(key, part):
    segment, kept_mask = row_split(jax.random.fold_in(key, 11), ROW_LEN, TOK_ROW)
    return kept_mask


def draw_memory_seg(key, part):
    segment, kept_mask = row_split(jax.random.fold_in(key, 12), MEM_LEN, MEM_ROW)
    return segment


def draw_memory_keep(key, part):
    segment, kept_mask = row_split(jax.random.fold_in(key, 12), MEM_LEN, MEM_ROW)
    return kept_mask


def levels(rng, shape, shards, low, high):
    gain, own = 1.0, jax.random.fold_in(rng, 6)
    for dim, parts in shards:
        steps = jnp.exp(jax.random.uniform(jax.random.fold_in(own, dim), (parts,), jnp.float32, low / len(shards), high / len(shards)))
        gain = gain * jnp.repeat(steps, shape[dim] // parts).reshape([-1 if axis == dim else 1 for axis in range(len(shape))])
    return gain


def scatter_about(stream_key, dims, width, limit, cuts=(), kind=jnp.bfloat16):
    drawn = width * jax.random.normal(stream_key, dims, jnp.float32)
    if cuts:
        drawn = drawn * levels(stream_key, dims, cuts, -0.22, 0.18)
    return jnp.clip(drawn, -limit, limit).astype(kind)


def setup_inputs(seed: int = 0) -> dict:
    key_list = jax.random.split(jax.random.key(seed), 23)
    return {
        "target": scatter_about(key_list[0], (ROWS, ROW_LEN, D), 1.0, 6.0, ((0, 4), (1, 8))),
        "memory": scatter_about(key_list[1], (ROWS, MEM_LEN, D), 1.0, 6.0, ((0, 4), (1, 8))),
        "target_seg": draw_target_seg(jax.random.fold_in(key_list[22], 71), 0),
        "target_keep": draw_target_keep(jax.random.fold_in(key_list[22], 71), 0),
        "memory_seg": draw_memory_seg(jax.random.fold_in(key_list[22], 71), 0),
        "memory_keep": draw_memory_keep(jax.random.fold_in(key_list[22], 71), 0),
        "cotangent": scatter_about(key_list[6], (ROWS, ROW_LEN, D), 1.0, 6.0, ((0, 4), (1, 8))),
        "norm1_gain": jnp.clip(1.0 + 0.1 * jax.random.normal(key_list[7], (D,), jnp.float32), 0.5, 1.5),
        "norm1_bias": scatter_about(key_list[8], (D,), 0.5, 3.0, (), jnp.float32),
        "w_qkv": scatter_about(key_list[9], (D, 3 * D), D ** -0.5, 0.25),
        "w_out": scatter_about(key_list[10], (D, D), (max(D // 128, 2)) ** -0.5, 3.0),
        "norm2_gain": jnp.clip(1.0 + 0.1 * jax.random.normal(key_list[11], (D,), jnp.float32), 0.5, 1.5),
        "norm2_bias": scatter_about(key_list[12], (D,), 0.5, 3.0, (), jnp.float32),
        "w_cross_q": scatter_about(key_list[13], (D, D), D ** -0.5, 0.25),
        "w_cross_kv": scatter_about(key_list[14], (D, 2 * D), D ** -0.5, 0.25),
        "w_cross_out": scatter_about(key_list[15], (D, D), (max(D // 128, 2)) ** -0.5, 3.0),
        "norm3_gain": jnp.clip(1.0 + 0.1 * jax.random.normal(key_list[16], (D,), jnp.float32), 0.5, 1.5),
        "norm3_bias": scatter_about(key_list[17], (D,), 0.5, 3.0, (), jnp.float32),
        "w_up": scatter_about(key_list[18], (D, FF), D ** -0.5, 0.25),
        "b_up": scatter_about(key_list[19], (FF,), 0.5, 3.0, (), jnp.float32),
        "w_down": scatter_about(key_list[20], (FF, D), FF ** -0.5, 0.125),
        "b_down": scatter_about(key_list[21], (D,), 0.3, 2.0, (), jnp.float32),
    }


@jax.custom_vjp
def low(v):
    return lax.optimization_barrier(v.astype(jnp.bfloat16)).astype(jnp.float32)

@jax.custom_vjp
def low_back(v):
    return v

def low_keep(v):
    return (low(v), None)

def low_pass(kept, grad):
    return (grad,)

def back_keep(v):
    return (v, None)

def back_low(kept, grad):
    return (low(grad),)
low.defvjp(low_keep, low_pass)
low_back.defvjp(back_keep, back_low)

def round_both(values):
    return low_back(low(values))

def product(left_side, right_side):
    return jnp.dot(left_side, right_side, precision=lax.Precision.HIGHEST)

def layer_norm(values, scale_gain, shift_bias):
    centered = values - lax.optimization_barrier(jnp.mean(values, axis=-1, keepdims=True))
    spread = lax.optimization_barrier(jnp.mean(centered * centered, axis=-1, keepdims=True))
    return centered * lax.rsqrt(spread + 1e-05) * scale_gain + shift_bias

def attention(queries, keys_now, values_now, query_seg, key_code):
    length = queries.shape[0]
    features = queries.shape[1]
    head_size = features // HEADS
    query_heads = queries.reshape(length, HEADS, head_size)
    key_heads = keys_now.reshape(keys_now.shape[0], HEADS, head_size)
    value_heads = values_now.reshape(values_now.shape[0], HEADS, head_size)
    scores = jnp.einsum('qhd,khd->hqk', query_heads, key_heads, precision=lax.Precision.HIGHEST) * head_size ** (-0.5)
    scores = low_back(scores)
    allowed = query_seg[None, :, None] == key_code[None, None, :]
    probability = jax.nn.softmax(jnp.where(allowed, scores, -1e+30), axis=-1)
    probability = low(probability)
    result = jnp.einsum('hqk,khd->qhd', probability, value_heads, precision=lax.Precision.HIGHEST)
    return result.reshape(length, features)

def one_row(weights_all, row_data):
    inputs, memory_row, query_seg, target_code, memory_code = row_data
    norm1_gain, norm1_bias, w_qkv, w_out, norm2_gain, norm2_bias, w_cross_q, w_cross_kv, w_cross_out, norm3_gain, norm3_bias, w_up, b_up, w_down, b_down = weights_all
    features = inputs.shape[-1]
    normed1 = low(layer_norm(inputs, norm1_gain, norm1_bias))
    projected = round_both(product(normed1, w_qkv))
    self_att = round_both(attention(projected[:, :features], projected[:, features:2 * features], projected[:, 2 * features:], query_seg, target_code))
    after_self = inputs + low_back(product(self_att, w_out))
    normed2 = low(layer_norm(after_self, norm2_gain, norm2_bias))
    cross_query = round_both(product(normed2, w_cross_q))
    memory_kv = round_both(product(memory_row, w_cross_kv))
    cross_att = round_both(attention(cross_query, memory_kv[:, :features], memory_kv[:, features:], query_seg, memory_code))
    after_cross = after_self + low_back(product(cross_att, w_cross_out))
    normed3 = low(layer_norm(after_cross, norm3_gain, norm3_bias))
    hidden = low_back(product(normed3, w_up) + b_up)
    activated = low(jax.nn.gelu(hidden))
    return after_cross + low_back(product(activated, w_down) + b_down)

def reference(target, memory, target_seg, target_keep, memory_seg, memory_keep, cotangent, norm1_gain, norm1_bias, w_qkv, w_out, norm2_gain, norm2_bias, w_cross_q, w_cross_kv, w_cross_out, norm3_gain, norm3_bias, w_up, b_up, w_down, b_down):
    target_code = jnp.where(target_keep == 1, target_seg, -1).astype(jnp.int32)
    memory_code = jnp.where(memory_keep == 1, memory_seg, -1).astype(jnp.int32)
    weights_all = tuple((item.astype(jnp.float32) for item in (norm1_gain, norm1_bias, w_qkv, w_out, norm2_gain, norm2_bias, w_cross_q, w_cross_kv, w_cross_out, norm3_gain, norm3_bias, w_up, b_up, w_down, b_down)))

    def forward(inputs, memory_all, weights_now):
        row_step = jax.checkpoint(partial(one_row, weights_now))
        return lax.map(row_step, (inputs, memory_all, target_seg, target_code, memory_code))
    block_out, backward = jax.vjp(forward, target.astype(jnp.float32), memory.astype(jnp.float32), weights_all)
    target_grad, memory_grad, weight_grads = backward(cotangent.astype(jnp.float32))
    g_norm1_gain, g_norm1_bias, g_w_qkv, g_w_out, g_norm2_gain, g_norm2_bias, g_w_cross_q, g_w_cross_kv, g_w_cross_out, g_norm3_gain, g_norm3_bias, g_w_up, g_b_up, g_w_down, g_b_down = weight_grads
    return (block_out, target_grad, memory_grad, g_norm1_gain, g_norm1_bias, g_w_qkv, g_w_out, g_norm2_gain, g_norm2_bias, g_w_cross_q, g_w_cross_kv, g_w_cross_out, g_norm3_gain, g_norm3_bias, g_w_up, g_b_up, g_w_down, g_b_down)
```

```python
import functools
import math

import jax
import jax.numpy as jnp
from jax import lax
from jax.experimental import pallas as pl
from jax.experimental.pallas import tpu as pltpu
from jax.sharding import PartitionSpec as P

HEADS = 8
NT = (((1,), (1,)), ((), ()))
NN = (((1,), (0,)), ((), ()))
TN = (((0,), (0,)), ((), ()))
f32 = jnp.float32
bf16 = jnp.bfloat16
VMEM = 60 * 1024 * 1024
QUERY_SCALE = 0.125 * math.log2(math.e)
HIDDEN_MASK = -1e30


def dot(left, right, dims=NN):
    return lax.dot_general(left, right, dims, preferred_element_type=f32)


def layer_norm(values, scale_gain, shift_bias):
    centered = values - jnp.mean(values, axis=-1, keepdims=True)
    spread = jnp.mean(centered * centered, axis=-1, keepdims=True)
    return centered * lax.rsqrt(spread + 1e-05) * scale_gain + shift_bias


def forward_kernel(q_ref, k_ref, v_ref, qmask_ref, kmask_ref, o_ref, lse_ref):
    low = lax.broadcasted_iota(jnp.int32, (1, 128), 1) < 64
    q, k, v = q_ref[...], k_ref[...], v_ref[...]
    qmask, kmask = qmask_ref[...], kmask_ref[...]
    outputs = []
    for head in range(2):
        mine = low if head == 0 else ~low
        scores = dot(jnp.where(mine, k, kmask), jnp.where(mine, q, qmask), NT)
        largest = jnp.max(scores, axis=0, keepdims=True)
        weights = jnp.exp2(scores - largest).astype(bf16)
        both = dot(jnp.where(mine, v, jnp.ones_like(v)), weights, TN)
        total = both[64 - head * 64 : 65 - head * 64]
        lse_ref[0, head : head + 1, :] = largest + jnp.log2(total)
        outputs.append(both[head * 64 : head * 64 + 64] / total)
    o_ref[...] = jnp.concatenate(outputs, 0).T.astype(bf16)


def attend(queries, keys, values, qmask, kmask):
    tokens, features = queries.shape
    length = keys.shape[0]
    pairs = features // 128
    of_queries = pl.BlockSpec((tokens, 128), lambda h: (0, h))
    of_keys = pl.BlockSpec((length, 128), lambda h: (0, h))
    return pl.pallas_call(
        forward_kernel,
        grid=(pairs,),
        in_specs=[
            of_queries,
            of_keys,
            of_keys,
            pl.BlockSpec((tokens, 128), lambda h: (0, 0)),
            pl.BlockSpec((length, 128), lambda h: (0, 0)),
        ],
        out_specs=[of_queries, pl.BlockSpec((1, 2, tokens), lambda h: (h, 0, 0))],
        out_shape=[
            jax.ShapeDtypeStruct((tokens, features), bf16),
            jax.ShapeDtypeStruct((pairs, 2, tokens), f32),
        ],
        compiler_params=pltpu.CompilerParams(vmem_limit_bytes=VMEM),
        cost_estimate=pl.CostEstimate(
            flops=HEADS * 4 * tokens * length * 128,
            bytes_accessed=2 * features * (2 * tokens + 2 * length),
            transcendentals=HEADS * tokens * length,
        ),
        name="attend",
    )(queries, keys, values, qmask, kmask)


def backward_kernel(
    chunk, q_ref, k_ref, v_ref, qmask_ref, kmask_ref, do_ref, o_ref, lse_ref, dq_ref, dk_ref, dv_ref
):
    low = lax.broadcasted_iota(jnp.int32, (1, 128), 1) < 64
    q, qmask, grad = q_ref[...], qmask_ref[...], do_ref[...]
    tokens, length = q.shape[0], k_ref.shape[0]
    product = grad.astype(f32) * o_ref[...].astype(f32)
    upper = product.astype(bf16)
    lower = (product - upper.astype(f32)).astype(bf16)
    rows = lax.broadcasted_iota(jnp.int32, (8, 128), 0)
    lanes = lax.broadcasted_iota(jnp.int32, (8, 128), 1)
    pick = jnp.where(rows == lanes // 64, 1.0, 0.0).astype(bf16)
    delta = dot(pick, upper, NT) + dot(pick, lower, NT)
    lse = lse_ref[0]
    zero = jnp.zeros_like(grad)
    q_heads = [jnp.where(low, q, qmask), jnp.where(low, qmask, q)]
    grad_heads = [jnp.where(low, grad, zero), jnp.where(low, zero, grad)]
    dq = [jnp.zeros((64, tokens), f32)] * 2
    for start in range(0, length, chunk):
        part = slice(start, start + chunk)
        k, v, kmask = k_ref[part, :], v_ref[part, :], kmask_ref[part, :]
        dk, dv = [], []
        for head in range(2):
            k_head = jnp.where(low, k, kmask) if head == 0 else jnp.where(low, kmask, k)
            weights = jnp.exp2(dot(k_head, q_heads[head], NT) - lse[head : head + 1, :])
            grad_weights = dot(v, grad_heads[head], NT)
            grad_scores = (weights * (grad_weights - delta[head : head + 1, :])).astype(bf16)
            dv.append(dot(weights.astype(bf16), grad))
            dk.append(dot(grad_scores, q))
            dq[head] = dq[head] + dot(k, grad_scores, TN)[head * 64 : head * 64 + 64]
        dk_ref[part, :] = (jnp.where(low, dk[0], dk[1]) * math.log(2.0)).astype(bf16)
        dv_ref[part, :] = jnp.where(low, dv[0], dv[1]).astype(bf16)
    dq_ref[...] = (jnp.concatenate(dq, 0).T * 0.125).astype(bf16)


def attend_back(queries, keys, values, qmask, kmask, grad, outputs, lse):
    tokens, features = queries.shape
    length = keys.shape[0]
    pairs = features // 128
    of_queries = pl.BlockSpec((tokens, 128), lambda h: (0, h))
    of_keys = pl.BlockSpec((length, 128), lambda h: (0, h))
    return pl.pallas_call(
        functools.partial(backward_kernel, min(1024, length)),
        grid=(pairs,),
        in_specs=[
            of_queries,
            of_keys,
            of_keys,
            pl.BlockSpec((tokens, 128), lambda h: (0, 0)),
            pl.BlockSpec((length, 128), lambda h: (0, 0)),
            of_queries,
            of_queries,
            pl.BlockSpec((1, 2, tokens), lambda h: (h, 0, 0)),
        ],
        out_specs=[of_queries, of_keys, of_keys],
        out_shape=[
            jax.ShapeDtypeStruct((tokens, features), bf16),
            jax.ShapeDtypeStruct((length, features), bf16),
            jax.ShapeDtypeStruct((length, features), bf16),
        ],
        compiler_params=pltpu.CompilerParams(vmem_limit_bytes=VMEM),
        cost_estimate=pl.CostEstimate(
            flops=HEADS * 10 * tokens * length * 128,
            bytes_accessed=2 * features * (4 * tokens + 4 * length),
            transcendentals=HEADS * tokens * length,
        ),
        name="attend_back",
    )(queries, keys, values, qmask, kmask, grad, outputs, lse)


class Layout:
    def __init__(self, rows, blocks):
        self.rows = rows
        self.share = blocks // rows
        index = lax.axis_index("blk")
        self.row = index // self.share

    def shift_rows(self, step):
        rows, share = self.rows, self.share
        return [
            (a * share + b, ((a + step) % rows) * share + b) for a in range(rows) for b in range(share)
        ]

    def shift_share(self, step):
        rows, share = self.rows, self.share
        return [
            (a * share + b, a * share + (b + step) % share) for a in range(rows) for b in range(share)
        ]

    def gather_row(self, values):
        parts = []
        for step in range(self.rows):
            wanted = lax.rem(self.row + step, self.rows)
            part = lax.dynamic_index_in_dim(values, wanted, 0, keepdims=False)
            if step:
                part = lax.ppermute(part, "blk", self.shift_rows(step))
            parts.append(part)
        return jnp.concatenate(parts, 0)

    def return_row(self, values):
        tokens, features = values.shape
        parts = values.reshape(self.rows, tokens // self.rows, features)
        result = jnp.zeros(parts.shape, f32)
        for step in range(self.rows):
            part = parts[step]
            if step:
                part = lax.ppermute(part.astype(bf16), "blk", self.shift_rows(self.rows - step))
            home = lax.rem(self.row + step, self.rows)
            result = lax.dynamic_update_index_in_dim(result, part.astype(f32), home, 0)
        return result

    def gather_share(self, values):
        parts = [values]
        for step in range(1, self.share):
            parts.append(lax.ppermute(values, "blk", self.shift_share(step)))
        return jnp.concatenate(parts, 0)

    def sum_share(self, values):
        tokens = values.shape[0] // self.share
        total = values[:tokens].astype(f32)
        for step in range(1, self.share):
            part = values[step * tokens : (step + 1) * tokens]
            total = total + lax.ppermute(part, "blk", self.shift_share(self.share - step)).astype(f32)
        return total.astype(bf16)


def query_mask(segments):
    lanes = lax.broadcasted_iota(jnp.int32, (1, 128), 1) % 64
    return jnp.where(segments[:, None] == lanes, 1.0, 0.0).astype(bf16)


def key_mask(codes):
    lanes = lax.broadcasted_iota(jnp.int32, (1, 128), 1) % 64
    return jnp.where((codes[:, None] != lanes) & (lanes < 3), HIDDEN_MASK, 0.0).astype(bf16)


def body(
    blocks,
    target,
    memory,
    target_seg,
    target_keep,
    memory_seg,
    memory_keep,
    cotangent,
    norm1_gain,
    norm1_bias,
    w_qkv,
    w_out,
    norm2_gain,
    norm2_bias,
    w_cross_q,
    w_cross_kv,
    w_cross_out,
    norm3_gain,
    norm3_bias,
    w_up,
    b_up,
    w_down,
    b_down,
):
    rows, length, features = target.shape
    layout = Layout(rows, blocks)
    packed = jnp.stack(
        [target_seg + 4 * (target_keep != 1), memory_seg + 4 * (memory_keep != 1)], axis=-1
    )
    target_row = layout.gather_row(target)
    packed_row = layout.gather_row(packed)
    packed_all = layout.gather_share(packed_row)
    memory_row = layout.gather_row(memory)
    grad_branch = layout.gather_row(cotangent)
    qmask = query_mask(packed_row[:, 0] % 4)
    self_kmask = key_mask(packed_all[:, 0])
    cross_kmask = key_mask(packed_all[:, 1])

    inputs = target_row.astype(f32)
    normed1, norm1_back = jax.vjp(layer_norm, inputs, norm1_gain, norm1_bias)
    normed1_low = normed1.astype(bf16)
    keyvals = dot(normed1_low, w_qkv[:, features:]).astype(bf16)
    keyvals = layout.gather_share(keyvals)
    queries = (dot(normed1_low, w_qkv[:, :features]) * QUERY_SCALE).astype(bf16)
    keys, values = keyvals[:, :features], keyvals[:, features:]
    memory_kv = layout.gather_share(dot(memory_row, w_cross_kv).astype(bf16))
    memory_keys, memory_values = memory_kv[:, :features], memory_kv[:, features:]

    self_low, self_lse = attend(queries, keys, values, qmask, self_kmask)
    after_self = inputs + dot(self_low, w_out)
    normed2, norm2_back = jax.vjp(layer_norm, after_self, norm2_gain, norm2_bias)
    normed2_low = normed2.astype(bf16)
    cross_query = (dot(normed2_low, w_cross_q) * QUERY_SCALE).astype(bf16)
    cross_low, cross_lse = attend(cross_query, memory_keys, memory_values, qmask, cross_kmask)
    after_cross = after_self + dot(cross_low, w_cross_out)
    normed3, norm3_back = jax.vjp(layer_norm, after_cross, norm3_gain, norm3_bias)
    normed3_low = normed3.astype(bf16)
    hidden = dot(normed3_low, w_up) + b_up
    activated, gelu_back = jax.vjp(jax.nn.gelu, hidden)
    activated_low = activated.astype(bf16)
    block_out = layout.return_row(after_cross + dot(activated_low, w_down) + b_down)

    grad_out = grad_branch.astype(f32)
    grad_w_down = dot(activated_low, grad_branch, TN)
    grad_b_down = jnp.sum(grad_out, axis=0)
    (grad_hidden,) = gelu_back(dot(grad_branch, w_down, NT))
    grad_hidden_low = grad_hidden.astype(bf16)
    grad_w_up = dot(normed3_low, grad_hidden_low, TN)
    grad_b_up = jnp.sum(grad_hidden_low.astype(f32), axis=0)
    grad_cross_side, grad_norm3_gain, grad_norm3_bias = norm3_back(dot(grad_hidden_low, w_up, NT))
    grad_after_cross = grad_out + grad_cross_side
    grad_cross_low = grad_after_cross.astype(bf16)
    grad_w_cross_out = dot(cross_low, grad_cross_low, TN)
    grad_cross_heads = dot(grad_cross_low, w_cross_out, NT).astype(bf16)

    grad_query_low, grad_mkeys, grad_mvalues = attend_back(
        cross_query, memory_keys, memory_values, qmask, cross_kmask, grad_cross_heads, cross_low, cross_lse
    )
    grad_memory_kv = layout.sum_share(jnp.concatenate([grad_mkeys, grad_mvalues], axis=1))
    grad_w_cross_kv = dot(memory_row, grad_memory_kv, TN)
    memory_grad = layout.return_row(dot(grad_memory_kv, w_cross_kv, NT))
    grad_w_cross_q = dot(normed2_low, grad_query_low, TN)
    grad_self_side, grad_norm2_gain, grad_norm2_bias = norm2_back(dot(grad_query_low, w_cross_q, NT))
    grad_after_self = grad_after_cross + grad_self_side
    grad_self_low = grad_after_self.astype(bf16)
    grad_w_out = dot(self_low, grad_self_low, TN)
    grad_self_heads = dot(grad_self_low, w_out, NT).astype(bf16)

    grad_query, grad_keys, grad_values = attend_back(
        queries, keys, values, qmask, self_kmask, grad_self_heads, self_low, self_lse
    )
    grad_keyvals = layout.sum_share(jnp.concatenate([grad_keys, grad_values], axis=1))
    grad_projected = jnp.concatenate([grad_query, grad_keyvals], axis=-1)
    grad_w_qkv = dot(normed1_low, grad_projected, TN)
    grad_input_side, grad_norm1_gain, grad_norm1_bias = norm1_back(dot(grad_projected, w_qkv, NT))
    target_grad = layout.return_row(grad_after_self + grad_input_side)

    everywhere = ("dp", "blk")

    def total_low(*grads):
        sums = lax.psum(tuple(grad.astype(bf16) for grad in grads), everywhere)
        return [grad.astype(f32) for grad in sums]

    grad_w_down, grad_w_up = total_low(grad_w_down, grad_w_up)
    (grad_w_cross_out, grad_w_cross_q, grad_w_cross_kv, grad_w_out, grad_w_qkv) = total_low(
        grad_w_cross_out, grad_w_cross_q, grad_w_cross_kv, grad_w_out, grad_w_qkv
    )
    (
        grad_norm1_gain,
        grad_norm1_bias,
        grad_norm2_gain,
        grad_norm2_bias,
        grad_norm3_gain,
        grad_norm3_bias,
        grad_b_up,
        grad_b_down,
    ) = lax.psum(
        (
            grad_norm1_gain,
            grad_norm1_bias,
            grad_norm2_gain,
            grad_norm2_bias,
            grad_norm3_gain,
            grad_norm3_bias,
            grad_b_up,
            grad_b_down,
        ),
        everywhere,
    )
    return (
        block_out,
        target_grad,
        memory_grad,
        grad_norm1_gain,
        grad_norm1_bias,
        grad_w_qkv,
        grad_w_out,
        grad_norm2_gain,
        grad_norm2_bias,
        grad_w_cross_q,
        grad_w_cross_kv,
        grad_w_cross_out,
        grad_norm3_gain,
        grad_norm3_bias,
        grad_w_up,
        grad_b_up,
        grad_w_down,
        grad_b_down,
    )


def solution(mesh):
    token = P("dp", "blk", None)
    code = P("dp", "blk")
    return jax.shard_map(
        functools.partial(body, mesh.shape["blk"]),
        mesh=mesh,
        in_specs=(token, token, code, code, code, code, token) + (P(),) * 15,
        out_specs=(token, token, token) + (P(),) * 15,
        check_vma=False,
    )
```

```python
import functools
import math

import jax
import jax.numpy as jnp
from jax import lax
from jax.experimental import pallas as pl
from jax.experimental.pallas import tpu as pltpu
from jax.sharding import PartitionSpec as P

HEADS = 8
NT = (((1,), (1,)), ((), ()))
NN = (((1,), (0,)), ((), ()))
TN = (((0,), (0,)), ((), ()))
f32 = jnp.float32
bf16 = jnp.bfloat16
VMEM = 60 * 1024 * 1024
QUERY_SCALE = 0.125 * math.log2(math.e)
HIDDEN_MASK = -1e30


def dot(left, right, dims=NN):
    return lax.dot_general(left, right, dims, preferred_element_type=f32)


def normalize(values):
    centered = values - jnp.mean(values, axis=1, keepdims=True)
    inverse = lax.rsqrt(jnp.mean(centered * centered, axis=1, keepdims=True) + 1e-05)
    return centered * inverse, inverse


def normalize_back(grad, normal, inverse, gain):
    grad = grad * gain
    shift = jnp.mean(grad, axis=1, keepdims=True)
    along = jnp.mean(grad * normal, axis=1, keepdims=True)
    return inverse * (grad - shift - normal * along)


def column_sums(values):
    return jnp.sum(values, axis=0, keepdims=True)


def whole(array, *index):
    shape = array.shape
    index = index or (0,) * len(shape)
    return pl.BlockSpec(shape, lambda *grid: index)


def shaped(shape, dtype=bf16):
    return jax.ShapeDtypeStruct(shape, dtype)


def run(kernel, name, operands, outs, flops, limit=60):
    specs, arrays = [], []
    for operand in operands:
        if isinstance(operand, tuple):
            array, width, column = operand
            specs.append(whole(shaped((array.shape[0], width)), 0, column))
        else:
            array = operand
            specs.append(whole(array))
        arrays.append(array)
    size = sum(item.size * item.dtype.itemsize for item in arrays + list(outs))
    return pl.pallas_call(
        kernel,
        grid=(1,),
        in_specs=specs,
        out_specs=[whole(out) for out in outs],
        out_shape=list(outs),
        compiler_params=pltpu.CompilerParams(vmem_limit_bytes=limit * 1024 * 1024),
        cost_estimate=pl.CostEstimate(flops=flops, bytes_accessed=size, transcendentals=0),
        name=name,
    )(*arrays)


def forward_kernel(parts, *refs):
    q_ref, qmask_ref = refs[:2]
    k_refs, v_refs, kmask_refs = (refs[2 + i * parts : 2 + (i + 1) * parts] for i in range(3))
    o_ref, lse_ref = refs[2 + 3 * parts :]
    low = lax.broadcasted_iota(jnp.int32, (1, 128), 1) < 64
    k = jnp.concatenate([ref[...] for ref in k_refs], 0)
    v = jnp.concatenate([ref[...] for ref in v_refs], 0)
    kmask = jnp.concatenate([ref[...] for ref in kmask_refs], 0)
    q, qmask = q_ref[...], qmask_ref[...]
    outputs = []
    for head in range(2):
        mine = low if head == 0 else ~low
        scores = dot(jnp.where(mine, k, kmask), jnp.where(mine, q, qmask), NT)
        largest = jnp.max(scores, axis=0, keepdims=True)
        weights = jnp.exp2(scores - largest).astype(bf16)
        both = dot(jnp.where(mine, v, jnp.ones_like(v)), weights, TN)
        total = both[64 - head * 64 : 65 - head * 64]
        lse_ref[0, head : head + 1, :] = largest + jnp.log2(total)
        outputs.append(both[head * 64 : head * 64 + 64] / total)
    o_ref[...] = jnp.concatenate(outputs, 0).T.astype(bf16)


def columns(rows, column, count):
    if callable(column):
        return [pl.BlockSpec((rows, 128), lambda h: (0, column(h)))] * count
    return [pl.BlockSpec((rows, 128), lambda h: (0, column))] * count


def attend(queries, qmask, keyvals, masks, mask_column):
    tokens, features = queries.shape
    parts = len(keyvals)
    length = parts * tokens
    pairs = features // 128
    of_queries = pl.BlockSpec((tokens, 128), lambda h: (0, h))
    return pl.pallas_call(
        functools.partial(forward_kernel, parts),
        grid=(pairs,),
        in_specs=[of_queries]
        + columns(tokens, 0, 1)
        + columns(tokens, lambda h: h, parts)
        + columns(tokens, lambda h: h + pairs, parts)
        + columns(tokens, mask_column, parts),
        out_specs=[of_queries, pl.BlockSpec((1, 2, tokens), lambda h: (h, 0, 0))],
        out_shape=[shaped((tokens, features)), shaped((pairs, 2, tokens), f32)],
        compiler_params=pltpu.CompilerParams(vmem_limit_bytes=VMEM),
        cost_estimate=pl.CostEstimate(
            flops=HEADS * 4 * tokens * length * 128,
            bytes_accessed=2 * features * (2 * tokens + 2 * length),
            transcendentals=HEADS * tokens * length,
        ),
        name="attend",
    )(queries, qmask, *keyvals, *keyvals, *masks)


def backward_kernel(parts, *refs):
    q_ref, qmask_ref, do_ref, o_ref, lse_ref = refs[:5]
    k_refs, v_refs, kmask_refs = (refs[5 + i * parts : 5 + (i + 1) * parts] for i in range(3))
    dq_ref, dkv_refs = refs[5 + 3 * parts], refs[6 + 3 * parts :]
    low = lax.broadcasted_iota(jnp.int32, (1, 128), 1) < 64
    q, qmask, grad = q_ref[...], qmask_ref[...], do_ref[...]
    tokens = q.shape[0]
    product = grad.astype(f32) * o_ref[...].astype(f32)
    upper = product.astype(bf16)
    lower = (product - upper.astype(f32)).astype(bf16)
    rows = lax.broadcasted_iota(jnp.int32, (8, 128), 0)
    lanes = lax.broadcasted_iota(jnp.int32, (8, 128), 1)
    pick = jnp.where(rows == lanes // 64, 1.0, 0.0).astype(bf16)
    delta = dot(pick, upper, NT) + dot(pick, lower, NT)
    lse = lse_ref[0]
    zero = jnp.zeros_like(grad)
    q_heads = [jnp.where(low, q, qmask), jnp.where(low, qmask, q)]
    grad_heads = [jnp.where(low, grad, zero), jnp.where(low, zero, grad)]
    dq = [jnp.zeros((64, tokens), f32)] * 2
    for part in range(parts):
        k, v = k_refs[part][...], v_refs[part][...]
        kmask = kmask_refs[part][...]
        dk, dv = [], []
        for head in range(2):
            k_head = jnp.where(low, k, kmask) if head == 0 else jnp.where(low, kmask, k)
            weights = jnp.exp2(dot(k_head, q_heads[head], NT) - lse[head : head + 1, :])
            grad_weights = dot(v, grad_heads[head], NT)
            grad_scores = (weights * (grad_weights - delta[head : head + 1, :])).astype(bf16)
            dv.append(dot(weights.astype(bf16), grad))
            dk.append(dot(grad_scores, q))
            dq[head] = dq[head] + dot(k, grad_scores, TN)[head * 64 : head * 64 + 64]
        dkv_refs[part][:, :128] = (jnp.where(low, dk[0], dk[1]) * math.log(2.0)).astype(bf16)
        dkv_refs[part][:, 128:] = jnp.where(low, dv[0], dv[1]).astype(bf16)
    dq_ref[...] = (jnp.concatenate(dq, 0).T * 0.125).astype(bf16)


def attend_back(queries, qmask, grad, outputs, lse, keyvals, masks, mask_column, first, count):
    tokens, features = queries.shape
    parts = len(keyvals)
    length = parts * tokens
    pairs = features // 128
    of_queries = pl.BlockSpec((tokens, 128), lambda h: (0, h + first))
    return pl.pallas_call(
        functools.partial(backward_kernel, parts),
        grid=(count,),
        in_specs=[
            of_queries,
            pl.BlockSpec((tokens, 128), lambda h: (0, 0)),
            of_queries,
            of_queries,
            pl.BlockSpec((1, 2, tokens), lambda h: (h + first, 0, 0)),
        ]
        + columns(tokens, lambda h: h + first, parts)
        + columns(tokens, lambda h: h + first + pairs, parts)
        + columns(tokens, mask_column, parts),
        out_specs=[pl.BlockSpec((tokens, 128), lambda h: (0, h))]
        + [pl.BlockSpec((tokens, 256), lambda h: (0, h))] * parts,
        out_shape=[shaped((tokens, count * 128))] + [shaped((tokens, count * 256))] * parts,
        compiler_params=pltpu.CompilerParams(vmem_limit_bytes=VMEM),
        cost_estimate=pl.CostEstimate(
            flops=count * 20 * tokens * length * 128,
            bytes_accessed=2 * count * 128 * (4 * tokens + 4 * length),
            transcendentals=2 * count * tokens * length,
        ),
        name="attend_back",
    )(queries, qmask, grad, outputs, lse, *keyvals, *keyvals, *masks)


def mask_rows(codes, of_queries):
    places = lax.broadcasted_iota(jnp.int32, (128, codes.shape[1]), 0) % 64
    codes = jnp.broadcast_to(codes.astype(jnp.int32), places.shape)
    if of_queries:
        mask = jnp.where(codes % 4 == places, 1.0, 0.0)
    else:
        mask = jnp.where((codes != places) & (places < 3), HIDDEN_MASK, 0.0)
    return mask.T.astype(bf16)


def project_kernel(parts, length, *refs):
    x_refs = refs[:parts]
    gain_ref, bias_ref, w_ref, x_ref, normed_ref, query_ref, keyvals_ref, qmask_ref = refs[parts:]
    features = x_ref.shape[1]
    for part in range(parts):
        rows = slice(part * length, (part + 1) * length)
        low = x_refs[part][:length, :]
        x_ref[rows, :] = low
        normal, inverse = normalize(low.astype(f32))
        normed = (normal * gain_ref[...] + bias_ref[...]).astype(bf16)
        normed_ref[rows, :] = normed
        projected = dot(normed, w_ref[...])
        query_ref[rows, :] = (projected[:, :features] * QUERY_SCALE).astype(bf16)
        keyvals_ref[rows, : 2 * features] = projected[:, features:].astype(bf16)
        codes = x_refs[part][length : length + 16, :].astype(f32)[0:1, :]
        qmask_ref[rows, :] = mask_rows(codes[:, :length], True)
        keyvals_ref[rows, 2 * features : 2 * features + 128] = mask_rows(codes[:, :length], False)
        keyvals_ref[rows, 2 * features + 128 :] = mask_rows(codes[:, length : 2 * length], False)


def row_specs(array, count):
    shape = (1,) + array.shape[1:]
    return [
        pl.BlockSpec(shape, lambda i, row, step=step: ((row[0] + step) % count, 0, 0)) for step in range(count)
    ]


def pack_target(row, target, codes):
    count, length, features = target.shape

    def kernel(row_ref, *refs):
        seg_ref, keep_ref, memory_seg_ref, memory_keep_ref = refs[count : count + 4]
        for step in range(count):
            out_ref = refs[count + 4 + step]
            out_ref[:length, :] = refs[step][0]
            which = pl.ds((row_ref[0] + step) % count, 1)
            pieces = [
                jnp.where(keep[which, :] == 1, seg[which, :], seg[which, :] + 4).astype(f32)
                for seg, keep in ((seg_ref, keep_ref), (memory_seg_ref, memory_keep_ref))
            ]
            if features > 2 * length:
                pieces.append(jnp.zeros((1, features - 2 * length), f32))
            pieces = jnp.concatenate(pieces, 1)
            out_ref[length:, :] = jnp.broadcast_to(pieces, (16, features)).astype(bf16)

    out = shaped((length + 16, features))
    return pl.pallas_call(
        kernel,
        grid_spec=pltpu.PrefetchScalarGridSpec(
            num_scalar_prefetch=1,
            grid=(1,),
            in_specs=row_specs(target, count) + [whole(item) for item in codes],
            out_specs=[whole(out)] * count,
        ),
        out_shape=[out] * count,
        compiler_params=pltpu.CompilerParams(vmem_limit_bytes=VMEM),
        name="pack_target",
    )(row.reshape(1), *[target] * count, *codes)


def pack_rows(row, arrays):
    count, length, features = arrays[0].shape
    total = count * len(arrays)

    def kernel(row_ref, *refs):
        for i in range(total):
            refs[total + i][...] = refs[i][0]

    out = shaped((length, features), arrays[0].dtype)
    outs = pl.pallas_call(
        kernel,
        grid_spec=pltpu.PrefetchScalarGridSpec(
            num_scalar_prefetch=1,
            grid=(1,),
            in_specs=[spec for array in arrays for spec in row_specs(array, count)],
            out_specs=[whole(out)] * total,
        ),
        out_shape=[out] * total,
        compiler_params=pltpu.CompilerParams(vmem_limit_bytes=VMEM),
        name="pack_rows",
    )(row.reshape(1), *[array for array in arrays for _ in range(count)])
    return [tuple(outs[i : i + count]) for i in range(0, total, count)]


def place_rows(row, parts):
    count = len(parts)
    length, features = parts[0].shape

    def kernel(row_ref, *refs):
        for step in range(count):

            @pl.when(pl.program_id(0) == step)
            def _():
                refs[count][0] = refs[step][...].astype(f32)

    return pl.pallas_call(
        kernel,
        grid_spec=pltpu.PrefetchScalarGridSpec(
            num_scalar_prefetch=1,
            grid=(count,),
            in_specs=[pl.BlockSpec((length, features), lambda i, row: (0, 0))] * count,
            out_specs=pl.BlockSpec((1, length, features), lambda i, row: ((row[0] + i) % count, 0, 0)),
        ),
        out_shape=shaped((count, length, features), f32),
        name="place_rows",
    )(row.reshape(1), *parts)


def unpack_feed(place, parts, hidden, block):
    share = len(parts)
    features = parts[0].shape[1]
    steps = hidden // block
    each = steps // share

    def kernel(place_ref, *refs):
        up_ref, down_ref = refs[share:]
        owner = pl.program_id(0) // each
        for step in range(share):

            @pl.when((place_ref[0] + share - owner) % share == step)
            def _():
                up_ref[...] = refs[step][:features, :].astype(f32)
                down_ref[...] = refs[step][features:, :].astype(f32)

    return pl.pallas_call(
        kernel,
        grid_spec=pltpu.PrefetchScalarGridSpec(
            num_scalar_prefetch=1,
            grid=(steps,),
            in_specs=[pl.BlockSpec((2 * features, features), lambda j, place: (j % each, 0))] * share,
            out_specs=[
                pl.BlockSpec((features, block), lambda j, place: (0, j)),
                pl.BlockSpec((block, features), lambda j, place: (j, 0)),
            ],
        ),
        out_shape=[shaped((features, hidden), f32), shaped((hidden, features), f32)],
        compiler_params=pltpu.CompilerParams(vmem_limit_bytes=VMEM),
        name="unpack_feed",
    )(place.reshape(1), *parts)


def unpack_columns(place, parts, widths):
    share = len(parts)
    rows = parts[0].shape[0]

    def kernel(place_ref, *refs):
        for step in range(share):

            @pl.when((place_ref[0] + share - pl.program_id(0)) % share == step)
            def _():
                start = 0
                for width, out_ref in zip(widths, refs[share:]):
                    out_ref[...] = refs[step][:, start : start + width].astype(f32)
                    start += width

    return pl.pallas_call(
        kernel,
        grid_spec=pltpu.PrefetchScalarGridSpec(
            num_scalar_prefetch=1,
            grid=(share,),
            in_specs=[pl.BlockSpec(part.shape, lambda j, place: (0, 0)) for part in parts],
            out_specs=[pl.BlockSpec((rows, width), lambda j, place: (j, 0)) for width in widths],
        ),
        out_shape=[shaped((share * rows, width), f32) for width in widths],
        compiler_params=pltpu.CompilerParams(vmem_limit_bytes=VMEM),
        name="unpack_columns",
    )(place.reshape(1), *parts)


def memory_kernel(parts, *refs):
    part_refs = refs[:parts]
    w_ref, memory_ref, keyvals_ref = refs[parts:]
    length = part_refs[0].shape[0]
    for part in range(parts):
        rows = slice(part * length, (part + 1) * length)
        memory = part_refs[part][...]
        memory_ref[rows, :] = memory
        keyvals_ref[rows, :] = dot(memory, w_ref[...]).astype(bf16)


def after_self_kernel(x_ref, attended_ref, w_out_ref, gain_ref, bias_ref, w_q_ref, after_ref, normed_ref, query_ref):
    after = x_ref[...].astype(f32) + dot(attended_ref[...], w_out_ref[...])
    after_ref[...] = after
    normal, inverse = normalize(after)
    normed = (normal * gain_ref[...] + bias_ref[...]).astype(bf16)
    normed_ref[...] = normed
    query_ref[...] = (dot(normed, w_q_ref[...]) * QUERY_SCALE).astype(bf16)


def feed_kernel(parts, share, each, place_ref, *refs):
    after_ref, attended_ref, w_out_ref, gain_ref, bias_ref, w_up_ref, b_up_ref, w_down_ref, b_down_ref = refs[:9]
    cotangent_refs, refs = refs[9 : 9 + parts], refs[9 + parts :]
    out_refs, grad_w_refs, refs = refs[:parts], refs[parts : parts + share], refs[parts + share :]
    grad_ref, grad_heads_ref, grad_out_ref, grad_b_up_ref, sums_ref = refs[:5]
    normed_ref, x_ref, total_ref, back_ref, cotangent_ref = refs[5:]
    features = w_up_ref.shape[0]
    length = out_refs[0].shape[0]
    step = pl.program_id(0)

    @pl.when(step == 0)
    def _():
        for part, part_ref in enumerate(cotangent_refs):
            cotangent_ref[part * length : (part + 1) * length, :] = part_ref[...]
        x = after_ref[...] + dot(attended_ref[...], w_out_ref[...])
        x_ref[...] = x
        total_ref[...] = x + b_down_ref[...]
        normal, inverse = normalize(x)
        normed_ref[...] = (normal * gain_ref[...] + bias_ref[...]).astype(bf16)
        back_ref[...] = jnp.zeros_like(back_ref)

    cotangent = cotangent_ref[...]
    normed, w_up, w_down = normed_ref[...], w_up_ref[...], w_down_ref[...]
    u = dot(normed, w_up) + b_up_ref[...]
    slope = math.sqrt(2.0 / math.pi)
    squared = u * u
    bent = jnp.tanh(u * (slope + slope * 0.044715 * squared))
    half = 0.5 + 0.5 * bent
    activated = (u * half).astype(bf16)
    gelu_slope = half + (0.5 * u) * (1.0 - bent * bent) * (slope + 3.0 * slope * 0.044715 * squared)
    total_ref[...] += dot(activated, w_down)
    grad_hidden = (dot(cotangent, w_down, NT) * gelu_slope).astype(bf16)
    grad_up = dot(normed, grad_hidden, TN).astype(bf16)
    grad_down = dot(activated, cotangent, TN).astype(bf16)
    for part, grad_w_ref in enumerate(grad_w_refs):

        @pl.when(step // each == share - 1 - part)
        def _():
            grad_w_ref[:features, :] = grad_up
            grad_w_ref[features:, :] = grad_down

    grad_b_up_ref[...] = column_sums(grad_hidden.astype(f32))
    back_ref[...] += dot(grad_hidden, w_up, NT)

    @pl.when(step == pl.num_programs(0) - 1)
    def _():
        for part, out_ref in enumerate(out_refs):
            out_ref[...] = total_ref[part * length : (part + 1) * length, :].astype(bf16)
        normal, inverse = normalize(x_ref[...])
        grad_normed = back_ref[...]
        grad_out = cotangent.astype(f32)
        sums_ref[0:1, :] = column_sums(grad_normed * normal)
        sums_ref[1:2, :] = column_sums(grad_normed)
        sums_ref[2:3, :] = column_sums(grad_out)
        grad = grad_out + normalize_back(grad_normed, normal, inverse, gain_ref[...])
        grad_ref[...] = grad
        low = grad.astype(bf16)
        grad_heads_ref[...] = dot(low, w_out_ref[...], NT).astype(bf16)
        grad_out_ref[...] = dot(attended_ref[...], low, TN).astype(bf16)


def feed_forward(place, share, after_self, attended, cotangents, w_out, gain, bias, w_up, b_up, w_down, b_down):
    tokens, features = after_self.shape
    hidden = w_up.shape[1]
    block = features
    parts = len(cotangents)
    length = tokens // parts
    steps = hidden // block
    each = steps // share
    row, one, square = shaped((tokens, features)), shaped((1, features)), shaped((features, features))
    part_row = shaped((length, features))

    def now(j, place):
        return ((place[0] + share - 1 - j // each) % share) * each + j % each

    def grad_spec(part):
        begin = (share - 1 - part) * each
        return pl.BlockSpec(
            (features + block, features), lambda j, place: (jnp.clip(j - begin, 0, each - 1), 0)
        )

    return pl.pallas_call(
        functools.partial(feed_kernel, parts, share, each),
        grid_spec=pltpu.PrefetchScalarGridSpec(
            num_scalar_prefetch=1,
            grid=(steps,),
            in_specs=[
                whole(row),
                whole(row),
                whole(square),
                whole(one),
                whole(one),
                pl.BlockSpec((features, block), lambda j, place: (0, now(j, place))),
                pl.BlockSpec((1, block), lambda j, place: (0, now(j, place))),
                pl.BlockSpec((block, features), lambda j, place: (now(j, place), 0)),
                whole(one),
            ]
            + [whole(part_row)] * parts,
            out_specs=[whole(part_row)] * parts
            + [grad_spec(part) for part in range(share)]
            + [
                whole(row),
                whole(row),
                whole(square),
                pl.BlockSpec((1, block), lambda j, place: (0, now(j, place))),
                whole(shaped((8, features))),
            ],
            scratch_shapes=[
                pltpu.VMEM((tokens, features), bf16),
                pltpu.VMEM((tokens, features), f32),
                pltpu.VMEM((tokens, features), f32),
                pltpu.VMEM((tokens, features), f32),
                pltpu.VMEM((tokens, features), bf16),
            ],
        ),
        out_shape=[part_row] * parts
        + [shaped((each * (features + block), features))] * share
        + [
            shaped((tokens, features), f32),
            row,
            square,
            shaped((1, hidden), f32),
            shaped((8, features), f32),
        ],
        compiler_params=pltpu.CompilerParams(vmem_limit_bytes=VMEM),
        cost_estimate=pl.CostEstimate(
            flops=2 * tokens * features * (6 * hidden + 3 * features),
            bytes_accessed=12 * features * hidden + 20 * tokens * features,
            transcendentals=tokens * hidden,
        ),
        name="feed_forward",
    )(place.reshape(1), after_self, attended, w_out, gain, bias, w_up, b_up, w_down, b_down, *cotangents)


def after_self_back_kernel(calls, *refs):
    dq_refs = refs[:calls]
    after_ref, normed_ref, attended_ref, grad_after_ref, gain_ref, w_q_ref, w_out_ref = refs[calls : calls + 7]
    grad_ref, grad_heads_ref, grad_w_ref, sums_ref = refs[calls + 7 :]
    features = after_ref.shape[1]
    grad_query = jnp.concatenate([ref[...] for ref in dq_refs], 1)
    grad_normed = dot(grad_query, w_q_ref[...], NT)
    normal, inverse = normalize(after_ref[...])
    sums_ref[0:1, :] = column_sums(grad_normed * normal)
    sums_ref[1:2, :] = column_sums(grad_normed)
    grad = grad_after_ref[...] + normalize_back(grad_normed, normal, inverse, gain_ref[...])
    grad_ref[...] = grad
    low = grad.astype(bf16)
    grad_heads_ref[...] = dot(low, w_out_ref[...], NT).astype(bf16)
    grad_w_ref[:, :features] = dot(normed_ref[...], grad_query, TN).astype(bf16)
    grad_w_ref[:, features:] = dot(attended_ref[...], low, TN).astype(bf16)


def summed_keyvals(refs):
    keys, values = [], []
    for call in refs:
        total = sum([ref[...].astype(f32) for ref in call[1:]], call[0][...].astype(f32)).astype(bf16)
        for pair in range(total.shape[1] // 256):
            keys.append(total[:, pair * 256 : pair * 256 + 128])
            values.append(total[:, pair * 256 + 128 : pair * 256 + 256])
    return keys + values


def memory_back_kernel(calls, parts, *refs):
    grad_refs = [refs[call * parts : (call + 1) * parts] for call in range(calls)]
    memory_ref, w_ref, out_ref, pair_ref, grad_w_ref = refs[calls * parts : calls * parts + 5]
    row_refs = refs[calls * parts + 5 :]
    features = out_ref.shape[1]
    grad = jnp.concatenate(summed_keyvals(grad_refs), 1)
    result = dot(grad, w_ref[...], NT).astype(bf16)
    length = row_refs[0].shape[0]
    for part, row_ref in enumerate(row_refs):
        row_ref[...] = result[part * length : (part + 1) * length, :]
    grad_w_ref[:, :features] = out_ref[...]
    grad_w_ref[:, features : 3 * features] = pair_ref[...]
    grad_w_ref[:, 3 * features :] = dot(memory_ref[...], grad, TN).astype(bf16)


def project_back_kernel(calls, parts, *refs):
    dq_refs = refs[:calls]
    refs = refs[calls:]
    grad_refs = [refs[call * parts : (call + 1) * parts] for call in range(calls)]
    refs = refs[calls * parts :]
    x_ref, normed_ref, gain_ref, w_ref, grad_after_ref, second_ref, third_ref, b_up_ref, grad_w_ref, sums_ref = refs[:10]
    row_refs = refs[10:]
    grad = jnp.concatenate([ref[...] for ref in dq_refs] + summed_keyvals(grad_refs), 1)
    grad_w_ref[...] = dot(normed_ref[...], grad, TN).astype(bf16)
    grad_normed = dot(grad, w_ref[...], NT)
    normal, inverse = normalize(x_ref[...].astype(f32))
    result = grad_after_ref[...] + normalize_back(grad_normed, normal, inverse, gain_ref[...])
    length = row_refs[0].shape[0]
    for part, row_ref in enumerate(row_refs):
        row_ref[...] = result[part * length : (part + 1) * length, :].astype(bf16)
    sums_ref[...] = jnp.zeros_like(sums_ref)
    width, features = sums_ref.shape[1], x_ref.shape[1]
    pieces = [column_sums(grad_normed * normal), column_sums(grad_normed), second_ref[0:1, :], second_ref[1:2, :]]
    pieces += [third_ref[0:1, :], third_ref[1:2, :], third_ref[2:3, :]]
    pieces += [b_up_ref[:, i : i + features] for i in range(0, b_up_ref.shape[1], features)]
    for i, piece in enumerate(pieces):
        row, column = divmod(i * features, width)
        sums_ref[row : row + 1, column : column + features] = piece.astype(bf16)


class Layout:
    def __init__(self, dp, rows, blocks):
        self.rows = rows
        self.share = share = blocks // rows
        self.blocks = blocks
        self.dp = dp
        place = lax.axis_index("blk")
        self.row = place // share
        self.place = lax.rem(place, share)

    def shift_rows(self, step):
        rows, share = self.rows, self.share
        return [
            (a * share + b, ((a + step) % rows) * share + b) for a in range(rows) for b in range(share)
        ]

    def shift_share(self, step):
        rows, share = self.rows, self.share
        return [
            (a * share + b, a * share + (b + step) % share) for a in range(rows) for b in range(share)
        ]

    def bring_rows(self, parts):
        return (parts[0],) + tuple(
            lax.ppermute(parts[step], "blk", self.shift_rows(step)) for step in range(1, self.rows)
        )

    def return_rows(self, parts):
        return (parts[0],) + tuple(
            lax.ppermute(parts[step], "blk", self.shift_rows(self.rows - step)) for step in range(1, self.rows)
        )

    def gather_share(self, values):
        return (values,) + tuple(
            lax.ppermute(values, "blk", self.shift_share(step)) for step in range(1, self.share)
        )

    def return_share(self, parts):
        return (parts[0],) + tuple(
            lax.ppermute(parts[step], "blk", self.shift_share(self.share - step))
            for step in range(1, self.share)
        )


class Sum:
    def __init__(self, layout, values, extra=None):
        share, rows, dp = layout.share, layout.rows, layout.dp
        place = lax.axis_index("blk")
        levels = [
            ("blk", share, lax.rem(place, share), layout.shift_share),
            ("dp", dp, lax.axis_index("dp"), lambda step: [(d, (d + step) % dp) for d in range(dp)]),
            ("blk", rows, place // share, layout.shift_rows),
        ]
        self.values = values
        self.extra = extra
        self.left = [(self.scatter,) + level for level in levels]
        self.left += [(self.gather,) + level for level in reversed(levels)]

    def scatter(self, axis, count, index, shift):
        if isinstance(self.values, tuple):
            parts = self.values
            total = parts[0].astype(f32)
            for step in range(1, count):
                total = total + lax.ppermute(parts[step], axis, shift(step)).astype(f32)
            self.values = total.astype(bf16)
            return
        part_rows = self.values.shape[0] // count

        def part(which):
            return lax.dynamic_slice_in_dim(self.values, which * part_rows, part_rows, 0)

        total = part(index).astype(f32)
        extra = None if self.extra is None else self.extra.astype(f32)
        arrived = []
        for step in range(1, count):
            send = part(lax.rem(index + step, count))
            if extra is not None:
                send = jnp.concatenate([send, self.extra], 0)
            arrived.append(lax.ppermute(send, axis, shift(step)))
        for item in arrived:
            total = total + item[:part_rows].astype(f32)
            if extra is not None:
                extra = extra + item[part_rows:].astype(f32)
        self.values = total.astype(bf16)
        if extra is not None:
            self.extra = extra.astype(bf16)

    def gather(self, axis, count, index, shift):
        mine = self.values
        part_rows = mine.shape[0]
        arrived = [lax.ppermute(mine, axis, shift(step)) for step in range(1, count)]
        if not self.left:
            self.values = (mine, *arrived)
            return
        result = jnp.zeros((count * part_rows, mine.shape[1]), mine.dtype)
        result = lax.dynamic_update_slice_in_dim(result, mine, index * part_rows, 0)
        for step, item in enumerate(arrived, 1):
            source = lax.rem(index + count - step, count)
            result = lax.dynamic_update_slice_in_dim(result, item, source * part_rows, 0)
        self.values = result

    def step(self):
        action = self.left.pop(0)
        action[0](*action[1:])


def join(*values):
    return lax.optimization_barrier(values)


def body(
    dp,
    blocks,
    target,
    memory,
    target_seg,
    target_keep,
    memory_seg,
    memory_keep,
    cotangent,
    norm1_gain,
    norm1_bias,
    w_qkv,
    w_out,
    norm2_gain,
    norm2_bias,
    w_cross_q,
    w_cross_kv,
    w_cross_out,
    norm3_gain,
    norm3_bias,
    w_up,
    b_up,
    w_down,
    b_down,
):
    rows, length, features = target.shape
    tokens = rows * length
    layout = Layout(dp, rows, blocks)
    target_parts = pack_target(layout.row, target, (target_seg, target_keep, memory_seg, memory_keep))
    target_parts = layout.bring_rows(target_parts)
    memory_parts, cotangent_parts = pack_rows(layout.row, (memory, cotangent))
    norm1_gain, norm1_bias, norm2_gain, norm2_bias, norm3_gain, norm3_bias, b_up, b_down = (
        item.reshape(1, -1)
        for item in (norm1_gain, norm1_bias, norm2_gain, norm2_bias, norm3_gain, norm3_bias, b_up, b_down)
    )
    hidden = w_up.shape[1]
    row, wide_row, full_row = (shaped((tokens, features)), shaped((tokens, 2 * features)), shaped((tokens, features), f32))
    row_parts = (shaped((length, features)),) * rows
    sums = shaped((8, features), f32)
    unit = 2 * tokens * features * features
    pairs = features // 128

    x, normed1, queries, keyvals, qmask = run(
        functools.partial(project_kernel, rows, length),
        "project",
        target_parts + (norm1_gain, norm1_bias, w_qkv),
        (row, row, row, shaped((tokens, 2 * features + 256)), shaped((tokens, 128))),
        3 * unit,
    )
    keyvals, memory_parts = join(keyvals, memory_parts)
    keyvals = layout.gather_share(keyvals)
    memory_parts = layout.bring_rows(memory_parts)
    self_masks = (keyvals, 2 * pairs)
    cross_masks = (keyvals, 2 * pairs + 1)
    self_low, self_lse = attend(queries, qmask, keyvals, *self_masks)
    self_low, memory_parts, cotangent_parts = join(self_low, memory_parts, cotangent_parts)
    memory_row, memory_keyvals = run(
        functools.partial(memory_kernel, rows), "memory", memory_parts + (w_cross_kv,), (row, wide_row), 2 * unit
    )
    memory_keyvals = layout.gather_share(memory_keyvals)
    after_self, normed2, cross_query = run(
        after_self_kernel,
        "after_self",
        (x, self_low, w_out, norm2_gain, norm2_bias, w_cross_q),
        (full_row, row, row),
        2 * unit,
    )
    cross_query, cotangent_parts, memory_keyvals = join(cross_query, cotangent_parts, memory_keyvals)
    cotangent_parts = layout.bring_rows(cotangent_parts)
    cross_low, cross_lse = attend(cross_query, qmask, memory_keyvals, *cross_masks)
    cross_low, cotangent_parts = join(cross_low, cotangent_parts)
    fed = feed_forward(
        layout.place,
        layout.share,
        after_self,
        cross_low,
        cotangent_parts,
        w_cross_out,
        norm3_gain,
        norm3_bias,
        w_up,
        b_up,
        w_down,
        b_down,
    )
    block_parts, grad_feed = tuple(fed[:rows]), tuple(fed[rows : rows + layout.share])
    grad_after_cross, grad_cross_heads, grad_w_cross_out, grad_b_up, sums3 = fed[rows + layout.share :]

    calls = 2
    count = pairs // calls
    first = Sum(layout, grad_feed)
    operands = (cross_query, qmask, grad_cross_heads, cross_low, cross_lse, memory_keyvals) + cross_masks[:1]
    first.step()
    block_parts = layout.return_rows(block_parts)
    dq, *dkv = attend_back(*operands, cross_masks[1], 0, count)
    operands, first.values, block_parts, dq, dkv = join(operands, first.values, block_parts, dq, dkv)
    cross_grads, cross_share = [dq], list(layout.return_share(dkv))
    first.step()
    dq, *dkv = attend_back(*operands, cross_masks[1], count, count)
    first.values, dq, dkv, cross_share = join(first.values, dq, dkv, cross_share)
    cross_grads.append(dq)
    cross_share += layout.return_share(dkv)
    first.step()
    grad_after_self, grad_self_heads, grad_w_pair, sums2 = run(
        functools.partial(after_self_back_kernel, calls),
        "after_self_back",
        tuple(cross_grads) + (after_self, normed2, self_low, grad_after_cross, norm2_gain, w_cross_q, w_out),
        (full_row, row, shaped((features, 2 * features)), sums),
        4 * unit,
    )
    cross_share, first.values, grad_w_pair = join(cross_share, first.values, grad_w_pair)
    first.step()
    grad_w_part, *memory_parts = run(
        functools.partial(memory_back_kernel, calls, layout.share),
        "memory_back",
        tuple(cross_share) + (memory_row, w_cross_kv, grad_w_cross_out, grad_w_pair),
        (shaped((features, 5 * features)),) + row_parts,
        4 * unit,
    )
    middle = Sum(layout, grad_w_part)

    operands = (queries, qmask, grad_self_heads, self_low, self_lse, keyvals)
    operands, middle.values, memory_parts, first.values = join(operands, middle.values, memory_parts, first.values)
    memory_parts = layout.return_rows(memory_parts)
    first.step()
    middle.step()
    dq, *dkv = attend_back(*operands, *self_masks, 0, count)
    operands, first.values, middle.values, memory_parts, dq, dkv = join(
        operands, first.values, middle.values, memory_parts, dq, dkv
    )
    self_grads, self_share = [dq], list(layout.return_share(dkv))
    first.step()
    middle.step()
    dq, *dkv = attend_back(*operands, *self_masks, count, count)
    first.values, middle.values, dq, dkv, self_share = join(first.values, middle.values, dq, dkv, self_share)
    self_grads.append(dq)
    self_share += layout.return_share(dkv)
    extra_rows = -(-(7 * features + hidden) // (16 * 3 * features)) * 16
    grad_w_qkv, small, *target_parts = run(
        functools.partial(project_back_kernel, calls, layout.share),
        "project_back",
        tuple(self_grads)
        + tuple(self_share)
        + (x, normed1, norm1_gain, w_qkv, grad_after_self, sums2, sums3, grad_b_up),
        (shaped((features, 3 * features)), shaped((extra_rows, 3 * features))) + row_parts,
        6 * unit,
    )
    last = Sum(layout, grad_w_qkv, small)
    last.step()
    last.values, first.values = join(last.values, first.values)
    grad_w_up, grad_w_down = unpack_feed(layout.place, first.values, hidden, features)
    last.step()
    last.values, grad_w_up, grad_w_down, block_parts = join(last.values, grad_w_up, grad_w_down, block_parts)
    last.values = jnp.concatenate([middle.values, last.values], 1)
    last.extra = jnp.pad(last.extra, ((0, 0), (0, middle.values.shape[1])))
    last.step()
    block_out = place_rows(layout.row, block_parts)
    last.values, block_out, memory_parts, target_parts = join(last.values, block_out, memory_parts, target_parts)
    last.step()
    memory_grad = place_rows(layout.row, memory_parts)
    last.values, memory_grad, target_parts = join(last.values, memory_grad, target_parts)
    target_parts = layout.return_rows(target_parts)
    last.step()
    last.values, target_parts = join(last.values, target_parts)
    last.step()
    target_grad = place_rows(layout.row, target_parts)
    grad_w_cross_out, grad_w_cross_q, grad_w_out, grad_w_cross_kv, grad_w_qkv = unpack_columns(
        layout.place, last.values, [features, features, features, 2 * features, 3 * features]
    )
    small = last.extra[:, : 3 * features].reshape(-1)[: 7 * features + hidden].astype(f32)
    (
        grad_norm1_gain,
        grad_norm1_bias,
        grad_norm2_gain,
        grad_norm2_bias,
        grad_norm3_gain,
        grad_norm3_bias,
        grad_b_down,
    ) = [small[i * features : (i + 1) * features] for i in range(7)]
    grad_b_up = small[7 * features :]
    return (
        block_out,
        target_grad,
        memory_grad,
        grad_norm1_gain,
        grad_norm1_bias,
        grad_w_qkv,
        grad_w_out,
        grad_norm2_gain,
        grad_norm2_bias,
        grad_w_cross_q,
        grad_w_cross_kv,
        grad_w_cross_out,
        grad_norm3_gain,
        grad_norm3_bias,
        grad_w_up,
        grad_b_up,
        grad_w_down,
        grad_b_down,
    )


def solution(mesh):
    token = P("dp", "blk", None)
    code = P("dp", "blk")
    return jax.shard_map(
        functools.partial(body, mesh.shape["dp"], mesh.shape["blk"]),
        mesh=mesh,
        in_specs=(token, token, code, code, code, code, token) + (P(),) * 15,
        out_specs=(token, token, token) + (P(),) * 15,
        check_vma=False,
    )
```

```python
import functools
import math

import jax
import jax.numpy as jnp
from jax import lax
from jax.experimental import pallas as pl
from jax.experimental.pallas import tpu as pltpu
from jax.sharding import PartitionSpec as P

HEADS = 8
NT = (((1,), (1,)), ((), ()))
NN = (((1,), (0,)), ((), ()))
TN = (((0,), (0,)), ((), ()))
f32 = jnp.float32
bf16 = jnp.bfloat16
VMEM = 60 * 1024 * 1024
SMALL = pl.CostEstimate(flops=1, bytes_accessed=1, transcendentals=0)
QUERY_SCALE = 0.125 * math.log2(math.e)
HIDDEN_MASK = -1e30


def dot(left, right, dims=NN):
    return lax.dot_general(left, right, dims, preferred_element_type=f32)


def normalize(values):
    centered = values - jnp.mean(values, axis=1, keepdims=True)
    inverse = lax.rsqrt(jnp.mean(centered * centered, axis=1, keepdims=True) + 1e-05)
    return centered * inverse, inverse


def normalize_back(grad, normal, inverse, gain):
    grad = grad * gain
    shift = jnp.mean(grad, axis=1, keepdims=True)
    along = jnp.mean(grad * normal, axis=1, keepdims=True)
    return inverse * (grad - shift - normal * along)


def column_sums(values):
    return jnp.sum(values, axis=0, keepdims=True)


def whole(array, *index):
    shape = array.shape
    index = index or (0,) * len(shape)
    return pl.BlockSpec(shape, lambda *grid: index)


def shaped(shape, dtype=bf16):
    return jax.ShapeDtypeStruct(shape, dtype)


def run(kernel, name, operands, outs, place=None, scratch=()):
    specs = [whole(array) for array in operands]
    if place is not None:
        specs = [pl.BlockSpec(memory_space=pltpu.SMEM)] + specs
        operands = (place.reshape(1), *operands)
    return pl.pallas_call(
        kernel,
        grid=(1,),
        in_specs=specs,
        out_specs=[whole(out) for out in outs],
        out_shape=list(outs),
        scratch_shapes=list(scratch),
        compiler_params=pltpu.CompilerParams(vmem_limit_bytes=VMEM),
        cost_estimate=SMALL,
        name=name,
    )(*operands)


def hand_out(place, source_ref, out_refs):
    share, size = len(out_refs), out_refs[0].shape[0]
    for step, out_ref in enumerate(out_refs):
        start = pl.multiple_of((place + step) % share * size, size)
        out_ref[...] = source_ref[pl.ds(start, size), :]


def forward_kernel(parts, *refs):
    q_ref, qmask_ref = refs[:2]
    k_refs, v_refs, kmask_refs = (refs[2 + i * parts : 2 + (i + 1) * parts] for i in range(3))
    o_ref, lse_ref = refs[2 + 3 * parts :]
    low = lax.broadcasted_iota(jnp.int32, (1, 128), 1) < 64
    k = jnp.concatenate([ref[...] for ref in k_refs], 0)
    v = jnp.concatenate([ref[...] for ref in v_refs], 0)
    kmask = jnp.concatenate([ref[...] for ref in kmask_refs], 0)
    q, qmask = q_ref[...], qmask_ref[...]
    outputs = []
    both_scores = [
        dot(jnp.where(low, k, kmask), jnp.where(low, q, qmask), NT),
        dot(jnp.where(low, kmask, k), jnp.where(low, qmask, q), NT),
    ]
    for head, scores in enumerate(both_scores):
        mine = low if head == 0 else ~low
        largest = jnp.max(scores, axis=0, keepdims=True)
        weights = jnp.exp2(scores - largest).astype(bf16)
        both = dot(jnp.where(mine, v, jnp.ones_like(v)), weights, TN)
        total = both[64 - head * 64 : 65 - head * 64]
        lse_ref[0, head : head + 1, :] = largest + jnp.log2(total)
        outputs.append(both[head * 64 : head * 64 + 64] / total)
    o_ref[...] = jnp.concatenate(outputs, 0).T.astype(bf16)


def columns(rows, column, count):
    if callable(column):
        return [pl.BlockSpec((rows, 128), lambda h: (0, column(h)))] * count
    return [pl.BlockSpec((rows, 128), lambda h: (0, column))] * count


def attend(queries, qmask, keyvals, masks, mask_column):
    tokens, features = queries.shape
    parts = len(keyvals)
    length = parts * tokens
    pairs = features // 128
    of_queries = pl.BlockSpec((tokens, 128), lambda h: (0, h))
    return pl.pallas_call(
        functools.partial(forward_kernel, parts),
        grid=(pairs,),
        in_specs=[of_queries]
        + columns(tokens, 0, 1)
        + columns(tokens, lambda h: h, parts)
        + columns(tokens, lambda h: h + pairs, parts)
        + columns(tokens, mask_column, parts),
        out_specs=[of_queries, pl.BlockSpec((1, 2, tokens), lambda h: (h, 0, 0))],
        out_shape=[shaped((tokens, features)), shaped((pairs, 2, tokens), f32)],
        compiler_params=pltpu.CompilerParams(vmem_limit_bytes=VMEM),
        cost_estimate=SMALL,
        name="attend",
    )(queries, qmask, *keyvals, *keyvals, *masks)


def backward_kernel(parts, *refs):
    q_ref, qmask_ref, do_ref, o_ref, lse_ref = refs[:5]
    k_refs, v_refs, kmask_refs = (refs[5 + i * parts : 5 + (i + 1) * parts] for i in range(3))
    dq_ref, dkv_refs = refs[5 + 3 * parts], refs[6 + 3 * parts :]
    low = lax.broadcasted_iota(jnp.int32, (1, 128), 1) < 64
    q, qmask, grad = q_ref[...], qmask_ref[...], do_ref[...]
    tokens = q.shape[0]
    product = grad.astype(f32) * o_ref[...].astype(f32)
    upper = product.astype(bf16)
    lower = (product - upper.astype(f32)).astype(bf16)
    rows = lax.broadcasted_iota(jnp.int32, (8, 128), 0)
    lanes = lax.broadcasted_iota(jnp.int32, (8, 128), 1)
    pick = jnp.where(rows == lanes // 64, 1.0, 0.0).astype(bf16)
    delta = dot(pick, upper, NT) + dot(pick, lower, NT)
    lse = lse_ref[0]
    zero = jnp.zeros_like(grad)
    q_heads = [jnp.where(low, q, qmask), jnp.where(low, qmask, q)]
    grad_heads = [jnp.where(low, grad, zero), jnp.where(low, zero, grad)]
    dq = [jnp.zeros((64, tokens), f32)] * 2
    for part in range(parts):
        k, v = k_refs[part][...], v_refs[part][...]
        kmask = kmask_refs[part][...]
        dk, dv = [], []
        for head in range(2):
            k_head = jnp.where(low, k, kmask) if head == 0 else jnp.where(low, kmask, k)
            weights = jnp.exp2(dot(k_head, q_heads[head], NT) - lse[head : head + 1, :])
            grad_weights = dot(v, grad_heads[head], NT)
            grad_scores = (weights * (grad_weights - delta[head : head + 1, :])).astype(bf16)
            dv.append(dot(weights.astype(bf16), grad))
            dk.append(dot(grad_scores, q))
            dq[head] = dq[head] + dot(k, grad_scores, TN)[head * 64 : head * 64 + 64]
        dkv_refs[part][:, :128] = (jnp.where(low, dk[0], dk[1]) * math.log(2.0)).astype(bf16)
        dkv_refs[part][:, 128:] = jnp.where(low, dv[0], dv[1]).astype(bf16)
    dq_ref[...] = (jnp.concatenate(dq, 0).T * 0.125).astype(bf16)


def attend_back(queries, qmask, grad, outputs, lse, keyvals, masks, mask_column, first, count):
    tokens, features = queries.shape
    parts = len(keyvals)
    length = parts * tokens
    pairs = features // 128
    of_queries = pl.BlockSpec((tokens, 128), lambda h: (0, h + first))
    return pl.pallas_call(
        functools.partial(backward_kernel, parts),
        grid=(count,),
        in_specs=[
            of_queries,
            pl.BlockSpec((tokens, 128), lambda h: (0, 0)),
            of_queries,
            of_queries,
            pl.BlockSpec((1, 2, tokens), lambda h: (h + first, 0, 0)),
        ]
        + columns(tokens, lambda h: h + first, parts)
        + columns(tokens, lambda h: h + first + pairs, parts)
        + columns(tokens, mask_column, parts),
        out_specs=[pl.BlockSpec((tokens, 128), lambda h: (0, h))]
        + [pl.BlockSpec((tokens, 256), lambda h: (0, h))] * parts,
        out_shape=[shaped((tokens, count * 128))] + [shaped((tokens, count * 256))] * parts,
        compiler_params=pltpu.CompilerParams(vmem_limit_bytes=VMEM),
        cost_estimate=SMALL,
        name="attend_back",
    )(queries, qmask, grad, outputs, lse, *keyvals, *keyvals, *masks)


def mask_rows(codes, of_queries):
    places = lax.broadcasted_iota(jnp.int32, (128, codes.shape[1]), 0) % 64
    codes = jnp.broadcast_to(codes.astype(jnp.int32), places.shape)
    if of_queries:
        mask = jnp.where(codes % 4 == places, 1.0, 0.0)
    else:
        mask = jnp.where((codes != places) & (places < 3), HIDDEN_MASK, 0.0)
    return mask.T.astype(bf16)


def project_kernel(parts, length, *refs):
    x_refs = refs[:parts]
    gain_ref, bias_ref, w_ref, x_ref, normed_ref, query_ref, keyvals_ref, qmask_ref = refs[parts:]
    features = x_ref.shape[1]
    for part in range(parts):
        rows = slice(part * length, (part + 1) * length)
        low = x_refs[part][:length, :]
        x_ref[rows, :] = low
        normal, inverse = normalize(low.astype(f32))
        normed = (normal * gain_ref[...] + bias_ref[...]).astype(bf16)
        normed_ref[rows, :] = normed
        projected = dot(normed, w_ref[...])
        query_ref[rows, :] = (projected[:, :features] * QUERY_SCALE).astype(bf16)
        keyvals_ref[rows, : 2 * features] = projected[:, features:].astype(bf16)
        codes = x_refs[part][length : length + 16, :].astype(f32)[0:1, :]
        qmask_ref[rows, :] = mask_rows(codes[:, :length], True)
        keyvals_ref[rows, 2 * features : 2 * features + 128] = mask_rows(codes[:, :length], False)
        keyvals_ref[rows, 2 * features + 128 :] = mask_rows(codes[:, length : 2 * length], False)


def row_specs(array, count):
    shape = (1,) + array.shape[1:]
    return [
        pl.BlockSpec(shape, lambda i, row, step=step: ((row[0] + step) % count, 0, 0)) for step in range(count)
    ]


def pack_target(row, target, codes):
    count, length, features = target.shape

    def kernel(row_ref, *refs):
        seg_ref, keep_ref, memory_seg_ref, memory_keep_ref = refs[count : count + 4]
        for step in range(count):
            out_ref = refs[count + 4 + step]
            out_ref[:length, :] = refs[step][0]
            which = pl.ds((row_ref[0] + step) % count, 1)
            pieces = [
                jnp.where(keep[which, :] == 1, seg[which, :], seg[which, :] + 4).astype(f32)
                for seg, keep in ((seg_ref, keep_ref), (memory_seg_ref, memory_keep_ref))
            ]
            if features > 2 * length:
                pieces.append(jnp.zeros((1, features - 2 * length), f32))
            pieces = jnp.concatenate(pieces, 1)
            out_ref[length:, :] = jnp.broadcast_to(pieces, (16, features)).astype(bf16)

    out = shaped((length + 16, features))
    return pl.pallas_call(
        kernel,
        grid_spec=pltpu.PrefetchScalarGridSpec(
            num_scalar_prefetch=1,
            grid=(1,),
            in_specs=row_specs(target, count) + [whole(item) for item in codes],
            out_specs=[whole(out)] * count,
        ),
        out_shape=[out] * count,
        compiler_params=pltpu.CompilerParams(vmem_limit_bytes=VMEM),
        cost_estimate=SMALL,
        name="pack_target",
    )(row.reshape(1), *[target] * count, *codes)


def pack_rows(row, arrays):
    count, length, features = arrays[0].shape
    total = count * len(arrays)

    def kernel(row_ref, *refs):
        for i in range(total):
            refs[total + i][...] = refs[i][0]

    out = shaped((length, features), arrays[0].dtype)
    outs = pl.pallas_call(
        kernel,
        grid_spec=pltpu.PrefetchScalarGridSpec(
            num_scalar_prefetch=1,
            grid=(1,),
            in_specs=[spec for array in arrays for spec in row_specs(array, count)],
            out_specs=[whole(out)] * total,
        ),
        out_shape=[out] * total,
        compiler_params=pltpu.CompilerParams(vmem_limit_bytes=VMEM),
        cost_estimate=SMALL,
        name="pack_rows",
    )(row.reshape(1), *[array for array in arrays for _ in range(count)])
    return [tuple(outs[i : i + count]) for i in range(0, total, count)]


def place_rows(row, parts):
    count = len(parts)
    length, features = parts[0].shape

    def kernel(row_ref, *refs):
        for step in range(count):

            @pl.when(pl.program_id(0) == step)
            def _():
                refs[count][0] = refs[step][...].astype(f32)

    return pl.pallas_call(
        kernel,
        grid_spec=pltpu.PrefetchScalarGridSpec(
            num_scalar_prefetch=1,
            grid=(count,),
            in_specs=[pl.BlockSpec((length, features), lambda i, row: (0, 0))] * count,
            out_specs=pl.BlockSpec((1, length, features), lambda i, row: ((row[0] + i) % count, 0, 0)),
        ),
        out_shape=shaped((count, length, features), f32),
        cost_estimate=SMALL,
        name="place_rows",
    )(row.reshape(1), *parts)


def unpack_feed(place, parts, hidden, block):
    share = len(parts)
    features = parts[0].shape[1]
    steps = hidden // block
    each = steps // share

    def kernel(place_ref, *refs):
        up_ref, down_ref = refs[share:]
        owner = pl.program_id(0) // each
        for step in range(share):

            @pl.when((place_ref[0] + share - owner) % share == step)
            def _():
                up_ref[...] = refs[step][:features, :].astype(f32)
                down_ref[...] = refs[step][features:, :].astype(f32)

    return pl.pallas_call(
        kernel,
        grid_spec=pltpu.PrefetchScalarGridSpec(
            num_scalar_prefetch=1,
            grid=(steps,),
            in_specs=[pl.BlockSpec((2 * features, features), lambda j, place: (j % each, 0))] * share,
            out_specs=[
                pl.BlockSpec((features, block), lambda j, place: (0, j)),
                pl.BlockSpec((block, features), lambda j, place: (j, 0)),
            ],
        ),
        out_shape=[shaped((features, hidden), f32), shaped((hidden, features), f32)],
        compiler_params=pltpu.CompilerParams(vmem_limit_bytes=VMEM),
        cost_estimate=SMALL,
        name="unpack_feed",
    )(place.reshape(1), *parts)


def unpack_columns(place, parts, widths, vectors):
    share = len(parts)
    rows = parts[0].shape[0]
    last = sum(widths)

    def kernel(place_ref, *refs):
        for step in range(share):

            @pl.when((place_ref[0] + share - pl.program_id(0)) % share == step)
            def _():
                start = 0
                for width, out_ref in zip(widths, refs[share:]):
                    out_ref[...] = refs[step][:, start : start + width].astype(f32)
                    start += width

                if not vectors:
                    return

                @pl.when(pl.program_id(0) == 0)
                def _():
                    line = 0
                    values = refs[step][:64, last:].astype(f32)
                    for length, out_ref in zip(vectors, refs[share + len(widths) :]):
                        for i in range(0, length, 128):
                            out_ref[:, i : i + 128] = values[line : line + 1, :]
                            line += 1

    return pl.pallas_call(
        kernel,
        grid_spec=pltpu.PrefetchScalarGridSpec(
            num_scalar_prefetch=1,
            grid=(share,),
            in_specs=[pl.BlockSpec(part.shape, lambda j, place: (0, 0)) for part in parts],
            out_specs=[pl.BlockSpec((rows, width), lambda j, place: (j, 0)) for width in widths]
            + [pl.BlockSpec((1, length), lambda j, place: (0, 0)) for length in vectors],
        ),
        out_shape=[shaped((share * rows, width), f32) for width in widths]
        + [shaped((1, length), f32) for length in vectors],
        compiler_params=pltpu.CompilerParams(vmem_limit_bytes=VMEM),
        cost_estimate=SMALL,
        name="unpack_columns",
    )(place.reshape(1), *parts)


def memory_kernel(parts, *refs):
    part_refs = refs[:parts]
    w_ref, memory_ref, keyvals_ref = refs[parts:]
    length = part_refs[0].shape[0]
    for part in range(parts):
        rows = slice(part * length, (part + 1) * length)
        memory = part_refs[part][...]
        memory_ref[rows, :] = memory
        keyvals_ref[rows, :] = dot(memory, w_ref[...]).astype(bf16)


def after_self_kernel(x_ref, attended_ref, w_out_ref, gain_ref, bias_ref, w_q_ref, after_ref, normed_ref, query_ref):
    after = x_ref[...].astype(f32) + dot(attended_ref[...], w_out_ref[...])
    after_ref[...] = after
    normal, inverse = normalize(after)
    normed = (normal * gain_ref[...] + bias_ref[...]).astype(bf16)
    normed_ref[...] = normed
    query_ref[...] = (dot(normed, w_q_ref[...]) * QUERY_SCALE).astype(bf16)


def feed_kernel(parts, share, each, place_ref, *refs):
    after_ref, attended_ref, w_out_ref, gain_ref, bias_ref, w_up_ref, b_up_ref, w_down_ref, b_down_ref = refs[:9]
    cotangent_refs, refs = refs[9 : 9 + parts], refs[9 + parts :]
    out_refs, grad_w_refs, refs = refs[:parts], refs[parts : parts + share], refs[parts + share :]
    grad_ref, grad_heads_ref, grad_out_ref, grad_b_up_ref, sums_ref = refs[:5]
    normed_ref, x_ref, total_ref, back_ref, cotangent_ref = refs[5:]
    features = w_up_ref.shape[0]
    length = out_refs[0].shape[0]
    step = pl.program_id(0)

    @pl.when(step == 0)
    def _():
        for part, part_ref in enumerate(cotangent_refs):
            cotangent_ref[part * length : (part + 1) * length, :] = part_ref[...]
        x = after_ref[...] + dot(attended_ref[...], w_out_ref[...])
        x_ref[...] = x
        total_ref[...] = x + b_down_ref[...]
        normal, inverse = normalize(x)
        normed_ref[...] = (normal * gain_ref[...] + bias_ref[...]).astype(bf16)
        back_ref[...] = jnp.zeros_like(back_ref)

    cotangent = cotangent_ref[...]
    normed, w_up, w_down = normed_ref[...], w_up_ref[...], w_down_ref[...]
    u = dot(normed, w_up) + b_up_ref[...]
    slope = math.sqrt(2.0 / math.pi)
    squared = u * u
    bent = jnp.tanh(u * (slope + slope * 0.044715 * squared))
    half = 0.5 + 0.5 * bent
    activated = (u * half).astype(bf16)
    gelu_slope = half + (0.5 * u) * (1.0 - bent * bent) * (slope + 3.0 * slope * 0.044715 * squared)
    total_ref[...] += dot(activated, w_down)
    grad_hidden = (dot(cotangent, w_down, NT) * gelu_slope).astype(bf16)
    grad_up = dot(normed, grad_hidden, TN).astype(bf16)
    grad_down = dot(activated, cotangent, TN).astype(bf16)
    for part, grad_w_ref in enumerate(grad_w_refs):

        @pl.when(step // each == share - 1 - part)
        def _():
            grad_w_ref[:features, :] = grad_up
            grad_w_ref[features:, :] = grad_down

    grad_b_up_ref[...] = column_sums(grad_hidden.astype(f32))
    back_ref[...] += dot(grad_hidden, w_up, NT)

    @pl.when(step == pl.num_programs(0) - 1)
    def _():
        for part, out_ref in enumerate(out_refs):
            out_ref[...] = total_ref[part * length : (part + 1) * length, :].astype(bf16)
        normal, inverse = normalize(x_ref[...])
        grad_normed = back_ref[...]
        grad_out = cotangent.astype(f32)
        sums_ref[0:1, :] = column_sums(grad_normed * normal)
        sums_ref[1:2, :] = column_sums(grad_normed)
        sums_ref[2:3, :] = column_sums(grad_out)
        grad = grad_out + normalize_back(grad_normed, normal, inverse, gain_ref[...])
        grad_ref[...] = grad
        low = grad.astype(bf16)
        grad_heads_ref[...] = dot(low, w_out_ref[...], NT).astype(bf16)
        grad_out_ref[...] = dot(attended_ref[...], low, TN).astype(bf16)


def feed_forward(place, share, after_self, attended, cotangents, w_out, gain, bias, w_up, b_up, w_down, b_down):
    tokens, features = after_self.shape
    hidden = w_up.shape[1]
    block = features
    parts = len(cotangents)
    length = tokens // parts
    steps = hidden // block
    each = steps // share
    row, one, square = shaped((tokens, features)), shaped((1, features)), shaped((features, features))
    part_row = shaped((length, features))

    def now(j, place):
        return ((place[0] + share - 1 - j // each) % share) * each + j % each

    def grad_spec(part):
        begin = (share - 1 - part) * each
        return pl.BlockSpec(
            (features + block, features), lambda j, place: (jnp.clip(j - begin, 0, each - 1), 0)
        )

    return pl.pallas_call(
        functools.partial(feed_kernel, parts, share, each),
        grid_spec=pltpu.PrefetchScalarGridSpec(
            num_scalar_prefetch=1,
            grid=(steps,),
            in_specs=[
                whole(row),
                whole(row),
                whole(square),
                whole(one),
                whole(one),
                pl.BlockSpec((features, block), lambda j, place: (0, now(j, place))),
                pl.BlockSpec((1, block), lambda j, place: (0, now(j, place))),
                pl.BlockSpec((block, features), lambda j, place: (now(j, place), 0)),
                whole(one),
            ]
            + [whole(part_row)] * parts,
            out_specs=[whole(part_row)] * parts
            + [grad_spec(part) for part in range(share)]
            + [
                whole(row),
                whole(row),
                whole(square),
                pl.BlockSpec((1, block), lambda j, place: (0, now(j, place))),
                whole(shaped((8, features))),
            ],
            scratch_shapes=[
                pltpu.VMEM((tokens, features), bf16),
                pltpu.VMEM((tokens, features), f32),
                pltpu.VMEM((tokens, features), f32),
                pltpu.VMEM((tokens, features), f32),
                pltpu.VMEM((tokens, features), bf16),
            ],
        ),
        out_shape=[part_row] * parts
        + [shaped((each * (features + block), features))] * share
        + [
            shaped((tokens, features), f32),
            row,
            square,
            shaped((1, hidden), f32),
            shaped((8, features), f32),
        ],
        compiler_params=pltpu.CompilerParams(vmem_limit_bytes=VMEM),
        cost_estimate=SMALL,
        name="feed_forward",
    )(place.reshape(1), after_self, attended, w_out, gain, bias, w_up, b_up, w_down, b_down, *cotangents)


def after_self_back_kernel(calls, *refs):
    dq_refs = refs[:calls]
    after_ref, normed_ref, attended_ref, grad_after_ref, gain_ref, w_q_ref, w_out_ref = refs[calls : calls + 7]
    grad_ref, grad_heads_ref, grad_w_ref, sums_ref = refs[calls + 7 :]
    features = after_ref.shape[1]
    grad_query = jnp.concatenate([ref[...] for ref in dq_refs], 1)
    grad_normed = dot(grad_query, w_q_ref[...], NT)
    normal, inverse = normalize(after_ref[...])
    sums_ref[0:1, :] = column_sums(grad_normed * normal)
    sums_ref[1:2, :] = column_sums(grad_normed)
    grad = grad_after_ref[...] + normalize_back(grad_normed, normal, inverse, gain_ref[...])
    grad_ref[...] = grad
    low = grad.astype(bf16)
    grad_heads_ref[...] = dot(low, w_out_ref[...], NT).astype(bf16)
    grad_w_ref[:, :features] = dot(normed_ref[...], grad_query, TN).astype(bf16)
    grad_w_ref[:, features:] = dot(attended_ref[...], low, TN).astype(bf16)


def summed_keyvals(refs):
    keys, values = [], []
    for call in refs:
        total = sum([ref[...].astype(f32) for ref in call[1:]], call[0][...].astype(f32)).astype(bf16)
        for pair in range(total.shape[1] // 256):
            keys.append(total[:, pair * 256 : pair * 256 + 128])
            values.append(total[:, pair * 256 + 128 : pair * 256 + 256])
    return keys + values


def memory_back_kernel(calls, parts, place_ref, *refs):
    *refs, sum_ref = refs
    grad_refs = [refs[call * parts : (call + 1) * parts] for call in range(calls)]
    memory_ref, w_ref, out_ref, pair_ref = refs[calls * parts : calls * parts + 4]
    grad_w_refs = refs[calls * parts + 4 : calls * parts + 4 + parts]
    row_refs = refs[calls * parts + 4 + parts :]
    features = out_ref.shape[1]
    grad = jnp.concatenate(summed_keyvals(grad_refs), 1)
    result = dot(grad, w_ref[...], NT).astype(bf16)
    length = row_refs[0].shape[0]
    for part, row_ref in enumerate(row_refs):
        row_ref[...] = result[part * length : (part + 1) * length, :]
    sum_ref[:, :features] = out_ref[...]
    sum_ref[:, features : 3 * features] = pair_ref[...]
    sum_ref[:, 3 * features :] = dot(memory_ref[...], grad, TN).astype(bf16)
    hand_out(place_ref[0], sum_ref, grad_w_refs)


def project_back_kernel(calls, parts, place_ref, *refs):
    *refs, sum_ref = refs
    dq_refs = refs[:calls]
    refs = refs[calls:]
    grad_refs = [refs[call * parts : (call + 1) * parts] for call in range(calls)]
    refs = refs[calls * parts :]
    x_ref, normed_ref, gain_ref, w_ref, grad_after_ref, second_ref, third_ref, b_up_ref = refs[:8]
    grad_w_refs, row_refs = refs[8 : 8 + parts], refs[8 + parts :]
    grad = jnp.concatenate([ref[...] for ref in dq_refs] + summed_keyvals(grad_refs), 1)
    features = x_ref.shape[1]
    sum_ref[:, : 3 * features] = dot(normed_ref[...], grad, TN).astype(bf16)
    grad_normed = dot(grad, w_ref[...], NT)
    normal, inverse = normalize(x_ref[...].astype(f32))
    result = grad_after_ref[...] + normalize_back(grad_normed, normal, inverse, gain_ref[...])
    length = row_refs[0].shape[0]
    for part, row_ref in enumerate(row_refs):
        row_ref[...] = result[part * length : (part + 1) * length, :].astype(bf16)
    pieces = [column_sums(grad_normed * normal), column_sums(grad_normed), second_ref[0:1, :], second_ref[1:2, :]]
    pieces += [third_ref[0:1, :], third_ref[1:2, :], third_ref[2:3, :]]
    pieces += [b_up_ref[:, i : i + features] for i in range(0, b_up_ref.shape[1], features)]
    lines = [piece[:, i : i + 128] for piece in pieces for i in range(0, features, 128)]
    lines.append(jnp.zeros((features - len(lines), 128), f32))
    sum_ref[:, 3 * features :] = jnp.concatenate(lines, 0).astype(bf16)
    hand_out(place_ref[0], sum_ref, grad_w_refs)


class Layout:
    def __init__(self, dp, rows, blocks):
        self.rows = rows
        self.share = share = blocks // rows
        self.blocks = blocks
        self.dp = dp
        place = lax.axis_index("blk")
        self.row = place // share
        self.place = lax.rem(place, share)
        self.device = lax.axis_index("dp") * blocks + place

    def shift_rows(self, step):
        rows, share = self.rows, self.share
        return [
            (a * share + b, ((a + step) % rows) * share + b) for a in range(rows) for b in range(share)
        ]

    def shift_share(self, step):
        rows, share = self.rows, self.share
        return [
            (a * share + b, a * share + (b + step) % share) for a in range(rows) for b in range(share)
        ]

    def bring_rows(self, parts):
        return (parts[0],) + tuple(
            lax.ppermute(parts[step], "blk", self.shift_rows(step)) for step in range(1, self.rows)
        )

    def return_row(self, parts, step):
        arrived = lax.ppermute(parts[step], "blk", self.shift_rows(self.rows - step))
        return (*parts[:step], arrived, *parts[step + 1 :])

    def gather_share(self, values):
        return (values,) + tuple(
            lax.ppermute(values, "blk", self.shift_share(step)) for step in range(1, self.share)
        )

    def return_share(self, parts):
        return (parts[0],) + tuple(
            lax.ppermute(parts[step], "blk", self.shift_share(self.share - step))
            for step in range(1, self.share)
        )


class Sum:
    def __init__(self, layout, values, halves=True):
        share, rows, dp, blocks = layout.share, layout.rows, layout.dp, layout.blocks
        self.layout = layout
        self.parts = values if isinstance(values, tuple) else None
        self.values = (values,)
        own = (share, layout.place, layout.shift_share)
        row = (rows, layout.row, layout.shift_rows)
        bits = [blocks << bit for bit in range((dp - 1).bit_length())]
        bits = list(zip(bits, bits[1:] + bits[:1]))
        self.left = [(self.scatter,) + own]
        self.left += [(self.halve,) + pair for pair in bits] if halves else [(self.scatter_far,)]
        self.left += [(self.scatter,) + row, (self.gather,) + row]
        self.left += [(self.double,) + pair for pair in reversed(bits)]
        self.left += [(self.gather,) + own]

    def part(self, start, size):
        items = [lax.dynamic_slice_in_dim(item, start, size, 0).astype(f32) for item in self.values]
        return sum(items[1:], items[0]).astype(bf16)

    def scatter(self, count, index, shift):
        parts = self.parts
        self.parts = None
        if parts is None:
            size = self.values[0].shape[0] // count
            parts = [self.part(lax.rem(index + step, count) * size, size) for step in range(count)]
        arrived = [lax.ppermute(parts[step], "blk", shift(step)) for step in range(1, count)]
        self.values = (parts[0], *arrived)

    def scatter_far(self):
        dp, device = self.layout.dp, self.layout.device
        count = (dp - 1).bit_length()
        size = self.values[0].shape[0] // dp
        place = device // self.layout.blocks

        def part(step):
            whose = lax.rem(place + step, dp)
            even = sum(((whose >> bit) & 1) << (count - 1 - bit) for bit in range(count))
            odd = sum(((whose >> ((bit + 1) % count)) & 1) << (count - 1 - bit) for bit in range(count))
            return self.part(jnp.where(device % 2 == 0, even, odd) * size, size)

        arrived = [
            lax.ppermute(part(step), "dp", [(d, (d + step) % dp) for d in range(dp)]) for step in range(1, dp)
        ]
        self.values = (part(0), *arrived)

    def gather(self, count, index, shift):
        mine = self.part(0, self.values[0].shape[0])
        part_rows = mine.shape[0]
        arrived = [lax.ppermute(mine, "blk", shift(step)) for step in range(1, count)]
        if not self.left:
            self.values = (mine, *arrived)
            return
        result = jnp.zeros((count * part_rows, mine.shape[1]), mine.dtype)
        result = lax.dynamic_update_slice_in_dim(result, mine, index * part_rows, 0)
        for step, item in enumerate(arrived, 1):
            source = lax.rem(index + count - step, count)
            result = lax.dynamic_update_slice_in_dim(result, item, source * part_rows, 0)
        self.values = (result,)

    def exchange(self, values, even, odd):
        pairs = [(d, d ^ (odd if d % 2 else even)) for d in range(self.layout.dp * self.layout.blocks)]
        return lax.ppermute(values, ("dp", "blk"), pairs)

    def upper(self, even, odd):
        device = self.layout.device
        return (device & jnp.where(device % 2 == 0, even, odd)) != 0

    def halve(self, even, odd):
        half = self.values[0].shape[0] // 2
        upper = self.upper(even, odd).astype(jnp.int32)
        send = self.part((1 - upper) * half, half)
        self.values = (self.part(upper * half, half), self.exchange(send, even, odd))

    def double(self, even, odd):
        (mine,) = self.values
        arrived = self.exchange(mine, even, odd)
        self.values = (
            jnp.where(
                self.upper(even, odd), jnp.concatenate([arrived, mine], 0), jnp.concatenate([mine, arrived], 0)
            ),
        )

    def step(self):
        if self.left:
            action = self.left.pop(0)
            action[0](*action[1:])


def beside(sums, kernel, operands, *others):
    for running in sums:
        running.step()
    result, operands, others, values = join(
        kernel(*operands), operands, others, [running.values for running in sums]
    )
    for running, value in zip(sums, values):
        running.values = value
    return result, operands, *others


def join(*values):
    return lax.optimization_barrier(values)


def body(
    dp,
    blocks,
    target,
    memory,
    target_seg,
    target_keep,
    memory_seg,
    memory_keep,
    cotangent,
    norm1_gain,
    norm1_bias,
    w_qkv,
    w_out,
    norm2_gain,
    norm2_bias,
    w_cross_q,
    w_cross_kv,
    w_cross_out,
    norm3_gain,
    norm3_bias,
    w_up,
    b_up,
    w_down,
    b_down,
):
    rows, length, features = target.shape
    tokens = rows * length
    layout = Layout(dp, rows, blocks)
    target_parts = pack_target(layout.row, target, (target_seg, target_keep, memory_seg, memory_keep))
    target_parts = layout.bring_rows(target_parts)
    memory_parts, cotangent_parts = pack_rows(layout.row, (memory, cotangent))
    norm1_gain, norm1_bias, norm2_gain, norm2_bias, norm3_gain, norm3_bias, b_up, b_down = (
        item.reshape(1, -1)
        for item in (norm1_gain, norm1_bias, norm2_gain, norm2_bias, norm3_gain, norm3_bias, b_up, b_down)
    )
    hidden = w_up.shape[1]
    row, wide_row, full_row = (shaped((tokens, features)), shaped((tokens, 2 * features)), shaped((tokens, features), f32))
    row_parts = (shaped((length, features)),) * rows
    sums = shaped((8, features), f32)
    pairs = features // 128

    x, normed1, queries, keyvals, qmask = run(
        functools.partial(project_kernel, rows, length),
        "project",
        target_parts + (norm1_gain, norm1_bias, w_qkv),
        (row, row, row, shaped((tokens, 2 * features + 256)), shaped((tokens, 128))),
    )
    keyvals, memory_parts = join(keyvals, memory_parts)
    keyvals = layout.gather_share(keyvals)
    memory_parts = layout.bring_rows(memory_parts)
    self_masks = (keyvals, 2 * pairs)
    cross_masks = (keyvals, 2 * pairs + 1)
    self_low, self_lse = attend(queries, qmask, keyvals, *self_masks)
    self_low, memory_parts, cotangent_parts = join(self_low, memory_parts, cotangent_parts)
    memory_row, memory_keyvals = run(
        functools.partial(memory_kernel, rows), "memory", memory_parts + (w_cross_kv,), (row, wide_row)
    )
    memory_keyvals = layout.gather_share(memory_keyvals)
    after_self, normed2, cross_query = run(
        after_self_kernel,
        "after_self",
        (x, self_low, w_out, norm2_gain, norm2_bias, w_cross_q),
        (full_row, row, row),
    )
    cross_query, cotangent_parts, memory_keyvals = join(cross_query, cotangent_parts, memory_keyvals)
    cotangent_parts = layout.bring_rows(cotangent_parts)
    cross_low, cross_lse = attend(cross_query, qmask, memory_keyvals, *cross_masks)
    cross_low, cotangent_parts = join(cross_low, cotangent_parts)
    fed = feed_forward(
        layout.place,
        layout.share,
        after_self,
        cross_low,
        cotangent_parts,
        w_cross_out,
        norm3_gain,
        norm3_bias,
        w_up,
        b_up,
        w_down,
        b_down,
    )
    block_parts, grad_feed = tuple(fed[:rows]), tuple(fed[rows : rows + layout.share])
    grad_after_cross, grad_cross_heads, grad_w_cross_out, grad_b_up, sums3 = fed[rows + layout.share :]

    first = Sum(layout, grad_feed, halves=False)
    calls = 2

    def back(masks, call):
        count = pairs // calls
        return lambda *operands: attend_back(*operands, *masks, call * count, count)

    operands = (cross_query, qmask, grad_cross_heads, cross_low, cross_lse, memory_keyvals)
    for step in range(1, rows - 1):
        block_parts = layout.return_row(block_parts, step)
    grads, operands, block_parts = beside([first], back(cross_masks, 0), operands, block_parts)
    cross_grads, share = [grads[0]], layout.return_share(grads[1:])
    block_parts = layout.return_row(block_parts, rows - 1)
    grads, operands, share, block_parts = beside([first], back(cross_masks, 1), operands, share, block_parts)
    cross_grads.append(grads[0])
    cross_share = list(share) + list(layout.return_share(grads[1:]))
    (grad_after_self, grad_self_heads, grad_w_pair, sums2), _, cross_share = beside(
        [first],
        lambda *operands: run(
            functools.partial(after_self_back_kernel, calls),
            "after_self_back",
            operands,
            (full_row, row, shaped((features, 2 * features)), sums),
        ),
        tuple(cross_grads) + (after_self, normed2, self_low, grad_after_cross, norm2_gain, w_cross_q, w_out),
        cross_share,
    )
    share = layout.share
    part = shaped((features // share, 5 * features))
    outs, _, grad_self_heads = beside(
        [first],
        lambda *operands: run(
            functools.partial(memory_back_kernel, calls, share),
            "memory_back",
            operands,
            (part,) * share + row_parts,
            layout.place,
            [pltpu.VMEM((features, 5 * features), bf16)],
        ),
        tuple(cross_share) + (memory_row, w_cross_kv, grad_w_cross_out, grad_w_pair),
        grad_self_heads,
    )
    middle = Sum(layout, tuple(outs[:share]))

    calls = 4
    operands = (queries, qmask, grad_self_heads, self_low, self_lse, keyvals)
    memory_parts = tuple(outs[share:])
    self_grads, self_share, sent = [], [], ()
    for call in range(calls):
        if call + 1 < rows:
            memory_parts = layout.return_row(memory_parts, call + 1)
        grads, operands, sent, memory_parts = beside(
            [first, middle], back(self_masks, call), operands, sent, memory_parts
        )
        self_grads.append(grads[0])
        self_share += sent
        sent = layout.return_share(grads[1:])
    self_share += sent
    self_share = join(self_share, self_grads)[0]
    part = shaped((features // share, 3 * features + 128))
    outs, _ = beside(
        [first],
        lambda *operands: run(
            functools.partial(project_back_kernel, calls, share),
            "project_back",
            operands,
            (part,) * share + row_parts,
            layout.place,
            [pltpu.VMEM((features, 3 * features + 128), bf16)],
        ),
        tuple(self_grads)
        + tuple(self_share)
        + (x, normed1, norm1_gain, w_qkv, grad_after_self, sums2, sums3, grad_b_up),
    )
    last = Sum(layout, tuple(outs[:share]))
    target_parts = tuple(outs[share:])
    while first.left:
        first.step()
    for step in [*range(2, rows), 1]:
        target_parts = layout.return_row(target_parts, step)
        late = (target_parts,) if step != 2 else ()
        _, _, *late = beside([last, middle], lambda: (), (), *late)
        target_parts = late[0] if late else target_parts

    def placed(*parts):
        return place_rows(layout.row, parts)

    target_grad, _ = beside([last, middle], placed, target_parts)
    while middle.left:
        middle.step()
    (grad_w_cross_out, grad_w_cross_q, grad_w_out, grad_w_cross_kv), _ = beside(
        [last],
        lambda *parts: unpack_columns(layout.place, parts, [features, features, features, 2 * features], []),
        middle.values,
    )
    memory_grad, _, block_parts = beside([last], placed, memory_parts, block_parts)
    (grad_w_up, grad_w_down), _ = beside(
        [last], lambda *parts: unpack_feed(layout.place, parts, hidden, features), first.values
    )
    block_out, _ = beside([last], placed, block_parts)
    while last.left:
        last.step()
    grad_w_qkv, *vectors = unpack_columns(layout.place, last.values, [3 * features], [features] * 7 + [hidden])
    (
        grad_norm1_gain,
        grad_norm1_bias,
        grad_norm2_gain,
        grad_norm2_bias,
        grad_norm3_gain,
        grad_norm3_bias,
        grad_b_down,
        grad_b_up,
    ) = [vector.reshape(-1) for vector in vectors]
    return (
        block_out,
        target_grad,
        memory_grad,
        grad_norm1_gain,
        grad_norm1_bias,
        grad_w_qkv,
        grad_w_out,
        grad_norm2_gain,
        grad_norm2_bias,
        grad_w_cross_q,
        grad_w_cross_kv,
        grad_w_cross_out,
        grad_norm3_gain,
        grad_norm3_bias,
        grad_w_up,
        grad_b_up,
        grad_w_down,
        grad_b_down,
    )


def solution(mesh):
    token = P("dp", "blk", None)
    code = P("dp", "blk")
    return jax.shard_map(
        functools.partial(body, mesh.shape["dp"], mesh.shape["blk"]),
        mesh=mesh,
        in_specs=(token, token, code, code, code, code, token) + (P(),) * 15,
        out_specs=(token, token, token) + (P(),) * 15,
        check_vma=False,
    )
```

```python
import functools
import math

import jax
import jax.numpy as jnp
from jax import lax
from jax.experimental import pallas as pl
from jax.experimental.pallas import tpu as pltpu
from jax.sharding import PartitionSpec as P

HEADS = 8
NT = (((1,), (1,)), ((), ()))
NN = (((1,), (0,)), ((), ()))
TN = (((0,), (0,)), ((), ()))
f32 = jnp.float32
bf16 = jnp.bfloat16
VMEM = 60 * 1024 * 1024
SMALL = pl.CostEstimate(flops=1, bytes_accessed=1, transcendentals=0)
QUERY_SCALE = 0.125 * math.log2(math.e)
HIDDEN_MASK = -1e30


def dot(left, right, dims=NN):
    return lax.dot_general(left, right, dims, preferred_element_type=f32)


def normalize(values):
    centered = values - jnp.mean(values, axis=1, keepdims=True)
    inverse = lax.rsqrt(jnp.mean(centered * centered, axis=1, keepdims=True) + 1e-05)
    return centered * inverse, inverse


def normalize_back(grad, normal, inverse, gain):
    grad = grad * gain
    shift = jnp.mean(grad, axis=1, keepdims=True)
    along = jnp.mean(grad * normal, axis=1, keepdims=True)
    return inverse * (grad - shift - normal * along)


def column_sums(values):
    return jnp.sum(values, axis=0, keepdims=True)


def whole(array, *index):
    shape = array.shape
    index = index or (0,) * len(shape)
    return pl.BlockSpec(shape, lambda *grid: index)


def shaped(shape, dtype=bf16):
    return jax.ShapeDtypeStruct(shape, dtype)


def run(kernel, name, operands, outs, place=None, scratch=()):
    specs = [whole(array) for array in operands]
    if place is not None:
        specs = [pl.BlockSpec(memory_space=pltpu.SMEM)] + specs
        operands = (place.reshape(1), *operands)
    return pl.pallas_call(
        kernel,
        grid=(1,),
        in_specs=specs,
        out_specs=[whole(out) for out in outs],
        out_shape=list(outs),
        scratch_shapes=list(scratch),
        compiler_params=pltpu.CompilerParams(vmem_limit_bytes=VMEM),
        cost_estimate=SMALL,
        name=name,
    )(*operands)


def hand_out(place, source_ref, out_refs):
    share, size = len(out_refs), out_refs[0].shape[0]
    for step, out_ref in enumerate(out_refs):
        start = pl.multiple_of((place + step) % share * size, size)
        out_ref[...] = source_ref[pl.ds(start, size), :]


def forward_kernel(parts, *refs):
    q_ref, qmask_ref = refs[:2]
    k_refs, v_refs, kmask_refs = (refs[2 + i * parts : 2 + (i + 1) * parts] for i in range(3))
    o_ref, lse_ref = refs[2 + 3 * parts :]
    low = lax.broadcasted_iota(jnp.int32, (1, 128), 1) < 64
    k = jnp.concatenate([ref[...] for ref in k_refs], 0)
    v = jnp.concatenate([ref[...] for ref in v_refs], 0)
    kmask = jnp.concatenate([ref[...] for ref in kmask_refs], 0)
    q, qmask = q_ref[...], qmask_ref[...]
    outputs = []
    both_scores = [
        dot(jnp.where(low, k, kmask), jnp.where(low, q, qmask), NT),
        dot(jnp.where(low, kmask, k), jnp.where(low, qmask, q), NT),
    ]
    for head, scores in enumerate(both_scores):
        mine = low if head == 0 else ~low
        largest = jnp.max(scores, axis=0, keepdims=True)
        weights = jnp.exp2(scores - largest).astype(bf16)
        both = dot(jnp.where(mine, v, jnp.ones_like(v)), weights, TN)
        total = both[64 - head * 64 : 65 - head * 64]
        lse_ref[0, head : head + 1, :] = largest + jnp.log2(total)
        outputs.append(both[head * 64 : head * 64 + 64] / total)
    o_ref[...] = jnp.concatenate(outputs, 0).T.astype(bf16)


def columns(rows, column, count):
    if callable(column):
        return [pl.BlockSpec((rows, 128), lambda h: (0, column(h)))] * count
    return [pl.BlockSpec((rows, 128), lambda h: (0, column))] * count


def attend(queries, qmask, keyvals, masks, mask_column):
    tokens, features = queries.shape
    parts = len(keyvals)
    length = parts * tokens
    pairs = features // 128
    of_queries = pl.BlockSpec((tokens, 128), lambda h: (0, h))
    return pl.pallas_call(
        functools.partial(forward_kernel, parts),
        grid=(pairs,),
        in_specs=[of_queries]
        + columns(tokens, 0, 1)
        + columns(tokens, lambda h: h, parts)
        + columns(tokens, lambda h: h + pairs, parts)
        + columns(tokens, mask_column, parts),
        out_specs=[of_queries, pl.BlockSpec((1, 2, tokens), lambda h: (h, 0, 0))],
        out_shape=[shaped((tokens, features)), shaped((pairs, 2, tokens), f32)],
        compiler_params=pltpu.CompilerParams(vmem_limit_bytes=VMEM),
        cost_estimate=SMALL,
        name="attend",
    )(queries, qmask, *keyvals, *keyvals, *masks)


def backward_kernel(parts, *refs):
    q_ref, qmask_ref, do_ref, o_ref, lse_ref = refs[:5]
    k_refs, v_refs, kmask_refs = (refs[5 + i * parts : 5 + (i + 1) * parts] for i in range(3))
    dq_ref, dkv_refs = refs[5 + 3 * parts], refs[6 + 3 * parts :]
    low = lax.broadcasted_iota(jnp.int32, (1, 128), 1) < 64
    q, qmask, grad = q_ref[...], qmask_ref[...], do_ref[...]
    tokens = q.shape[0]
    product = grad.astype(f32) * o_ref[...].astype(f32)
    upper = product.astype(bf16)
    lower = (product - upper.astype(f32)).astype(bf16)
    rows = lax.broadcasted_iota(jnp.int32, (8, 128), 0)
    lanes = lax.broadcasted_iota(jnp.int32, (8, 128), 1)
    pick = jnp.where(rows == lanes // 64, 1.0, 0.0).astype(bf16)
    delta = dot(pick, upper, NT) + dot(pick, lower, NT)
    lse = lse_ref[0]
    zero = jnp.zeros_like(grad)
    q_heads = [jnp.where(low, q, qmask), jnp.where(low, qmask, q)]
    grad_heads = [jnp.where(low, grad, zero), jnp.where(low, zero, grad)]
    dq = [jnp.zeros((64, tokens), f32)] * 2
    for part in range(parts):
        k, v = k_refs[part][...], v_refs[part][...]
        kmask = kmask_refs[part][...]
        dk, dv = [], []
        for head in range(2):
            k_head = jnp.where(low, k, kmask) if head == 0 else jnp.where(low, kmask, k)
            weights = jnp.exp2(dot(k_head, q_heads[head], NT) - lse[head : head + 1, :])
            grad_weights = dot(v, grad_heads[head], NT)
            grad_scores = (weights * (grad_weights - delta[head : head + 1, :])).astype(bf16)
            dv.append(dot(weights.astype(bf16), grad))
            dk.append(dot(grad_scores, q))
            dq[head] = dq[head] + dot(k, grad_scores, TN)[head * 64 : head * 64 + 64]
        dkv_refs[part][:, :128] = (jnp.where(low, dk[0], dk[1]) * math.log(2.0)).astype(bf16)
        dkv_refs[part][:, 128:] = jnp.where(low, dv[0], dv[1]).astype(bf16)
    dq_ref[...] = (jnp.concatenate(dq, 0).T * 0.125).astype(bf16)


def attend_back(queries, qmask, grad, outputs, lse, keyvals, masks, mask_column, first, count):
    tokens, features = queries.shape
    parts = len(keyvals)
    length = parts * tokens
    pairs = features // 128
    of_queries = pl.BlockSpec((tokens, 128), lambda h: (0, h + first))
    return pl.pallas_call(
        functools.partial(backward_kernel, parts),
        grid=(count,),
        in_specs=[
            of_queries,
            pl.BlockSpec((tokens, 128), lambda h: (0, 0)),
            of_queries,
            of_queries,
            pl.BlockSpec((1, 2, tokens), lambda h: (h + first, 0, 0)),
        ]
        + columns(tokens, lambda h: h + first, parts)
        + columns(tokens, lambda h: h + first + pairs, parts)
        + columns(tokens, mask_column, parts),
        out_specs=[pl.BlockSpec((tokens, 128), lambda h: (0, h))]
        + [pl.BlockSpec((tokens, 256), lambda h: (0, h))] * parts,
        out_shape=[shaped((tokens, count * 128))] + [shaped((tokens, count * 256))] * parts,
        compiler_params=pltpu.CompilerParams(vmem_limit_bytes=VMEM),
        cost_estimate=SMALL,
        name="attend_back",
    )(queries, qmask, grad, outputs, lse, *keyvals, *keyvals, *masks)


def mask_rows(codes, of_queries):
    places = lax.broadcasted_iota(jnp.int32, (128, codes.shape[1]), 0) % 64
    codes = jnp.broadcast_to(codes.astype(jnp.int32), places.shape)
    if of_queries:
        mask = jnp.where(codes % 4 == places, 1.0, 0.0)
    else:
        mask = jnp.where((codes != places) & (places < 3), HIDDEN_MASK, 0.0)
    return mask.T.astype(bf16)


def project_kernel(parts, length, *refs):
    x_refs = refs[:parts]
    gain_ref, bias_ref, w_ref, x_ref, normed_ref, query_ref, keyvals_ref, qmask_ref = refs[parts:]
    features = x_ref.shape[1]
    for part in range(parts):
        rows = slice(part * length, (part + 1) * length)
        low = x_refs[part][:length, :]
        x_ref[rows, :] = low
        normal, inverse = normalize(low.astype(f32))
        normed = (normal * gain_ref[...] + bias_ref[...]).astype(bf16)
        normed_ref[rows, :] = normed
        projected = dot(normed, w_ref[...])
        query_ref[rows, :] = (projected[:, :features] * QUERY_SCALE).astype(bf16)
        keyvals_ref[rows, : 2 * features] = projected[:, features:].astype(bf16)
        codes = x_refs[part][length : length + 16, :].astype(f32)[0:1, :]
        qmask_ref[rows, :] = mask_rows(codes[:, :length], True)
        keyvals_ref[rows, 2 * features : 2 * features + 128] = mask_rows(codes[:, :length], False)
        keyvals_ref[rows, 2 * features + 128 :] = mask_rows(codes[:, length : 2 * length], False)


def row_specs(array, count):
    shape = (1,) + array.shape[1:]
    return [
        pl.BlockSpec(shape, lambda i, row, step=step: ((row[0] + step) % count, 0, 0)) for step in range(count)
    ]


def pack_target(row, target, codes):
    count, length, features = target.shape

    def kernel(row_ref, *refs):
        seg_ref, keep_ref, memory_seg_ref, memory_keep_ref = refs[count : count + 4]
        for step in range(count):
            out_ref = refs[count + 4 + step]
            out_ref[:length, :] = refs[step][0]
            which = pl.ds((row_ref[0] + step) % count, 1)
            pieces = [
                jnp.where(keep[which, :] == 1, seg[which, :], seg[which, :] + 4).astype(f32)
                for seg, keep in ((seg_ref, keep_ref), (memory_seg_ref, memory_keep_ref))
            ]
            if features > 2 * length:
                pieces.append(jnp.zeros((1, features - 2 * length), f32))
            pieces = jnp.concatenate(pieces, 1)
            out_ref[length:, :] = jnp.broadcast_to(pieces, (16, features)).astype(bf16)

    out = shaped((length + 16, features))
    return pl.pallas_call(
        kernel,
        grid_spec=pltpu.PrefetchScalarGridSpec(
            num_scalar_prefetch=1,
            grid=(1,),
            in_specs=row_specs(target, count) + [whole(item) for item in codes],
            out_specs=[whole(out)] * count,
        ),
        out_shape=[out] * count,
        compiler_params=pltpu.CompilerParams(vmem_limit_bytes=VMEM),
        cost_estimate=SMALL,
        name="pack_target",
    )(row.reshape(1), *[target] * count, *codes)


def pack_rows(row, arrays):
    count, length, features = arrays[0].shape
    total = count * len(arrays)

    def kernel(row_ref, *refs):
        for i in range(total):
            refs[total + i][...] = refs[i][0]

    out = shaped((length, features), arrays[0].dtype)
    outs = pl.pallas_call(
        kernel,
        grid_spec=pltpu.PrefetchScalarGridSpec(
            num_scalar_prefetch=1,
            grid=(1,),
            in_specs=[spec for array in arrays for spec in row_specs(array, count)],
            out_specs=[whole(out)] * total,
        ),
        out_shape=[out] * total,
        compiler_params=pltpu.CompilerParams(vmem_limit_bytes=VMEM),
        cost_estimate=SMALL,
        name="pack_rows",
    )(row.reshape(1), *[array for array in arrays for _ in range(count)])
    return [tuple(outs[i : i + count]) for i in range(0, total, count)]


def place_rows(row, parts):
    count = len(parts)
    length, features = parts[0].shape

    def kernel(row_ref, *refs):
        for step in range(count):

            @pl.when(pl.program_id(0) == step)
            def _():
                refs[count][0] = refs[step][...].astype(f32)

    return pl.pallas_call(
        kernel,
        grid_spec=pltpu.PrefetchScalarGridSpec(
            num_scalar_prefetch=1,
            grid=(count,),
            in_specs=[pl.BlockSpec((length, features), lambda i, row: (0, 0))] * count,
            out_specs=pl.BlockSpec((1, length, features), lambda i, row: ((row[0] + i) % count, 0, 0)),
        ),
        out_shape=shaped((count, length, features), f32),
        cost_estimate=SMALL,
        name="place_rows",
    )(row.reshape(1), *parts)


def unpack_feed(place, parts, hidden, block):
    share = len(parts)
    features = parts[0].shape[1]
    steps = hidden // block
    each = steps // share

    def kernel(place_ref, *refs):
        up_ref, down_ref = refs[share:]
        owner = pl.program_id(0) // each
        for step in range(share):

            @pl.when((place_ref[0] + share - owner) % share == step)
            def _():
                up_ref[...] = refs[step][:features, :].astype(f32)
                down_ref[...] = refs[step][features:, :].astype(f32)

    return pl.pallas_call(
        kernel,
        grid_spec=pltpu.PrefetchScalarGridSpec(
            num_scalar_prefetch=1,
            grid=(steps,),
            in_specs=[pl.BlockSpec((2 * features, features), lambda j, place: (j % each, 0))] * share,
            out_specs=[
                pl.BlockSpec((features, block), lambda j, place: (0, j)),
                pl.BlockSpec((block, features), lambda j, place: (j, 0)),
            ],
        ),
        out_shape=[shaped((features, hidden), f32), shaped((hidden, features), f32)],
        compiler_params=pltpu.CompilerParams(vmem_limit_bytes=VMEM),
        cost_estimate=SMALL,
        name="unpack_feed",
    )(place.reshape(1), *parts)


def unpack_columns(place, parts, widths, vectors):
    share = len(parts)
    rows = parts[0].shape[0]
    last = sum(widths)

    def kernel(place_ref, *refs):
        for step in range(share):

            @pl.when((place_ref[0] + share - pl.program_id(0)) % share == step)
            def _():
                start = 0
                for width, out_ref in zip(widths, refs[share:]):
                    out_ref[...] = refs[step][:, start : start + width].astype(f32)
                    start += width

                if not vectors:
                    return

                @pl.when(pl.program_id(0) == 0)
                def _():
                    line = 0
                    values = refs[step][:64, last:].astype(f32)
                    for length, out_ref in zip(vectors, refs[share + len(widths) :]):
                        for i in range(0, length, 128):
                            out_ref[:, i : i + 128] = values[line : line + 1, :]
                            line += 1

    return pl.pallas_call(
        kernel,
        grid_spec=pltpu.PrefetchScalarGridSpec(
            num_scalar_prefetch=1,
            grid=(share,),
            in_specs=[pl.BlockSpec(part.shape, lambda j, place: (0, 0)) for part in parts],
            out_specs=[pl.BlockSpec((rows, width), lambda j, place: (j, 0)) for width in widths]
            + [pl.BlockSpec((1, length), lambda j, place: (0, 0)) for length in vectors],
        ),
        out_shape=[shaped((share * rows, width), f32) for width in widths]
        + [shaped((1, length), f32) for length in vectors],
        compiler_params=pltpu.CompilerParams(vmem_limit_bytes=VMEM),
        cost_estimate=SMALL,
        name="unpack_columns",
    )(place.reshape(1), *parts)


def memory_kernel(parts, *refs):
    part_refs = refs[:parts]
    w_ref, memory_ref, keyvals_ref = refs[parts:]
    length = part_refs[0].shape[0]
    for part in range(parts):
        rows = slice(part * length, (part + 1) * length)
        memory = part_refs[part][...]
        memory_ref[rows, :] = memory
        keyvals_ref[rows, :] = dot(memory, w_ref[...]).astype(bf16)


def after_self_kernel(x_ref, attended_ref, w_out_ref, gain_ref, bias_ref, w_q_ref, after_ref, normed_ref, query_ref):
    after = x_ref[...].astype(f32) + dot(attended_ref[...], w_out_ref[...])
    after_ref[...] = after.astype(bf16)
    normal, inverse = normalize(after)
    normed = (normal * gain_ref[...] + bias_ref[...]).astype(bf16)
    normed_ref[...] = normed
    query_ref[...] = (dot(normed, w_q_ref[...]) * QUERY_SCALE).astype(bf16)


def feed_kernel(parts, share, each, place_ref, *refs):
    after_ref, attended_ref, w_out_ref, gain_ref, bias_ref, w_up_ref, b_up_ref, w_down_ref, b_down_ref = refs[:9]
    cotangent_refs, refs = refs[9 : 9 + parts], refs[9 + parts :]
    out_refs, grad_w_refs, refs = refs[:parts], refs[parts : parts + share], refs[parts + share :]
    grad_ref, grad_heads_ref, grad_out_ref, grad_b_up_ref, sums_ref = refs[:5]
    normed_ref, x_ref, total_ref, back_ref, cotangent_ref = refs[5:]
    features = w_up_ref.shape[0]
    length = out_refs[0].shape[0]
    step = pl.program_id(0)

    @pl.when(step == 0)
    def _():
        for part, part_ref in enumerate(cotangent_refs):
            cotangent_ref[part * length : (part + 1) * length, :] = part_ref[...]
        x = after_ref[...].astype(f32) + dot(attended_ref[...], w_out_ref[...])
        x_ref[...] = x
        total_ref[...] = x + b_down_ref[...]
        normal, inverse = normalize(x)
        normed_ref[...] = (normal * gain_ref[...] + bias_ref[...]).astype(bf16)
        back_ref[...] = jnp.zeros_like(back_ref)

    cotangent = cotangent_ref[...]
    normed, w_up, w_down = normed_ref[...], w_up_ref[...], w_down_ref[...]
    u = dot(normed, w_up) + b_up_ref[...]
    slope = math.sqrt(2.0 / math.pi)
    squared = u * u
    bent = jnp.tanh(u * (slope + slope * 0.044715 * squared))
    half = 0.5 + 0.5 * bent
    activated = (u * half).astype(bf16)
    gelu_slope = half + (0.5 * u) * (1.0 - bent * bent) * (slope + 3.0 * slope * 0.044715 * squared)
    total_ref[...] += dot(activated, w_down)
    grad_hidden = (dot(cotangent, w_down, NT) * gelu_slope).astype(bf16)
    grad_up = dot(normed, grad_hidden, TN).astype(bf16)
    grad_down = dot(activated, cotangent, TN).astype(bf16)
    for part, grad_w_ref in enumerate(grad_w_refs):

        @pl.when(step // each == share - 1 - part)
        def _():
            for i in range(0, grad_up.shape[1], features):
                grad_w_ref[2 * i : 2 * i + features, :] = grad_up[:, i : i + features]
                grad_w_ref[2 * i + features : 2 * i + 2 * features, :] = grad_down[i : i + features, :]

    grad_b_up_ref[...] = column_sums(grad_hidden.astype(f32))
    back_ref[...] += dot(grad_hidden, w_up, NT)

    @pl.when(step == pl.num_programs(0) - 1)
    def _():
        for part, out_ref in enumerate(out_refs):
            out_ref[...] = total_ref[part * length : (part + 1) * length, :].astype(bf16)
        normal, inverse = normalize(x_ref[...])
        grad_normed = back_ref[...]
        grad_out = cotangent.astype(f32)
        sums_ref[0:1, :] = column_sums(grad_normed * normal)
        sums_ref[1:2, :] = column_sums(grad_normed)
        sums_ref[2:3, :] = column_sums(grad_out)
        grad = grad_out + normalize_back(grad_normed, normal, inverse, gain_ref[...])
        low = grad.astype(bf16)
        grad_ref[...] = low
        grad_heads_ref[...] = dot(low, w_out_ref[...], NT).astype(bf16)
        grad_out_ref[...] = dot(attended_ref[...], low, TN).astype(bf16)


def feed_forward(place, share, after_self, attended, cotangents, w_out, gain, bias, w_up, b_up, w_down, b_down):
    tokens, features = after_self.shape
    hidden = w_up.shape[1]
    block = features * (1 if hidden // features // share % 2 else 2)
    parts = len(cotangents)
    length = tokens // parts
    steps = hidden // block
    each = steps // share
    row, one, square = shaped((tokens, features)), shaped((1, features)), shaped((features, features))
    part_row = shaped((length, features))

    def now(j, place):
        return ((place[0] + share - 1 - j // each) % share) * each + j % each

    def grad_spec(part):
        begin = (share - 1 - part) * each
        return pl.BlockSpec(
            (2 * block, features), lambda j, place: (jnp.clip(j - begin, 0, each - 1), 0)
        )

    return pl.pallas_call(
        functools.partial(feed_kernel, parts, share, each),
        grid_spec=pltpu.PrefetchScalarGridSpec(
            num_scalar_prefetch=1,
            grid=(steps,),
            in_specs=[
                whole(row),
                whole(row),
                whole(square),
                whole(one),
                whole(one),
                pl.BlockSpec((features, block), lambda j, place: (0, now(j, place))),
                pl.BlockSpec((1, block), lambda j, place: (0, now(j, place))),
                pl.BlockSpec((block, features), lambda j, place: (now(j, place), 0)),
                whole(one),
            ]
            + [whole(part_row)] * parts,
            out_specs=[whole(part_row)] * parts
            + [grad_spec(part) for part in range(share)]
            + [
                whole(row),
                whole(row),
                whole(square),
                pl.BlockSpec((1, block), lambda j, place: (0, now(j, place))),
                whole(shaped((8, features))),
            ],
            scratch_shapes=[
                pltpu.VMEM((tokens, features), bf16),
                pltpu.VMEM((tokens, features), f32),
                pltpu.VMEM((tokens, features), f32),
                pltpu.VMEM((tokens, features), f32),
                pltpu.VMEM((tokens, features), bf16),
            ],
        ),
        out_shape=[part_row] * parts
        + [shaped((each * 2 * block, features))] * share
        + [
            row,
            row,
            square,
            shaped((1, hidden), f32),
            shaped((8, features), f32),
        ],
        compiler_params=pltpu.CompilerParams(vmem_limit_bytes=VMEM),
        cost_estimate=SMALL,
        name="feed_forward",
    )(place.reshape(1), after_self, attended, w_out, gain, bias, w_up, b_up, w_down, b_down, *cotangents)


def after_self_back_kernel(calls, *refs):
    dq_refs = refs[:calls]
    after_ref, normed_ref, attended_ref, grad_after_ref, gain_ref, w_q_ref, w_out_ref = refs[calls : calls + 7]
    grad_ref, grad_heads_ref, grad_w_ref, sums_ref = refs[calls + 7 :]
    features = after_ref.shape[1]
    grad_query = jnp.concatenate([ref[...] for ref in dq_refs], 1)
    grad_normed = dot(grad_query, w_q_ref[...], NT)
    normal, inverse = normalize(after_ref[...].astype(f32))
    sums_ref[0:1, :] = column_sums(grad_normed * normal)
    sums_ref[1:2, :] = column_sums(grad_normed)
    grad = grad_after_ref[...].astype(f32) + normalize_back(grad_normed, normal, inverse, gain_ref[...])
    low = grad.astype(bf16)
    grad_ref[...] = low
    grad_heads_ref[...] = dot(low, w_out_ref[...], NT).astype(bf16)
    grad_w_ref[:, :features] = dot(normed_ref[...], grad_query, TN).astype(bf16)
    grad_w_ref[:, features:] = dot(attended_ref[...], low, TN).astype(bf16)


def summed_keyvals(refs):
    keys, values = [], []
    for call in refs:
        total = sum([ref[...].astype(f32) for ref in call[1:]], call[0][...].astype(f32)).astype(bf16)
        for pair in range(total.shape[1] // 256):
            keys.append(total[:, pair * 256 : pair * 256 + 128])
            values.append(total[:, pair * 256 + 128 : pair * 256 + 256])
    return keys + values


def memory_back_kernel(calls, parts, place_ref, *refs):
    *refs, sum_ref = refs
    grad_refs = [refs[call * parts : (call + 1) * parts] for call in range(calls)]
    memory_ref, w_ref, out_ref, pair_ref = refs[calls * parts : calls * parts + 4]
    grad_w_refs = refs[calls * parts + 4 : calls * parts + 4 + parts]
    row_refs = refs[calls * parts + 4 + parts :]
    features = out_ref.shape[1]
    grad = jnp.concatenate(summed_keyvals(grad_refs), 1)
    result = dot(grad, w_ref[...], NT).astype(bf16)
    length = row_refs[0].shape[0]
    for part, row_ref in enumerate(row_refs):
        row_ref[...] = result[part * length : (part + 1) * length, :]
    sum_ref[:, :features] = out_ref[...]
    sum_ref[:, features : 3 * features] = pair_ref[...]
    sum_ref[:, 3 * features :] = dot(memory_ref[...], grad, TN).astype(bf16)
    hand_out(place_ref[0], sum_ref, grad_w_refs)


def project_back_kernel(calls, parts, place_ref, *refs):
    *refs, sum_ref = refs
    dq_refs = refs[:calls]
    refs = refs[calls:]
    grad_refs = [refs[call * parts : (call + 1) * parts] for call in range(calls)]
    refs = refs[calls * parts :]
    x_ref, normed_ref, gain_ref, w_ref, grad_after_ref, second_ref, third_ref, b_up_ref = refs[:8]
    grad_w_refs, row_refs = refs[8 : 8 + parts], refs[8 + parts :]
    grad = jnp.concatenate([ref[...] for ref in dq_refs] + summed_keyvals(grad_refs), 1)
    features = x_ref.shape[1]
    sum_ref[:, : 3 * features] = dot(normed_ref[...], grad, TN).astype(bf16)
    grad_normed = dot(grad, w_ref[...], NT)
    normal, inverse = normalize(x_ref[...].astype(f32))
    result = grad_after_ref[...].astype(f32) + normalize_back(grad_normed, normal, inverse, gain_ref[...])
    length = row_refs[0].shape[0]
    for part, row_ref in enumerate(row_refs):
        row_ref[...] = result[part * length : (part + 1) * length, :].astype(bf16)
    pieces = [column_sums(grad_normed * normal), column_sums(grad_normed), second_ref[0:1, :], second_ref[1:2, :]]
    pieces += [third_ref[0:1, :], third_ref[1:2, :], third_ref[2:3, :]]
    pieces += [b_up_ref[:, i : i + features] for i in range(0, b_up_ref.shape[1], features)]
    lines = [piece[:, i : i + 128] for piece in pieces for i in range(0, features, 128)]
    lines.append(jnp.zeros((features - len(lines), 128), f32))
    sum_ref[:, 3 * features :] = jnp.concatenate(lines, 0).astype(bf16)
    hand_out(place_ref[0], sum_ref, grad_w_refs)


class Layout:
    def __init__(self, dp, rows, blocks):
        self.rows = rows
        self.share = share = blocks // rows
        self.blocks = blocks
        self.dp = dp
        place = lax.axis_index("blk")
        self.row = place // share
        self.place = lax.rem(place, share)
        self.device = lax.axis_index("dp") * blocks + place

    def shift_rows(self, step):
        rows, share = self.rows, self.share
        return [
            (a * share + b, ((a + step) % rows) * share + b) for a in range(rows) for b in range(share)
        ]

    def shift_share(self, step):
        rows, share = self.rows, self.share
        return [
            (a * share + b, a * share + (b + step) % share) for a in range(rows) for b in range(share)
        ]

    def bring_rows(self, parts):
        return (parts[0],) + tuple(
            lax.ppermute(parts[step], "blk", self.shift_rows(step)) for step in range(1, self.rows)
        )

    def return_row(self, parts, step):
        arrived = lax.ppermute(parts[step], "blk", self.shift_rows(self.rows - step))
        return (*parts[:step], arrived, *parts[step + 1 :])

    def gather_share(self, values):
        return (values,) + tuple(
            lax.ppermute(values, "blk", self.shift_share(step)) for step in range(1, self.share)
        )

    def return_share(self, parts):
        return (parts[0],) + tuple(
            lax.ppermute(parts[step], "blk", self.shift_share(self.share - step))
            for step in range(1, self.share)
        )


class Sum:
    def __init__(self, layout, values, halves=True):
        share, rows, dp, blocks = layout.share, layout.rows, layout.dp, layout.blocks
        self.layout = layout
        self.parts = values if isinstance(values, tuple) else None
        self.values = (values,)
        own = (share, layout.place, layout.shift_share)
        row = (rows, layout.row, layout.shift_rows)
        bits = [blocks << bit for bit in range((dp - 1).bit_length())]
        bits = list(zip(bits, bits[1:] + bits[:1]))
        self.left = [(self.scatter,) + own]
        self.left += [(self.halve,) + pair for pair in bits] if halves else [(self.scatter_far,)]
        self.left += [(self.scatter,) + row, (self.gather,) + row]
        self.left += [(self.double,) + pair for pair in reversed(bits)]
        self.left += [(self.gather,) + own]

    def part(self, start, size):
        items = [lax.dynamic_slice_in_dim(item, start, size, 0).astype(f32) for item in self.values]
        return sum(items[1:], items[0]).astype(bf16)

    def scatter(self, count, index, shift):
        parts = self.parts
        self.parts = None
        if parts is None:
            size = self.values[0].shape[0] // count
            parts = [self.part(lax.rem(index + step, count) * size, size) for step in range(count)]
        arrived = [lax.ppermute(parts[step], "blk", shift(step)) for step in range(1, count)]
        self.values = (parts[0], *arrived)

    def scatter_far(self):
        dp, device = self.layout.dp, self.layout.device
        count = (dp - 1).bit_length()
        size = self.values[0].shape[0] // dp
        place = device // self.layout.blocks

        def part(step):
            whose = lax.rem(place + step, dp)
            even = sum(((whose >> bit) & 1) << (count - 1 - bit) for bit in range(count))
            odd = sum(((whose >> ((bit + 1) % count)) & 1) << (count - 1 - bit) for bit in range(count))
            return self.part(jnp.where(device % 2 == 0, even, odd) * size, size)

        arrived = [
            lax.ppermute(part(step), "dp", [(d, (d + step) % dp) for d in range(dp)]) for step in range(1, dp)
        ]
        self.values = (part(0), *arrived)

    def gather(self, count, index, shift):
        mine = self.part(0, self.values[0].shape[0])
        part_rows = mine.shape[0]
        arrived = [lax.ppermute(mine, "blk", shift(step)) for step in range(1, count)]
        if not self.left:
            self.values = (mine, *arrived)
            return
        result = jnp.zeros((count * part_rows, mine.shape[1]), mine.dtype)
        result = lax.dynamic_update_slice_in_dim(result, mine, index * part_rows, 0)
        for step, item in enumerate(arrived, 1):
            source = lax.rem(index + count - step, count)
            result = lax.dynamic_update_slice_in_dim(result, item, source * part_rows, 0)
        self.values = (result,)

    def exchange(self, values, even, odd):
        pairs = [(d, d ^ (odd if d % 2 else even)) for d in range(self.layout.dp * self.layout.blocks)]
        return lax.ppermute(values, ("dp", "blk"), pairs)

    def upper(self, even, odd):
        device = self.layout.device
        return (device & jnp.where(device % 2 == 0, even, odd)) != 0

    def halve(self, even, odd):
        half = self.values[0].shape[0] // 2
        upper = self.upper(even, odd).astype(jnp.int32)
        send = self.part((1 - upper) * half, half)
        self.values = (self.part(upper * half, half), self.exchange(send, even, odd))

    def double(self, even, odd):
        (mine,) = self.values
        arrived = self.exchange(mine, even, odd)
        self.values = (
            jnp.where(
                self.upper(even, odd), jnp.concatenate([arrived, mine], 0), jnp.concatenate([mine, arrived], 0)
            ),
        )

    def step(self):
        if self.left:
            action = self.left.pop(0)
            action[0](*action[1:])


def beside(sums, kernel, operands, *others):
    for running in sums:
        running.step()
    result, operands, others, values = join(
        kernel(*operands), operands, others, [running.values for running in sums]
    )
    for running, value in zip(sums, values):
        running.values = value
    return result, operands, *others


def join(*values):
    return lax.optimization_barrier(values)


def body(
    dp,
    blocks,
    target,
    memory,
    target_seg,
    target_keep,
    memory_seg,
    memory_keep,
    cotangent,
    norm1_gain,
    norm1_bias,
    w_qkv,
    w_out,
    norm2_gain,
    norm2_bias,
    w_cross_q,
    w_cross_kv,
    w_cross_out,
    norm3_gain,
    norm3_bias,
    w_up,
    b_up,
    w_down,
    b_down,
):
    rows, length, features = target.shape
    tokens = rows * length
    layout = Layout(dp, rows, blocks)
    target_parts = pack_target(layout.row, target, (target_seg, target_keep, memory_seg, memory_keep))
    target_parts = layout.bring_rows(target_parts)
    memory_parts, cotangent_parts = pack_rows(layout.row, (memory, cotangent))
    norm1_gain, norm1_bias, norm2_gain, norm2_bias, norm3_gain, norm3_bias, b_up, b_down = (
        item.reshape(1, -1)
        for item in (norm1_gain, norm1_bias, norm2_gain, norm2_bias, norm3_gain, norm3_bias, b_up, b_down)
    )
    hidden = w_up.shape[1]
    row, wide_row = shaped((tokens, features)), shaped((tokens, 2 * features))
    row_parts = (shaped((length, features)),) * rows
    sums = shaped((8, features), f32)
    pairs = features // 128

    x, normed1, queries, keyvals, qmask = run(
        functools.partial(project_kernel, rows, length),
        "project",
        target_parts + (norm1_gain, norm1_bias, w_qkv),
        (row, row, row, shaped((tokens, 2 * features + 256)), shaped((tokens, 128))),
    )
    keyvals, memory_parts = join(keyvals, memory_parts)
    keyvals = layout.gather_share(keyvals)
    memory_parts = layout.bring_rows(memory_parts)
    self_masks = (keyvals, 2 * pairs)
    cross_masks = (keyvals, 2 * pairs + 1)
    self_low, self_lse = attend(queries, qmask, keyvals, *self_masks)
    self_low, memory_parts, cotangent_parts = join(self_low, memory_parts, cotangent_parts)
    memory_row, memory_keyvals = run(
        functools.partial(memory_kernel, rows), "memory", memory_parts + (w_cross_kv,), (row, wide_row)
    )
    memory_keyvals = layout.gather_share(memory_keyvals)
    after_self, normed2, cross_query = run(
        after_self_kernel,
        "after_self",
        (x, self_low, w_out, norm2_gain, norm2_bias, w_cross_q),
        (row, row, row),
    )
    cross_query, cotangent_parts, memory_keyvals = join(cross_query, cotangent_parts, memory_keyvals)
    cotangent_parts = layout.bring_rows(cotangent_parts)
    cross_low, cross_lse = attend(cross_query, qmask, memory_keyvals, *cross_masks)
    cross_low, cotangent_parts = join(cross_low, cotangent_parts)
    fed = feed_forward(
        layout.place,
        layout.share,
        after_self,
        cross_low,
        cotangent_parts,
        w_cross_out,
        norm3_gain,
        norm3_bias,
        w_up,
        b_up,
        w_down,
        b_down,
    )
    block_parts, grad_feed = tuple(fed[:rows]), tuple(fed[rows : rows + layout.share])
    grad_after_cross, grad_cross_heads, grad_w_cross_out, grad_b_up, sums3 = fed[rows + layout.share :]

    first = Sum(layout, grad_feed, halves=False)
    calls = 2

    def back(masks, call):
        count = pairs // calls
        return lambda *operands: attend_back(*operands, *masks, call * count, count)

    operands = (cross_query, qmask, grad_cross_heads, cross_low, cross_lse, memory_keyvals)
    for step in range(1, rows - 1):
        block_parts = layout.return_row(block_parts, step)
    grads, operands, block_parts = beside([first], back(cross_masks, 0), operands, block_parts)
    cross_grads, share = [grads[0]], layout.return_share(grads[1:])
    block_parts = layout.return_row(block_parts, rows - 1)
    grads, operands, share, block_parts = beside([first], back(cross_masks, 1), operands, share, block_parts)
    cross_grads.append(grads[0])
    cross_share = list(share) + list(layout.return_share(grads[1:]))
    (grad_after_self, grad_self_heads, grad_w_pair, sums2), _, cross_share = beside(
        [first],
        lambda *operands: run(
            functools.partial(after_self_back_kernel, calls),
            "after_self_back",
            operands,
            (row, row, shaped((features, 2 * features)), sums),
        ),
        tuple(cross_grads) + (after_self, normed2, self_low, grad_after_cross, norm2_gain, w_cross_q, w_out),
        cross_share,
    )
    share = layout.share
    part = shaped((features // share, 5 * features))
    outs, _, grad_self_heads = beside(
        [first],
        lambda *operands: run(
            functools.partial(memory_back_kernel, calls, share),
            "memory_back",
            operands,
            (part,) * share + row_parts,
            layout.place,
            [pltpu.VMEM((features, 5 * features), bf16)],
        ),
        tuple(cross_share) + (memory_row, w_cross_kv, grad_w_cross_out, grad_w_pair),
        grad_self_heads,
    )
    middle = Sum(layout, tuple(outs[:share]))

    calls = 4
    operands = (queries, qmask, grad_self_heads, self_low, self_lse, keyvals)
    memory_parts = tuple(outs[share:])
    self_grads, self_share, sent = [], [], ()
    for call in range(calls):
        if call + 1 < rows:
            memory_parts = layout.return_row(memory_parts, call + 1)
        if call == 1:
            first.step()
        grads, operands, sent, memory_parts, *late = beside(
            [middle] if call in (1, 2) else [first, middle],
            back(self_masks, call),
            operands,
            sent,
            memory_parts,
            *([first.values] if call == 2 else []),
        )
        if late:
            first.values = late[0]
        self_grads.append(grads[0])
        self_share += sent
        sent = layout.return_share(grads[1:])
    self_share += sent
    self_share = join(self_share, self_grads)[0]
    part = shaped((features // share, 3 * features + 128))
    outs, _ = beside(
        [first],
        lambda *operands: run(
            functools.partial(project_back_kernel, calls, share),
            "project_back",
            operands,
            (part,) * share + row_parts,
            layout.place,
            [pltpu.VMEM((features, 3 * features + 128), bf16)],
        ),
        tuple(self_grads)
        + tuple(self_share)
        + (x, normed1, norm1_gain, w_qkv, grad_after_self, sums2, sums3, grad_b_up),
    )
    last = Sum(layout, tuple(outs[:share]))
    target_parts = tuple(outs[share:])
    while first.left:
        first.step()
    far = rows // 2
    for steps in [(), (far,), [step for step in range(1, rows) if step != far]]:
        for step in steps:
            target_parts = layout.return_row(target_parts, step)
        _, _, *late = beside([last, middle], lambda: (), (), *([target_parts] if steps else []))
        target_parts = late[0] if steps else target_parts

    def placed(*parts):
        return place_rows(layout.row, parts)

    target_grad, _ = beside([last, middle], placed, target_parts)
    while middle.left:
        middle.step()
    (grad_w_cross_out, grad_w_cross_q, grad_w_out, grad_w_cross_kv), _ = beside(
        [last],
        lambda *parts: unpack_columns(layout.place, parts, [features, features, features, 2 * features], []),
        middle.values,
    )
    memory_grad, _, block_parts = beside([last], placed, memory_parts, block_parts)
    (grad_w_up, grad_w_down), _ = beside(
        [last], lambda *parts: unpack_feed(layout.place, parts, hidden, features), first.values
    )
    block_out, _ = beside([last], placed, block_parts)
    while last.left:
        last.step()
    grad_w_qkv, *vectors = unpack_columns(layout.place, last.values, [3 * features], [features] * 7 + [hidden])
    (
        grad_norm1_gain,
        grad_norm1_bias,
        grad_norm2_gain,
        grad_norm2_bias,
        grad_norm3_gain,
        grad_norm3_bias,
        grad_b_down,
        grad_b_up,
    ) = [vector.reshape(-1) for vector in vectors]
    return (
        block_out,
        target_grad,
        memory_grad,
        grad_norm1_gain,
        grad_norm1_bias,
        grad_w_qkv,
        grad_w_out,
        grad_norm2_gain,
        grad_norm2_bias,
        grad_w_cross_q,
        grad_w_cross_kv,
        grad_w_cross_out,
        grad_norm3_gain,
        grad_norm3_bias,
        grad_w_up,
        grad_b_up,
        grad_w_down,
        grad_b_down,
    )


def solution(mesh):
    token = P("dp", "blk", None)
    code = P("dp", "blk")
    return jax.shard_map(
        functools.partial(body, mesh.shape["dp"], mesh.shape["blk"]),
        mesh=mesh,
        in_specs=(token, token, code, code, code, code, token) + (P(),) * 15,
        out_specs=(token, token, token) + (P(),) * 15,
        check_vma=False,
    )
```

```python
import functools
import math

import jax
import jax.numpy as jnp
from jax import lax
from jax.experimental import pallas as pl
from jax.experimental.pallas import tpu as pltpu
from jax.sharding import PartitionSpec as P

HEADS = 8
NT = (((1,), (1,)), ((), ()))
NN = (((1,), (0,)), ((), ()))
TN = (((0,), (0,)), ((), ()))
f32 = jnp.float32
bf16 = jnp.bfloat16
VMEM = 60 * 1024 * 1024
SMALL = pl.CostEstimate(flops=1, bytes_accessed=1, transcendentals=0)
QUERY_SCALE = 0.125 * math.log2(math.e)
HIDDEN_MASK = -1e30


def dot(left, right, dims=NN):
    return lax.dot_general(left, right, dims, preferred_element_type=f32)


def normalize(values):
    centered = values - jnp.mean(values, axis=1, keepdims=True)
    inverse = lax.rsqrt(jnp.mean(centered * centered, axis=1, keepdims=True) + 1e-05)
    return centered * inverse, inverse


def normalize_back(grad, normal, inverse, gain):
    grad = grad * gain
    shift = jnp.mean(grad, axis=1, keepdims=True)
    along = jnp.mean(grad * normal, axis=1, keepdims=True)
    return inverse * (grad - shift - normal * along)


def column_sums(values):
    return jnp.sum(values, axis=0, keepdims=True)


def whole(array, *index):
    shape = array.shape
    index = index or (0,) * len(shape)
    return pl.BlockSpec(shape, lambda *grid: index)


def shaped(shape, dtype=bf16):
    return jax.ShapeDtypeStruct(shape, dtype)


def run(kernel, name, operands, outs, place=None, scratch=()):
    specs = [whole(array) for array in operands]
    if place is not None:
        specs = [pl.BlockSpec(memory_space=pltpu.SMEM)] + specs
        operands = (place.reshape(1), *operands)
    return pl.pallas_call(
        kernel,
        grid=(1,),
        in_specs=specs,
        out_specs=[whole(out) for out in outs],
        out_shape=list(outs),
        scratch_shapes=list(scratch),
        compiler_params=pltpu.CompilerParams(vmem_limit_bytes=VMEM),
        cost_estimate=SMALL,
        name=name,
    )(*operands)


def hand_out(place, source_ref, out_refs):
    share, size = len(out_refs), out_refs[0].shape[0]
    for step, out_ref in enumerate(out_refs):
        start = pl.multiple_of((place + step) % share * size, size)
        out_ref[...] = source_ref[pl.ds(start, size), :]


def forward_kernel(parts, *refs):
    q_ref, qmask_ref = refs[:2]
    k_refs, v_refs, kmask_refs = (refs[2 + i * parts : 2 + (i + 1) * parts] for i in range(3))
    o_ref, lse_ref = refs[2 + 3 * parts :]
    low = lax.broadcasted_iota(jnp.int32, (1, 128), 1) < 64
    k = jnp.concatenate([ref[...] for ref in k_refs], 0)
    v = jnp.concatenate([ref[...] for ref in v_refs], 0)
    kmask = jnp.concatenate([ref[...] for ref in kmask_refs], 0)
    q, qmask = q_ref[...], qmask_ref[...]
    outputs = []
    both_scores = [
        dot(jnp.where(low, k, kmask), jnp.where(low, q, qmask), NT),
        dot(jnp.where(low, kmask, k), jnp.where(low, qmask, q), NT),
    ]
    for head, scores in enumerate(both_scores):
        mine = low if head == 0 else ~low
        largest = jnp.max(scores, axis=0, keepdims=True)
        weights = jnp.exp2(scores - largest).astype(bf16)
        both = dot(jnp.where(mine, v, jnp.ones_like(v)), weights, TN)
        total = both[64 - head * 64 : 65 - head * 64]
        lse_ref[0, head : head + 1, :] = largest + jnp.log2(total)
        outputs.append(both[head * 64 : head * 64 + 64] / total)
    o_ref[...] = jnp.concatenate(outputs, 0).T.astype(bf16)


def columns(rows, column, count):
    if callable(column):
        return [pl.BlockSpec((rows, 128), lambda h: (0, column(h)))] * count
    return [pl.BlockSpec((rows, 128), lambda h: (0, column))] * count


def attend(queries, qmask, keyvals, masks, mask_column):
    tokens, features = queries.shape
    parts = len(keyvals)
    length = parts * tokens
    pairs = features // 128
    of_queries = pl.BlockSpec((tokens, 128), lambda h: (0, h))
    return pl.pallas_call(
        functools.partial(forward_kernel, parts),
        grid=(pairs,),
        in_specs=[of_queries]
        + columns(tokens, 0, 1)
        + columns(tokens, lambda h: h, parts)
        + columns(tokens, lambda h: h + pairs, parts)
        + columns(tokens, mask_column, parts),
        out_specs=[of_queries, pl.BlockSpec((1, 2, tokens), lambda h: (h, 0, 0))],
        out_shape=[shaped((tokens, features)), shaped((pairs, 2, tokens), f32)],
        compiler_params=pltpu.CompilerParams(vmem_limit_bytes=VMEM),
        cost_estimate=SMALL,
        name="attend",
    )(queries, qmask, *keyvals, *keyvals, *masks)


def backward_kernel(parts, *refs):
    q_ref, qmask_ref, do_ref, o_ref, lse_ref = refs[:5]
    k_refs, v_refs, kmask_refs = (refs[5 + i * parts : 5 + (i + 1) * parts] for i in range(3))
    dq_ref, dkv_refs = refs[5 + 3 * parts], refs[6 + 3 * parts :]
    low = lax.broadcasted_iota(jnp.int32, (1, 128), 1) < 64
    q, qmask, grad = q_ref[...], qmask_ref[...], do_ref[...]
    tokens = q.shape[0]
    product = grad.astype(f32) * o_ref[...].astype(f32)
    upper = product.astype(bf16)
    lower = (product - upper.astype(f32)).astype(bf16)
    rows = lax.broadcasted_iota(jnp.int32, (8, 128), 0)
    lanes = lax.broadcasted_iota(jnp.int32, (8, 128), 1)
    pick = jnp.where(rows == lanes // 64, 1.0, 0.0).astype(bf16)
    delta = dot(pick, upper, NT) + dot(pick, lower, NT)
    lse = lse_ref[0]
    zero = jnp.zeros_like(grad)
    q_heads = [jnp.where(low, q, qmask), jnp.where(low, qmask, q)]
    grad_heads = [jnp.where(low, grad, zero), jnp.where(low, zero, grad)]
    dq = [jnp.zeros((64, tokens), f32)] * 2
    for part in range(parts):
        k, v = k_refs[part][...], v_refs[part][...]
        kmask = kmask_refs[part][...]
        dk, dv = [], []
        for head in range(2):
            k_head = jnp.where(low, k, kmask) if head == 0 else jnp.where(low, kmask, k)
            weights = jnp.exp2(dot(k_head, q_heads[head], NT) - lse[head : head + 1, :])
            grad_weights = dot(v, grad_heads[head], NT)
            grad_scores = (weights * (grad_weights - delta[head : head + 1, :])).astype(bf16)
            dv.append(dot(weights.astype(bf16), grad))
            dk.append(dot(grad_scores, q))
            dq[head] = dq[head] + dot(k, grad_scores, TN)[head * 64 : head * 64 + 64]
        dkv_refs[part][:, :128] = (jnp.where(low, dk[0], dk[1]) * math.log(2.0)).astype(bf16)
        dkv_refs[part][:, 128:] = jnp.where(low, dv[0], dv[1]).astype(bf16)
    dq_ref[...] = (jnp.concatenate(dq, 0).T * 0.125).astype(bf16)


def attend_back(queries, qmask, grad, outputs, lse, keyvals, masks, mask_column, first, count):
    tokens, features = queries.shape
    parts = len(keyvals)
    length = parts * tokens
    pairs = features // 128
    of_queries = pl.BlockSpec((tokens, 128), lambda h: (0, h + first))
    return pl.pallas_call(
        functools.partial(backward_kernel, parts),
        grid=(count,),
        in_specs=[
            of_queries,
            pl.BlockSpec((tokens, 128), lambda h: (0, 0)),
            of_queries,
            of_queries,
            pl.BlockSpec((1, 2, tokens), lambda h: (h + first, 0, 0)),
        ]
        + columns(tokens, lambda h: h + first, parts)
        + columns(tokens, lambda h: h + first + pairs, parts)
        + columns(tokens, mask_column, parts),
        out_specs=[pl.BlockSpec((tokens, 128), lambda h: (0, h))]
        + [pl.BlockSpec((tokens, 256), lambda h: (0, h))] * parts,
        out_shape=[shaped((tokens, count * 128))] + [shaped((tokens, count * 256))] * parts,
        compiler_params=pltpu.CompilerParams(vmem_limit_bytes=VMEM),
        cost_estimate=SMALL,
        name="attend_back",
    )(queries, qmask, grad, outputs, lse, *keyvals, *keyvals, *masks)


def mask_rows(codes, of_queries):
    places = lax.broadcasted_iota(jnp.int32, (128, codes.shape[1]), 0) % 64
    codes = jnp.broadcast_to(codes.astype(jnp.int32), places.shape)
    if of_queries:
        mask = jnp.where(codes % 4 == places, 1.0, 0.0)
    else:
        mask = jnp.where((codes != places) & (places < 3), HIDDEN_MASK, 0.0)
    return mask.T.astype(bf16)


def project_kernel(parts, length, *refs):
    x_refs = refs[:parts]
    gain_ref, bias_ref, w_ref, x_ref, normed_ref, query_ref, keyvals_ref, qmask_ref = refs[parts:]
    features = x_ref.shape[1]
    for part in range(parts):
        rows = slice(part * length, (part + 1) * length)
        low = x_refs[part][:length, :]
        x_ref[rows, :] = low
        normal, inverse = normalize(low.astype(f32))
        normed = (normal * gain_ref[...] + bias_ref[...]).astype(bf16)
        normed_ref[rows, :] = normed
        projected = dot(normed, w_ref[...])
        query_ref[rows, :] = (projected[:, :features] * QUERY_SCALE).astype(bf16)
        keyvals_ref[rows, : 2 * features] = projected[:, features:].astype(bf16)
        codes = x_refs[part][length : length + 16, :].astype(f32)[0:1, :]
        qmask_ref[rows, :] = mask_rows(codes[:, :length], True)
        keyvals_ref[rows, 2 * features : 2 * features + 128] = mask_rows(codes[:, :length], False)
        keyvals_ref[rows, 2 * features + 128 :] = mask_rows(codes[:, length : 2 * length], False)


def row_specs(array, count):
    shape = (1,) + array.shape[1:]
    return [
        pl.BlockSpec(shape, lambda i, row, step=step: ((row[0] + step) % count, 0, 0)) for step in range(count)
    ]


def pack_target(row, target, codes):
    count, length, features = target.shape

    def kernel(row_ref, *refs):
        seg_ref, keep_ref, memory_seg_ref, memory_keep_ref = refs[count : count + 4]
        for step in range(count):
            out_ref = refs[count + 4 + step]
            out_ref[:length, :] = refs[step][0]
            which = pl.ds((row_ref[0] + step) % count, 1)
            pieces = [
                jnp.where(keep[which, :] == 1, seg[which, :], seg[which, :] + 4).astype(f32)
                for seg, keep in ((seg_ref, keep_ref), (memory_seg_ref, memory_keep_ref))
            ]
            if features > 2 * length:
                pieces.append(jnp.zeros((1, features - 2 * length), f32))
            pieces = jnp.concatenate(pieces, 1)
            out_ref[length:, :] = jnp.broadcast_to(pieces, (16, features)).astype(bf16)

    out = shaped((length + 16, features))
    return pl.pallas_call(
        kernel,
        grid_spec=pltpu.PrefetchScalarGridSpec(
            num_scalar_prefetch=1,
            grid=(1,),
            in_specs=row_specs(target, count) + [whole(item) for item in codes],
            out_specs=[whole(out)] * count,
        ),
        out_shape=[out] * count,
        compiler_params=pltpu.CompilerParams(vmem_limit_bytes=VMEM),
        cost_estimate=SMALL,
        name="pack_target",
    )(row.reshape(1), *[target] * count, *codes)


def pack_rows(row, arrays):
    count, length, features = arrays[0].shape
    total = count * len(arrays)

    def kernel(row_ref, *refs):
        for i in range(total):
            refs[total + i][...] = refs[i][0]

    out = shaped((length, features), arrays[0].dtype)
    outs = pl.pallas_call(
        kernel,
        grid_spec=pltpu.PrefetchScalarGridSpec(
            num_scalar_prefetch=1,
            grid=(1,),
            in_specs=[spec for array in arrays for spec in row_specs(array, count)],
            out_specs=[whole(out)] * total,
        ),
        out_shape=[out] * total,
        compiler_params=pltpu.CompilerParams(vmem_limit_bytes=VMEM),
        cost_estimate=SMALL,
        name="pack_rows",
    )(row.reshape(1), *[array for array in arrays for _ in range(count)])
    return [tuple(outs[i : i + count]) for i in range(0, total, count)]


def place_rows(row, parts):
    count = len(parts)
    length, features = parts[0].shape

    def kernel(row_ref, *refs):
        for step in range(count):
            refs[count][pl.ds((row_ref[0] + step) % count, 1), :, :] = refs[step][...].astype(f32)[None]

    out = shaped((count, length, features), f32)
    return pl.pallas_call(
        kernel,
        grid_spec=pltpu.PrefetchScalarGridSpec(
            num_scalar_prefetch=1,
            grid=(1,),
            in_specs=[whole(part) for part in parts],
            out_specs=whole(out),
        ),
        out_shape=out,
        compiler_params=pltpu.CompilerParams(vmem_limit_bytes=VMEM),
        cost_estimate=SMALL,
        name="place_rows",
    )(row.reshape(1), *parts)


def unpack_feed(place, parts, hidden, block):
    share = len(parts)
    features = parts[0].shape[1]
    steps = hidden // block
    each = steps // share

    def kernel(place_ref, *refs):
        up_ref, down_ref = refs[share:]
        owner = pl.program_id(0) // each
        for step in range(share):

            @pl.when((place_ref[0] + share - owner) % share == step)
            def _():
                up_ref[...] = refs[step][:features, :].astype(f32)
                down_ref[...] = refs[step][features:, :].astype(f32)

    return pl.pallas_call(
        kernel,
        grid_spec=pltpu.PrefetchScalarGridSpec(
            num_scalar_prefetch=1,
            grid=(steps,),
            in_specs=[pl.BlockSpec((2 * features, features), lambda j, place: (j % each, 0))] * share,
            out_specs=[
                pl.BlockSpec((features, block), lambda j, place: (0, j)),
                pl.BlockSpec((block, features), lambda j, place: (j, 0)),
            ],
        ),
        out_shape=[shaped((features, hidden), f32), shaped((hidden, features), f32)],
        compiler_params=pltpu.CompilerParams(vmem_limit_bytes=VMEM),
        cost_estimate=SMALL,
        name="unpack_feed",
    )(place.reshape(1), *parts)


def unpack_columns(place, parts, widths, vectors):
    share = len(parts)
    rows = parts[0].shape[0]
    last = sum(widths)

    def kernel(place_ref, *refs):
        for step in range(share):

            @pl.when((place_ref[0] + share - pl.program_id(0)) % share == step)
            def _():
                start = 0
                for width, out_ref in zip(widths, refs[share:]):
                    out_ref[...] = refs[step][:, start : start + width].astype(f32)
                    start += width

                if not vectors:
                    return

                @pl.when(pl.program_id(0) == 0)
                def _():
                    line = 0
                    values = refs[step][:64, last:].astype(f32)
                    for length, out_ref in zip(vectors, refs[share + len(widths) :]):
                        for i in range(0, length, 128):
                            out_ref[:, i : i + 128] = values[line : line + 1, :]
                            line += 1

    return pl.pallas_call(
        kernel,
        grid_spec=pltpu.PrefetchScalarGridSpec(
            num_scalar_prefetch=1,
            grid=(share,),
            in_specs=[pl.BlockSpec(part.shape, lambda j, place: (0, 0)) for part in parts],
            out_specs=[pl.BlockSpec((rows, width), lambda j, place: (j, 0)) for width in widths]
            + [pl.BlockSpec((1, length), lambda j, place: (0, 0)) for length in vectors],
        ),
        out_shape=[shaped((share * rows, width), f32) for width in widths]
        + [shaped((1, length), f32) for length in vectors],
        compiler_params=pltpu.CompilerParams(vmem_limit_bytes=VMEM),
        cost_estimate=SMALL,
        name="unpack_columns",
    )(place.reshape(1), *parts)


def memory_kernel(parts, *refs):
    part_refs = refs[:parts]
    w_ref, memory_ref, keyvals_ref = refs[parts:]
    length = part_refs[0].shape[0]
    for part in range(parts):
        rows = slice(part * length, (part + 1) * length)
        memory = part_refs[part][...]
        memory_ref[rows, :] = memory
        keyvals_ref[rows, :] = dot(memory, w_ref[...]).astype(bf16)


def after_self_kernel(x_ref, attended_ref, w_out_ref, gain_ref, bias_ref, w_q_ref, after_ref, normed_ref, query_ref):
    after = x_ref[...].astype(f32) + dot(attended_ref[...], w_out_ref[...])
    after_ref[...] = after.astype(bf16)
    normal, inverse = normalize(after)
    normed = (normal * gain_ref[...] + bias_ref[...]).astype(bf16)
    normed_ref[...] = normed
    query_ref[...] = (dot(normed, w_q_ref[...]) * QUERY_SCALE).astype(bf16)


def feed_kernel(parts, share, each, place_ref, *refs):
    after_ref, attended_ref, w_out_ref, gain_ref, bias_ref, w_up_ref, b_up_ref, w_down_ref, b_down_ref = refs[:9]
    cotangent_refs, refs = refs[9 : 9 + parts], refs[9 + parts :]
    out_refs, grad_w_refs, refs = refs[:parts], refs[parts : parts + share], refs[parts + share :]
    grad_ref, grad_heads_ref, grad_out_ref, grad_b_up_ref, sums_ref = refs[:5]
    normed_ref, x_ref, total_ref, back_ref, cotangent_ref = refs[5:]
    features = w_up_ref.shape[0]
    length = out_refs[0].shape[0]
    step = pl.program_id(0)

    @pl.when(step == 0)
    def _():
        for part, part_ref in enumerate(cotangent_refs):
            cotangent_ref[part * length : (part + 1) * length, :] = part_ref[...]
        x = after_ref[...].astype(f32) + dot(attended_ref[...], w_out_ref[...])
        x_ref[...] = x
        total_ref[...] = x + b_down_ref[...]
        normal, inverse = normalize(x)
        normed_ref[...] = (normal * gain_ref[...] + bias_ref[...]).astype(bf16)
        back_ref[...] = jnp.zeros_like(back_ref)

    cotangent = cotangent_ref[...]
    normed, w_up, w_down = normed_ref[...], w_up_ref[...], w_down_ref[...]
    u = dot(normed, w_up) + b_up_ref[...]
    slope = math.sqrt(2.0 / math.pi)
    squared = u * u
    bent = jnp.tanh(u * (slope + slope * 0.044715 * squared))
    half = 0.5 + 0.5 * bent
    activated = (u * half).astype(bf16)
    gelu_slope = half + (0.5 * u) * (1.0 - bent * bent) * (slope + 3.0 * slope * 0.044715 * squared)
    total_ref[...] += dot(activated, w_down)
    grad_hidden = (dot(cotangent, w_down, NT) * gelu_slope).astype(bf16)
    grad_up = dot(normed, grad_hidden, TN).astype(bf16)
    grad_down = dot(activated, cotangent, TN).astype(bf16)
    for part, grad_w_ref in enumerate(grad_w_refs):

        @pl.when(step // each == share - 1 - part)
        def _():
            for i in range(0, grad_up.shape[1], features):
                grad_w_ref[2 * i : 2 * i + features, :] = grad_up[:, i : i + features]
                grad_w_ref[2 * i + features : 2 * i + 2 * features, :] = grad_down[i : i + features, :]

    grad_b_up_ref[...] = column_sums(grad_hidden.astype(f32))
    back_ref[...] += dot(grad_hidden, w_up, NT)

    @pl.when(step == pl.num_programs(0) - 1)
    def _():
        for part, out_ref in enumerate(out_refs):
            out_ref[...] = total_ref[part * length : (part + 1) * length, :].astype(bf16)
        normal, inverse = normalize(x_ref[...])
        grad_normed = back_ref[...]
        grad_out = cotangent.astype(f32)
        sums_ref[0:1, :] = column_sums(grad_normed * normal)
        sums_ref[1:2, :] = column_sums(grad_normed)
        sums_ref[2:3, :] = column_sums(grad_out)
        grad = grad_out + normalize_back(grad_normed, normal, inverse, gain_ref[...])
        low = grad.astype(bf16)
        grad_ref[...] = low
        grad_heads_ref[...] = dot(low, w_out_ref[...], NT).astype(bf16)
        grad_out_ref[...] = dot(attended_ref[...], low, TN).astype(bf16)


def feed_forward(place, share, after_self, attended, cotangents, w_out, gain, bias, w_up, b_up, w_down, b_down):
    tokens, features = after_self.shape
    hidden = w_up.shape[1]
    block = features * (1 if hidden // features // share % 2 else 2)
    parts = len(cotangents)
    length = tokens // parts
    steps = hidden // block
    each = steps // share
    row, one, square = shaped((tokens, features)), shaped((1, features)), shaped((features, features))
    part_row = shaped((length, features))

    def now(j, place):
        return ((place[0] + share - 1 - j // each) % share) * each + j % each

    def grad_spec(part):
        begin = (share - 1 - part) * each
        return pl.BlockSpec(
            (2 * block, features), lambda j, place: (jnp.clip(j - begin, 0, each - 1), 0)
        )

    return pl.pallas_call(
        functools.partial(feed_kernel, parts, share, each),
        grid_spec=pltpu.PrefetchScalarGridSpec(
            num_scalar_prefetch=1,
            grid=(steps,),
            in_specs=[
                whole(row),
                whole(row),
                whole(square),
                whole(one),
                whole(one),
                pl.BlockSpec((features, block), lambda j, place: (0, now(j, place))),
                pl.BlockSpec((1, block), lambda j, place: (0, now(j, place))),
                pl.BlockSpec((block, features), lambda j, place: (now(j, place), 0)),
                whole(one),
            ]
            + [whole(part_row)] * parts,
            out_specs=[whole(part_row)] * parts
            + [grad_spec(part) for part in range(share)]
            + [
                whole(row),
                whole(row),
                whole(square),
                pl.BlockSpec((1, block), lambda j, place: (0, now(j, place))),
                whole(shaped((8, features))),
            ],
            scratch_shapes=[
                pltpu.VMEM((tokens, features), bf16),
                pltpu.VMEM((tokens, features), f32),
                pltpu.VMEM((tokens, features), f32),
                pltpu.VMEM((tokens, features), f32),
                pltpu.VMEM((tokens, features), bf16),
            ],
        ),
        out_shape=[part_row] * parts
        + [shaped((each * 2 * block, features))] * share
        + [
            row,
            row,
            square,
            shaped((1, hidden), f32),
            shaped((8, features), f32),
        ],
        compiler_params=pltpu.CompilerParams(vmem_limit_bytes=VMEM),
        cost_estimate=SMALL,
        name="feed_forward",
    )(place.reshape(1), after_self, attended, w_out, gain, bias, w_up, b_up, w_down, b_down, *cotangents)


def after_self_back_kernel(calls, *refs):
    dq_refs = refs[:calls]
    after_ref, normed_ref, attended_ref, grad_after_ref, gain_ref, w_q_ref, w_out_ref = refs[calls : calls + 7]
    grad_ref, grad_heads_ref, grad_w_ref, sums_ref = refs[calls + 7 :]
    features = after_ref.shape[1]
    grad_query = jnp.concatenate([ref[...] for ref in dq_refs], 1)
    grad_normed = dot(grad_query, w_q_ref[...], NT)
    normal, inverse = normalize(after_ref[...].astype(f32))
    sums_ref[0:1, :] = column_sums(grad_normed * normal)
    sums_ref[1:2, :] = column_sums(grad_normed)
    grad = grad_after_ref[...].astype(f32) + normalize_back(grad_normed, normal, inverse, gain_ref[...])
    low = grad.astype(bf16)
    grad_ref[...] = low
    grad_heads_ref[...] = dot(low, w_out_ref[...], NT).astype(bf16)
    grad_w_ref[:, :features] = dot(normed_ref[...], grad_query, TN).astype(bf16)
    grad_w_ref[:, features:] = dot(attended_ref[...], low, TN).astype(bf16)


def summed_keyvals(refs):
    keys, values = [], []
    for call in refs:
        total = sum([ref[...].astype(f32) for ref in call[1:]], call[0][...].astype(f32)).astype(bf16)
        for pair in range(total.shape[1] // 256):
            keys.append(total[:, pair * 256 : pair * 256 + 128])
            values.append(total[:, pair * 256 + 128 : pair * 256 + 256])
    return keys + values


def memory_back_kernel(calls, parts, place_ref, *refs):
    *refs, sum_ref = refs
    grad_refs = [refs[call * parts : (call + 1) * parts] for call in range(calls)]
    memory_ref, w_ref, out_ref, pair_ref = refs[calls * parts : calls * parts + 4]
    grad_w_refs = refs[calls * parts + 4 : calls * parts + 4 + parts]
    row_refs = refs[calls * parts + 4 + parts :]
    features = out_ref.shape[1]
    grad = jnp.concatenate(summed_keyvals(grad_refs), 1)
    result = dot(grad, w_ref[...], NT).astype(bf16)
    length = row_refs[0].shape[0]
    for part, row_ref in enumerate(row_refs):
        row_ref[...] = result[part * length : (part + 1) * length, :]
    sum_ref[:, :features] = out_ref[...]
    sum_ref[:, features : 3 * features] = pair_ref[...]
    sum_ref[:, 3 * features :] = dot(memory_ref[...], grad, TN).astype(bf16)
    hand_out(place_ref[0], sum_ref, grad_w_refs)


def project_back_kernel(calls, parts, place_ref, *refs):
    *refs, sum_ref = refs
    dq_refs = refs[:calls]
    refs = refs[calls:]
    grad_refs = [refs[call * parts : (call + 1) * parts] for call in range(calls)]
    refs = refs[calls * parts :]
    x_ref, normed_ref, gain_ref, w_ref, grad_after_ref, second_ref, third_ref, b_up_ref = refs[:8]
    grad_w_refs, row_refs = refs[8 : 8 + parts], refs[8 + parts :]
    grad = jnp.concatenate([ref[...] for ref in dq_refs] + summed_keyvals(grad_refs), 1)
    features = x_ref.shape[1]
    sum_ref[:, : 3 * features] = dot(normed_ref[...], grad, TN).astype(bf16)
    grad_normed = dot(grad, w_ref[...], NT)
    normal, inverse = normalize(x_ref[...].astype(f32))
    result = grad_after_ref[...].astype(f32) + normalize_back(grad_normed, normal, inverse, gain_ref[...])
    length = row_refs[0].shape[0]
    for part, row_ref in enumerate(row_refs):
        row_ref[...] = result[part * length : (part + 1) * length, :].astype(bf16)
    pieces = [column_sums(grad_normed * normal), column_sums(grad_normed), second_ref[0:1, :], second_ref[1:2, :]]
    pieces += [third_ref[0:1, :], third_ref[1:2, :], third_ref[2:3, :]]
    pieces += [b_up_ref[:, i : i + features] for i in range(0, b_up_ref.shape[1], features)]
    lines = [piece[:, i : i + 128] for piece in pieces for i in range(0, features, 128)]
    lines.append(jnp.zeros((features - len(lines), 128), f32))
    sum_ref[:, 3 * features :] = jnp.concatenate(lines, 0).astype(bf16)
    hand_out(place_ref[0], sum_ref, grad_w_refs)


class Layout:
    def __init__(self, dp, rows, blocks):
        self.rows = rows
        self.share = share = blocks // rows
        self.blocks = blocks
        self.dp = dp
        place = lax.axis_index("blk")
        self.row = place // share
        self.place = lax.rem(place, share)
        self.device = lax.axis_index("dp") * blocks + place

    def shift_rows(self, step):
        rows, share = self.rows, self.share
        return [
            (a * share + b, ((a + step) % rows) * share + b) for a in range(rows) for b in range(share)
        ]

    def shift_share(self, step):
        rows, share = self.rows, self.share
        return [
            (a * share + b, a * share + (b + step) % share) for a in range(rows) for b in range(share)
        ]

    def bring_rows(self, parts):
        return (parts[0],) + tuple(
            lax.ppermute(parts[step], "blk", self.shift_rows(step)) for step in range(1, self.rows)
        )

    def return_row(self, parts, step):
        arrived = lax.ppermute(parts[step], "blk", self.shift_rows(self.rows - step))
        return (*parts[:step], arrived, *parts[step + 1 :])

    def gather_share(self, values):
        return (values,) + tuple(
            lax.ppermute(values, "blk", self.shift_share(step)) for step in range(1, self.share)
        )

    def return_share(self, parts):
        return (parts[0],) + tuple(
            lax.ppermute(parts[step], "blk", self.shift_share(self.share - step))
            for step in range(1, self.share)
        )


class Sum:
    def __init__(self, layout, values, halves=True):
        share, rows, dp, blocks = layout.share, layout.rows, layout.dp, layout.blocks
        self.layout = layout
        self.parts = values if isinstance(values, tuple) else None
        self.values = (values,)
        own = (share, layout.place, layout.shift_share)
        row = (rows, layout.row, layout.shift_rows)
        bits = [blocks << bit for bit in range((dp - 1).bit_length())]
        bits = list(zip(bits, bits[1:] + bits[:1]))
        self.left = [(self.scatter,) + own]
        self.left += [(self.halve,) + pair for pair in bits] if halves else [(self.scatter_far,)]
        self.left += [(self.scatter,) + row, (self.gather,) + row]
        self.left += [(self.double,) + pair for pair in reversed(bits)]
        self.left += [(self.gather,) + own]

    def part(self, start, size):
        items = [lax.dynamic_slice_in_dim(item, start, size, 0).astype(f32) for item in self.values]
        return sum(items[1:], items[0]).astype(bf16)

    def scatter(self, count, index, shift):
        parts = self.parts
        self.parts = None
        if parts is None:
            size = self.values[0].shape[0] // count
            parts = [self.part(lax.rem(index + step, count) * size, size) for step in range(count)]
        arrived = [lax.ppermute(parts[step], "blk", shift(step)) for step in range(1, count)]
        self.values = (parts[0], *arrived)

    def scatter_far(self):
        dp, device = self.layout.dp, self.layout.device
        count = (dp - 1).bit_length()
        size = self.values[0].shape[0] // dp
        place = device // self.layout.blocks

        def part(step):
            whose = lax.rem(place + step, dp)
            even = sum(((whose >> bit) & 1) << (count - 1 - bit) for bit in range(count))
            odd = sum(((whose >> ((bit + 1) % count)) & 1) << (count - 1 - bit) for bit in range(count))
            return self.part(jnp.where(device % 2 == 0, even, odd) * size, size)

        arrived = [
            lax.ppermute(part(step), "dp", [(d, (d + step) % dp) for d in range(dp)]) for step in range(1, dp)
        ]
        self.values = (part(0), *arrived)

    def gather(self, count, index, shift):
        mine = self.part(0, self.values[0].shape[0])
        part_rows = mine.shape[0]
        arrived = [lax.ppermute(mine, "blk", shift(step)) for step in range(1, count)]
        if not self.left:
            self.values = (mine, *arrived)
            return
        result = jnp.zeros((count * part_rows, mine.shape[1]), mine.dtype)
        result = lax.dynamic_update_slice_in_dim(result, mine, index * part_rows, 0)
        for step, item in enumerate(arrived, 1):
            source = lax.rem(index + count - step, count)
            result = lax.dynamic_update_slice_in_dim(result, item, source * part_rows, 0)
        self.values = (result,)

    def exchange(self, values, even, odd):
        pairs = [(d, d ^ (odd if d % 2 else even)) for d in range(self.layout.dp * self.layout.blocks)]
        return lax.ppermute(values, ("dp", "blk"), pairs)

    def upper(self, even, odd):
        device = self.layout.device
        return (device & jnp.where(device % 2 == 0, even, odd)) != 0

    def halve(self, even, odd):
        half = self.values[0].shape[0] // 2
        upper = self.upper(even, odd).astype(jnp.int32)
        send = self.part((1 - upper) * half, half)
        self.values = (self.part(upper * half, half), self.exchange(send, even, odd))

    def double(self, even, odd):
        (mine,) = self.values
        arrived = self.exchange(mine, even, odd)
        self.values = (
            jnp.where(
                self.upper(even, odd), jnp.concatenate([arrived, mine], 0), jnp.concatenate([mine, arrived], 0)
            ),
        )

    def step(self):
        if self.left:
            action = self.left.pop(0)
            action[0](*action[1:])


def beside(sums, kernel, operands, *others):
    for running in sums:
        running.step()
    result, operands, others, values = join(
        kernel(*operands), operands, others, [running.values for running in sums]
    )
    for running, value in zip(sums, values):
        running.values = value
    return result, operands, *others


def join(*values):
    return lax.optimization_barrier(values)


def body(
    dp,
    blocks,
    target,
    memory,
    target_seg,
    target_keep,
    memory_seg,
    memory_keep,
    cotangent,
    norm1_gain,
    norm1_bias,
    w_qkv,
    w_out,
    norm2_gain,
    norm2_bias,
    w_cross_q,
    w_cross_kv,
    w_cross_out,
    norm3_gain,
    norm3_bias,
    w_up,
    b_up,
    w_down,
    b_down,
):
    rows, length, features = target.shape
    tokens = rows * length
    layout = Layout(dp, rows, blocks)
    target_parts = pack_target(layout.row, target, (target_seg, target_keep, memory_seg, memory_keep))
    target_parts = layout.bring_rows(target_parts)
    memory_parts, cotangent_parts = pack_rows(layout.row, (memory, cotangent))
    norm1_gain, norm1_bias, norm2_gain, norm2_bias, norm3_gain, norm3_bias, b_up, b_down = (
        item.reshape(1, -1)
        for item in (norm1_gain, norm1_bias, norm2_gain, norm2_bias, norm3_gain, norm3_bias, b_up, b_down)
    )
    hidden = w_up.shape[1]
    row, wide_row = shaped((tokens, features)), shaped((tokens, 2 * features))
    row_parts = (shaped((length, features)),) * rows
    sums = shaped((8, features), f32)
    pairs = features // 128

    x, normed1, queries, keyvals, qmask = run(
        functools.partial(project_kernel, rows, length),
        "project",
        target_parts + (norm1_gain, norm1_bias, w_qkv),
        (row, row, row, shaped((tokens, 2 * features + 256)), shaped((tokens, 128))),
    )
    keyvals, memory_parts = join(keyvals, memory_parts)
    keyvals = layout.gather_share(keyvals)
    memory_parts = layout.bring_rows(memory_parts)
    self_masks = (keyvals, 2 * pairs)
    cross_masks = (keyvals, 2 * pairs + 1)
    self_low, self_lse = attend(queries, qmask, keyvals, *self_masks)
    self_low, memory_parts, cotangent_parts = join(self_low, memory_parts, cotangent_parts)
    memory_row, memory_keyvals = run(
        functools.partial(memory_kernel, rows), "memory", memory_parts + (w_cross_kv,), (row, wide_row)
    )
    memory_keyvals = layout.gather_share(memory_keyvals)
    after_self, normed2, cross_query = run(
        after_self_kernel,
        "after_self",
        (x, self_low, w_out, norm2_gain, norm2_bias, w_cross_q),
        (row, row, row),
    )
    cross_query, cotangent_parts, memory_keyvals = join(cross_query, cotangent_parts, memory_keyvals)
    cotangent_parts = layout.bring_rows(cotangent_parts)
    cross_low, cross_lse = attend(cross_query, qmask, memory_keyvals, *cross_masks)
    cross_low, cotangent_parts = join(cross_low, cotangent_parts)
    fed = feed_forward(
        layout.place,
        layout.share,
        after_self,
        cross_low,
        cotangent_parts,
        w_cross_out,
        norm3_gain,
        norm3_bias,
        w_up,
        b_up,
        w_down,
        b_down,
    )
    block_parts, grad_feed = tuple(fed[:rows]), tuple(fed[rows : rows + layout.share])
    grad_after_cross, grad_cross_heads, grad_w_cross_out, grad_b_up, sums3 = fed[rows + layout.share :]

    first = Sum(layout, grad_feed, halves=False)
    calls = 2

    def back(masks, call):
        count = pairs // calls
        return lambda *operands: attend_back(*operands, *masks, call * count, count)

    operands = (cross_query, qmask, grad_cross_heads, cross_low, cross_lse, memory_keyvals)
    for step in range(1, rows - 1):
        block_parts = layout.return_row(block_parts, step)
    grads, operands, block_parts = beside([first], back(cross_masks, 0), operands, block_parts)
    cross_grads, share = [grads[0]], layout.return_share(grads[1:])
    block_parts = layout.return_row(block_parts, rows - 1)
    grads, operands, share, block_parts = beside([first], back(cross_masks, 1), operands, share, block_parts)
    cross_grads.append(grads[0])
    cross_share = list(share) + list(layout.return_share(grads[1:]))
    (grad_after_self, grad_self_heads, grad_w_pair, sums2), _, cross_share = beside(
        [first],
        lambda *operands: run(
            functools.partial(after_self_back_kernel, calls),
            "after_self_back",
            operands,
            (row, row, shaped((features, 2 * features)), sums),
        ),
        tuple(cross_grads) + (after_self, normed2, self_low, grad_after_cross, norm2_gain, w_cross_q, w_out),
        cross_share,
    )
    share = layout.share
    part = shaped((features // share, 5 * features))
    outs, _, grad_self_heads = beside(
        [first],
        lambda *operands: run(
            functools.partial(memory_back_kernel, calls, share),
            "memory_back",
            operands,
            (part,) * share + row_parts,
            layout.place,
            [pltpu.VMEM((features, 5 * features), bf16)],
        ),
        tuple(cross_share) + (memory_row, w_cross_kv, grad_w_cross_out, grad_w_pair),
        grad_self_heads,
    )
    middle = Sum(layout, tuple(outs[:share]))

    calls = 4
    operands = (queries, qmask, grad_self_heads, self_low, self_lse, keyvals)
    memory_parts = tuple(outs[share:])
    self_grads, self_share, sent = [], [], ()
    for call in range(calls):
        if call + 1 < rows:
            memory_parts = layout.return_row(memory_parts, call + 1)
        if call == 1:
            first.step()
        grads, operands, sent, memory_parts, *late = beside(
            [middle] if call in (1, 2) else [first, middle],
            back(self_masks, call),
            operands,
            sent,
            memory_parts,
            *([first.values] if call == 2 else []),
        )
        if late:
            first.values = late[0]
        self_grads.append(grads[0])
        self_share += sent
        sent = layout.return_share(grads[1:])
    self_share += sent
    self_share = join(self_share, self_grads)[0]
    part = shaped((features // share, 3 * features + 128))
    outs, _ = beside(
        [first],
        lambda *operands: run(
            functools.partial(project_back_kernel, calls, share),
            "project_back",
            operands,
            (part,) * share + row_parts,
            layout.place,
            [pltpu.VMEM((features, 3 * features + 128), bf16)],
        ),
        tuple(self_grads)
        + tuple(self_share)
        + (x, normed1, norm1_gain, w_qkv, grad_after_self, sums2, sums3, grad_b_up),
    )
    last = Sum(layout, tuple(outs[:share]))
    target_parts = tuple(outs[share:])
    while first.left:
        first.step()
    far = rows // 2
    block_out = None

    def placed(*parts):
        return place_rows(layout.row, parts)

    for steps in [(), (far,), [step for step in range(1, rows) if step != far]]:
        for step in steps:
            target_parts = layout.return_row(target_parts, step)
        job, taken = (placed, block_parts) if steps == (far,) else ((lambda: ()), ())
        result, _, *late = beside([last, middle], job, taken, *([target_parts] if steps else []))
        target_parts = late[0] if steps else target_parts
        block_out = result if taken else block_out

    target_grad, _ = beside([last, middle], placed, target_parts)
    while middle.left:
        middle.step()
    (grad_w_cross_out, grad_w_cross_q, grad_w_out, grad_w_cross_kv), _ = beside(
        [last],
        lambda *parts: unpack_columns(layout.place, parts, [features, features, features, 2 * features], []),
        middle.values,
    )
    memory_grad, _ = beside([last], placed, memory_parts)
    (grad_w_up, grad_w_down), _ = beside(
        [last], lambda *parts: unpack_feed(layout.place, parts, hidden, features), first.values
    )
    while last.left:
        last.step()
    grad_w_qkv, *vectors = unpack_columns(layout.place, last.values, [3 * features], [features] * 7 + [hidden])
    (
        grad_norm1_gain,
        grad_norm1_bias,
        grad_norm2_gain,
        grad_norm2_bias,
        grad_norm3_gain,
        grad_norm3_bias,
        grad_b_down,
        grad_b_up,
    ) = [vector.reshape(-1) for vector in vectors]
    return (
        block_out,
        target_grad,
        memory_grad,
        grad_norm1_gain,
        grad_norm1_bias,
        grad_w_qkv,
        grad_w_out,
        grad_norm2_gain,
        grad_norm2_bias,
        grad_w_cross_q,
        grad_w_cross_kv,
        grad_w_cross_out,
        grad_norm3_gain,
        grad_norm3_bias,
        grad_w_up,
        grad_b_up,
        grad_w_down,
        grad_b_down,
    )


def solution(mesh):
    token = P("dp", "blk", None)
    code = P("dp", "blk")
    return jax.shard_map(
        functools.partial(body, mesh.shape["dp"], mesh.shape["blk"]),
        mesh=mesh,
        in_specs=(token, token, code, code, code, code, token) + (P(),) * 15,
        out_specs=(token, token, token) + (P(),) * 15,
        check_vma=False,
    )
```

```python
import functools
import math

import jax
import jax.numpy as jnp
from jax import lax
from jax.experimental import pallas as pl
from jax.experimental.pallas import tpu as pltpu
from jax.sharding import PartitionSpec as P

HEADS = 8
NT = (((1,), (1,)), ((), ()))
NN = (((1,), (0,)), ((), ()))
TN = (((0,), (0,)), ((), ()))
f32 = jnp.float32
bf16 = jnp.bfloat16
VMEM = 60 * 1024 * 1024
SMALL = pl.CostEstimate(flops=1, bytes_accessed=1, transcendentals=0)
QUERY_SCALE = 0.125 * math.log2(math.e)
HIDDEN_MASK = -1e30


def dot(left, right, dims=NN):
    return lax.dot_general(left, right, dims, preferred_element_type=f32)


def normalize(values):
    centered = values - jnp.mean(values, axis=1, keepdims=True)
    inverse = lax.rsqrt(jnp.mean(centered * centered, axis=1, keepdims=True) + 1e-05)
    return centered * inverse, inverse


def normalize_back(grad, normal, inverse, gain):
    grad = grad * gain
    shift = jnp.mean(grad, axis=1, keepdims=True)
    along = jnp.mean(grad * normal, axis=1, keepdims=True)
    return inverse * (grad - shift - normal * along)


def column_sums(values):
    return jnp.sum(values, axis=0, keepdims=True)


def whole(array, *index):
    shape = array.shape
    index = index or (0,) * len(shape)
    return pl.BlockSpec(shape, lambda *grid: index)


def shaped(shape, dtype=bf16):
    return jax.ShapeDtypeStruct(shape, dtype)


def run(kernel, name, operands, outs, place=None, scratch=()):
    specs = [whole(array) for array in operands]
    if place is not None:
        specs = [pl.BlockSpec(memory_space=pltpu.SMEM)] + specs
        operands = (place.reshape(1), *operands)
    return pl.pallas_call(
        kernel,
        grid=(1,),
        in_specs=specs,
        out_specs=[whole(out) for out in outs],
        out_shape=list(outs),
        scratch_shapes=list(scratch),
        compiler_params=pltpu.CompilerParams(vmem_limit_bytes=VMEM),
        cost_estimate=SMALL,
        name=name,
    )(*operands)


def hand_out(place, source_ref, out_refs):
    share, size = len(out_refs), out_refs[0].shape[0]
    for step, out_ref in enumerate(out_refs):
        start = pl.multiple_of((place + step) % share * size, size)
        out_ref[...] = source_ref[pl.ds(start, size), :]


def forward_kernel(parts, *refs):
    q_ref, qmask_ref = refs[:2]
    k_refs, v_refs, kmask_refs = (refs[2 + i * parts : 2 + (i + 1) * parts] for i in range(3))
    o_ref, lse_ref = refs[2 + 3 * parts :]
    low = lax.broadcasted_iota(jnp.int32, (1, 128), 1) < 64
    k = jnp.concatenate([ref[...] for ref in k_refs], 0)
    v = jnp.concatenate([ref[...] for ref in v_refs], 0)
    kmask = jnp.concatenate([ref[...] for ref in kmask_refs], 0)
    q, qmask = q_ref[...], qmask_ref[...]
    outputs = []
    both_scores = [
        dot(jnp.where(low, k, kmask), jnp.where(low, q, qmask), NT),
        dot(jnp.where(low, kmask, k), jnp.where(low, qmask, q), NT),
    ]
    for head, scores in enumerate(both_scores):
        mine = low if head == 0 else ~low
        largest = jnp.max(scores, axis=0, keepdims=True)
        weights = jnp.exp2(scores - largest).astype(bf16)
        both = dot(jnp.where(mine, v, jnp.ones_like(v)), weights, TN)
        total = both[64 - head * 64 : 65 - head * 64]
        lse_ref[0, head : head + 1, :] = largest + jnp.log2(total)
        outputs.append(both[head * 64 : head * 64 + 64] / total)
    o_ref[...] = jnp.concatenate(outputs, 0).T.astype(bf16)


def columns(rows, column, count):
    if callable(column):
        return [pl.BlockSpec((rows, 128), lambda h: (0, column(h)))] * count
    return [pl.BlockSpec((rows, 128), lambda h: (0, column))] * count


def attend(queries, qmask, keyvals, masks, mask_column):
    tokens, features = queries.shape
    parts = len(keyvals)
    length = parts * tokens
    pairs = features // 128
    of_queries = pl.BlockSpec((tokens, 128), lambda h: (0, h))
    return pl.pallas_call(
        functools.partial(forward_kernel, parts),
        grid=(pairs,),
        in_specs=[of_queries]
        + columns(tokens, 0, 1)
        + columns(tokens, lambda h: h, parts)
        + columns(tokens, lambda h: h + pairs, parts)
        + columns(tokens, mask_column, parts),
        out_specs=[of_queries, pl.BlockSpec((1, 2, tokens), lambda h: (h, 0, 0))],
        out_shape=[shaped((tokens, features)), shaped((pairs, 2, tokens), f32)],
        compiler_params=pltpu.CompilerParams(vmem_limit_bytes=VMEM),
        cost_estimate=SMALL,
        name="attend",
    )(queries, qmask, *keyvals, *keyvals, *masks)


def backward_kernel(parts, *refs):
    q_ref, qmask_ref, do_ref, o_ref, lse_ref = refs[:5]
    k_refs, v_refs, kmask_refs = (refs[5 + i * parts : 5 + (i + 1) * parts] for i in range(3))
    dq_ref, dkv_refs = refs[5 + 3 * parts], refs[6 + 3 * parts :]
    low = lax.broadcasted_iota(jnp.int32, (1, 128), 1) < 64
    q, qmask, grad = q_ref[...], qmask_ref[...], do_ref[...]
    tokens = q.shape[0]
    product = grad.astype(f32) * o_ref[...].astype(f32)
    upper = product.astype(bf16)
    lower = (product - upper.astype(f32)).astype(bf16)
    rows = lax.broadcasted_iota(jnp.int32, (8, 128), 0)
    lanes = lax.broadcasted_iota(jnp.int32, (8, 128), 1)
    pick = jnp.where(rows == lanes // 64, 1.0, 0.0).astype(bf16)
    delta = dot(pick, upper, NT) + dot(pick, lower, NT)
    lse = lse_ref[0]
    zero = jnp.zeros_like(grad)
    q_heads = [jnp.where(low, q, qmask), jnp.where(low, qmask, q)]
    grad_heads = [jnp.where(low, grad, zero), jnp.where(low, zero, grad)]
    dq = [jnp.zeros((64, tokens), f32)] * 2
    for part in range(parts):
        k, v = k_refs[part][...], v_refs[part][...]
        kmask = kmask_refs[part][...]
        dk, dv = [], []
        for head in range(2):
            k_head = jnp.where(low, k, kmask) if head == 0 else jnp.where(low, kmask, k)
            weights = jnp.exp2(dot(k_head, q_heads[head], NT) - lse[head : head + 1, :])
            grad_weights = dot(v, grad_heads[head], NT)
            grad_scores = (weights * (grad_weights - delta[head : head + 1, :])).astype(bf16)
            dv.append(dot(weights.astype(bf16), grad))
            dk.append(dot(grad_scores, q))
            dq[head] = dq[head] + dot(k, grad_scores, TN)[head * 64 : head * 64 + 64]
        dkv_refs[part][:, :128] = (jnp.where(low, dk[0], dk[1]) * math.log(2.0)).astype(bf16)
        dkv_refs[part][:, 128:] = jnp.where(low, dv[0], dv[1]).astype(bf16)
    dq_ref[...] = (jnp.concatenate(dq, 0).T * 0.125).astype(bf16)


def attend_back(queries, qmask, grad, outputs, lse, keyvals, masks, mask_column, first, count):
    tokens, features = queries.shape
    parts = len(keyvals)
    length = parts * tokens
    pairs = features // 128
    of_queries = pl.BlockSpec((tokens, 128), lambda h: (0, h + first))
    return pl.pallas_call(
        functools.partial(backward_kernel, parts),
        grid=(count,),
        in_specs=[
            of_queries,
            pl.BlockSpec((tokens, 128), lambda h: (0, 0)),
            of_queries,
            of_queries,
            pl.BlockSpec((1, 2, tokens), lambda h: (h + first, 0, 0)),
        ]
        + columns(tokens, lambda h: h + first, parts)
        + columns(tokens, lambda h: h + first + pairs, parts)
        + columns(tokens, mask_column, parts),
        out_specs=[pl.BlockSpec((tokens, 128), lambda h: (0, h))]
        + [pl.BlockSpec((tokens, 256), lambda h: (0, h))] * parts,
        out_shape=[shaped((tokens, count * 128))] + [shaped((tokens, count * 256))] * parts,
        compiler_params=pltpu.CompilerParams(vmem_limit_bytes=VMEM),
        cost_estimate=SMALL,
        name="attend_back",
    )(queries, qmask, grad, outputs, lse, *keyvals, *keyvals, *masks)


def mask_rows(codes, of_queries):
    places = lax.broadcasted_iota(jnp.int32, (128, codes.shape[1]), 0) % 64
    codes = jnp.broadcast_to(codes.astype(jnp.int32), places.shape)
    if of_queries:
        mask = jnp.where(codes % 4 == places, 1.0, 0.0)
    else:
        mask = jnp.where((codes != places) & (places < 3), HIDDEN_MASK, 0.0)
    return mask.T.astype(bf16)


def project_kernel(parts, length, *refs):
    x_refs = refs[:parts]
    gain_ref, bias_ref, w_ref, x_ref, normed_ref, query_ref, keyvals_ref, qmask_ref = refs[parts:]
    features = x_ref.shape[1]
    for part in range(parts):
        rows = slice(part * length, (part + 1) * length)
        low = x_refs[part][:length, :]
        x_ref[rows, :] = low
        normal, inverse = normalize(low.astype(f32))
        normed = (normal * gain_ref[...] + bias_ref[...]).astype(bf16)
        normed_ref[rows, :] = normed
        projected = dot(normed, w_ref[...])
        query_ref[rows, :] = (projected[:, :features] * QUERY_SCALE).astype(bf16)
        keyvals_ref[rows, : 2 * features] = projected[:, features:].astype(bf16)
        codes = x_refs[part][length : length + 16, :].astype(f32)[0:1, :]
        qmask_ref[rows, :] = mask_rows(codes[:, :length], True)
        keyvals_ref[rows, 2 * features : 2 * features + 128] = mask_rows(codes[:, :length], False)
        keyvals_ref[rows, 2 * features + 128 :] = mask_rows(codes[:, length : 2 * length], False)


def row_specs(array, count):
    shape = (1,) + array.shape[1:]
    return [
        pl.BlockSpec(shape, lambda i, row, step=step: ((row[0] + step) % count, 0, 0)) for step in range(count)
    ]


def pack_target(row, target, codes):
    count, length, features = target.shape

    def kernel(row_ref, *refs):
        seg_ref, keep_ref, memory_seg_ref, memory_keep_ref = refs[count : count + 4]
        for step in range(count):
            out_ref = refs[count + 4 + step]
            out_ref[:length, :] = refs[step][0]
            which = pl.ds((row_ref[0] + step) % count, 1)
            pieces = [
                jnp.where(keep[which, :] == 1, seg[which, :], seg[which, :] + 4).astype(f32)
                for seg, keep in ((seg_ref, keep_ref), (memory_seg_ref, memory_keep_ref))
            ]
            if features > 2 * length:
                pieces.append(jnp.zeros((1, features - 2 * length), f32))
            pieces = jnp.concatenate(pieces, 1)
            out_ref[length:, :] = jnp.broadcast_to(pieces, (16, features)).astype(bf16)

    out = shaped((length + 16, features))
    return pl.pallas_call(
        kernel,
        grid_spec=pltpu.PrefetchScalarGridSpec(
            num_scalar_prefetch=1,
            grid=(1,),
            in_specs=row_specs(target, count) + [whole(item) for item in codes],
            out_specs=[whole(out)] * count,
        ),
        out_shape=[out] * count,
        compiler_params=pltpu.CompilerParams(vmem_limit_bytes=VMEM),
        cost_estimate=SMALL,
        name="pack_target",
    )(row.reshape(1), *[target] * count, *codes)


def pack_rows(row, arrays):
    count, length, features = arrays[0].shape
    total = count * len(arrays)

    def kernel(row_ref, *refs):
        for i in range(total):
            refs[total + i][...] = refs[i][0]

    out = shaped((length, features), arrays[0].dtype)
    outs = pl.pallas_call(
        kernel,
        grid_spec=pltpu.PrefetchScalarGridSpec(
            num_scalar_prefetch=1,
            grid=(1,),
            in_specs=[spec for array in arrays for spec in row_specs(array, count)],
            out_specs=[whole(out)] * total,
        ),
        out_shape=[out] * total,
        compiler_params=pltpu.CompilerParams(vmem_limit_bytes=VMEM),
        cost_estimate=SMALL,
        name="pack_rows",
    )(row.reshape(1), *[array for array in arrays for _ in range(count)])
    return [tuple(outs[i : i + count]) for i in range(0, total, count)]


def place_rows(row, parts):
    count = len(parts)
    length, features = parts[0].shape

    def kernel(row_ref, *refs):
        for step in range(count):
            refs[count][pl.ds((row_ref[0] + step) % count, 1), :, :] = refs[step][...].astype(f32)[None]

    out = shaped((count, length, features), f32)
    return pl.pallas_call(
        kernel,
        grid_spec=pltpu.PrefetchScalarGridSpec(
            num_scalar_prefetch=1,
            grid=(1,),
            in_specs=[whole(part) for part in parts],
            out_specs=whole(out),
        ),
        out_shape=out,
        compiler_params=pltpu.CompilerParams(vmem_limit_bytes=VMEM),
        cost_estimate=SMALL,
        name="place_rows",
    )(row.reshape(1), *parts)


def unpack_feed(place, parts, hidden, block):
    share = len(parts)
    features = parts[0].shape[1]
    steps = hidden // block
    each = steps // share

    def kernel(place_ref, *refs):
        up_ref, down_ref = refs[share:]
        owner = pl.program_id(0) // each
        for step in range(share):

            @pl.when((place_ref[0] + share - owner) % share == step)
            def _():
                up_ref[...] = refs[step][:features, :].astype(f32)
                down_ref[...] = refs[step][features:, :].astype(f32)

    return pl.pallas_call(
        kernel,
        grid_spec=pltpu.PrefetchScalarGridSpec(
            num_scalar_prefetch=1,
            grid=(steps,),
            in_specs=[pl.BlockSpec((2 * features, features), lambda j, place: (j % each, 0))] * share,
            out_specs=[
                pl.BlockSpec((features, block), lambda j, place: (0, j)),
                pl.BlockSpec((block, features), lambda j, place: (j, 0)),
            ],
        ),
        out_shape=[shaped((features, hidden), f32), shaped((hidden, features), f32)],
        compiler_params=pltpu.CompilerParams(vmem_limit_bytes=VMEM),
        cost_estimate=SMALL,
        name="unpack_feed",
    )(place.reshape(1), *parts)


def unpack_columns(place, parts, widths, vectors):
    share = len(parts)
    rows = parts[0].shape[0]
    last = sum(widths)

    def kernel(place_ref, *refs):
        for step in range(share):

            @pl.when((place_ref[0] + share - pl.program_id(0)) % share == step)
            def _():
                start = 0
                for width, out_ref in zip(widths, refs[share:]):
                    out_ref[...] = refs[step][:, start : start + width].astype(f32)
                    start += width

                if not vectors:
                    return

                @pl.when(pl.program_id(0) == 0)
                def _():
                    line = 0
                    values = refs[step][:64, last:].astype(f32)
                    for length, out_ref in zip(vectors, refs[share + len(widths) :]):
                        for i in range(0, length, 128):
                            out_ref[:, i : i + 128] = values[line : line + 1, :]
                            line += 1

    return pl.pallas_call(
        kernel,
        grid_spec=pltpu.PrefetchScalarGridSpec(
            num_scalar_prefetch=1,
            grid=(share,),
            in_specs=[pl.BlockSpec(part.shape, lambda j, place: (0, 0)) for part in parts],
            out_specs=[pl.BlockSpec((rows, width), lambda j, place: (j, 0)) for width in widths]
            + [pl.BlockSpec((1, length), lambda j, place: (0, 0)) for length in vectors],
        ),
        out_shape=[shaped((share * rows, width), f32) for width in widths]
        + [shaped((1, length), f32) for length in vectors],
        compiler_params=pltpu.CompilerParams(vmem_limit_bytes=VMEM),
        cost_estimate=SMALL,
        name="unpack_columns",
    )(place.reshape(1), *parts)


def memory_kernel(parts, *refs):
    part_refs = refs[:parts]
    w_ref, memory_ref, keyvals_ref = refs[parts:]
    length = part_refs[0].shape[0]
    for part in range(parts):
        rows = slice(part * length, (part + 1) * length)
        memory = part_refs[part][...]
        memory_ref[rows, :] = memory
        keyvals_ref[rows, :] = dot(memory, w_ref[...]).astype(bf16)


def after_self_kernel(x_ref, attended_ref, w_out_ref, gain_ref, bias_ref, w_q_ref, after_ref, normed_ref, query_ref):
    after = x_ref[...].astype(f32) + dot(attended_ref[...], w_out_ref[...])
    after_ref[...] = after.astype(bf16)
    normal, inverse = normalize(after)
    normed = (normal * gain_ref[...] + bias_ref[...]).astype(bf16)
    normed_ref[...] = normed
    query_ref[...] = (dot(normed, w_q_ref[...]) * QUERY_SCALE).astype(bf16)


def feed_kernel(parts, share, each, place_ref, *refs):
    after_ref, attended_ref, w_out_ref, gain_ref, bias_ref, w_up_ref, b_up_ref, w_down_ref, b_down_ref = refs[:9]
    cotangent_refs, refs = refs[9 : 9 + parts], refs[9 + parts :]
    out_refs, grad_w_refs, refs = refs[:parts], refs[parts : parts + share], refs[parts + share :]
    grad_ref, grad_heads_ref, grad_out_ref, grad_b_up_ref, sums_ref = refs[:5]
    normed_ref, x_ref, total_ref, back_ref, cotangent_ref = refs[5:]
    features = w_up_ref.shape[0]
    length = out_refs[0].shape[0]
    step = pl.program_id(0)

    @pl.when(step == 0)
    def _():
        for part, part_ref in enumerate(cotangent_refs):
            cotangent_ref[part * length : (part + 1) * length, :] = part_ref[...]
        x = after_ref[...].astype(f32) + dot(attended_ref[...], w_out_ref[...])
        x_ref[...] = x
        total_ref[...] = x + b_down_ref[...]
        normal, inverse = normalize(x)
        normed_ref[...] = (normal * gain_ref[...] + bias_ref[...]).astype(bf16)
        back_ref[...] = jnp.zeros_like(back_ref)

    cotangent = cotangent_ref[...]
    normed, w_up, w_down = normed_ref[...], w_up_ref[...], w_down_ref[...]
    u = dot(normed, w_up) + b_up_ref[...]
    slope = math.sqrt(2.0 / math.pi)
    squared = u * u
    bent = jnp.tanh(u * (slope + slope * 0.044715 * squared))
    half = 0.5 + 0.5 * bent
    activated = (u * half).astype(bf16)
    gelu_slope = half + (0.5 * u) * (1.0 - bent * bent) * (slope + 3.0 * slope * 0.044715 * squared)
    total_ref[...] += dot(activated, w_down)
    grad_hidden = (dot(cotangent, w_down, NT) * gelu_slope).astype(bf16)
    grad_up = dot(normed, grad_hidden, TN).astype(bf16)
    grad_down = dot(activated, cotangent, TN).astype(bf16)
    for part, grad_w_ref in enumerate(grad_w_refs):

        @pl.when(step // each == share - 1 - part)
        def _():
            for i in range(0, grad_up.shape[1], features):
                grad_w_ref[2 * i : 2 * i + features, :] = grad_up[:, i : i + features]
                grad_w_ref[2 * i + features : 2 * i + 2 * features, :] = grad_down[i : i + features, :]

    grad_b_up_ref[...] = column_sums(grad_hidden.astype(f32))
    back_ref[...] += dot(grad_hidden, w_up, NT)

    @pl.when(step == pl.num_programs(0) - 1)
    def _():
        for part, out_ref in enumerate(out_refs):
            out_ref[...] = total_ref[part * length : (part + 1) * length, :].astype(bf16)
        normal, inverse = normalize(x_ref[...])
        grad_normed = back_ref[...]
        grad_out = cotangent.astype(f32)
        sums_ref[0:1, :] = column_sums(grad_normed * normal)
        sums_ref[1:2, :] = column_sums(grad_normed)
        sums_ref[2:3, :] = column_sums(grad_out)
        grad = grad_out + normalize_back(grad_normed, normal, inverse, gain_ref[...])
        low = grad.astype(bf16)
        grad_ref[...] = low
        grad_heads_ref[...] = dot(low, w_out_ref[...], NT).astype(bf16)
        grad_out_ref[...] = dot(attended_ref[...], low, TN).astype(bf16)


def feed_forward(place, share, after_self, attended, cotangents, w_out, gain, bias, w_up, b_up, w_down, b_down):
    tokens, features = after_self.shape
    hidden = w_up.shape[1]
    block = features * (1 if hidden // features // share % 2 else 2)
    parts = len(cotangents)
    length = tokens // parts
    steps = hidden // block
    each = steps // share
    row, one, square = shaped((tokens, features)), shaped((1, features)), shaped((features, features))
    part_row = shaped((length, features))

    def now(j, place):
        return ((place[0] + share - 1 - j // each) % share) * each + j % each

    def grad_spec(part):
        begin = (share - 1 - part) * each
        return pl.BlockSpec(
            (2 * block, features), lambda j, place: (jnp.clip(j - begin, 0, each - 1), 0)
        )

    return pl.pallas_call(
        functools.partial(feed_kernel, parts, share, each),
        grid_spec=pltpu.PrefetchScalarGridSpec(
            num_scalar_prefetch=1,
            grid=(steps,),
            in_specs=[
                whole(row),
                whole(row),
                whole(square),
                whole(one),
                whole(one),
                pl.BlockSpec((features, block), lambda j, place: (0, now(j, place))),
                pl.BlockSpec((1, block), lambda j, place: (0, now(j, place))),
                pl.BlockSpec((block, features), lambda j, place: (now(j, place), 0)),
                whole(one),
            ]
            + [whole(part_row)] * parts,
            out_specs=[whole(part_row)] * parts
            + [grad_spec(part) for part in range(share)]
            + [
                whole(row),
                whole(row),
                whole(square),
                pl.BlockSpec((1, block), lambda j, place: (0, now(j, place))),
                whole(shaped((8, features))),
            ],
            scratch_shapes=[
                pltpu.VMEM((tokens, features), bf16),
                pltpu.VMEM((tokens, features), f32),
                pltpu.VMEM((tokens, features), f32),
                pltpu.VMEM((tokens, features), f32),
                pltpu.VMEM((tokens, features), bf16),
            ],
        ),
        out_shape=[part_row] * parts
        + [shaped((each * 2 * block, features))] * share
        + [
            row,
            row,
            square,
            shaped((1, hidden), f32),
            shaped((8, features), f32),
        ],
        compiler_params=pltpu.CompilerParams(vmem_limit_bytes=VMEM),
        cost_estimate=SMALL,
        name="feed_forward",
    )(place.reshape(1), after_self, attended, w_out, gain, bias, w_up, b_up, w_down, b_down, *cotangents)


def after_self_back_kernel(calls, *refs):
    dq_refs = refs[:calls]
    after_ref, normed_ref, attended_ref, grad_after_ref, gain_ref, w_q_ref, w_out_ref = refs[calls : calls + 7]
    grad_ref, grad_heads_ref, grad_w_ref, sums_ref = refs[calls + 7 :]
    features = after_ref.shape[1]
    grad_query = jnp.concatenate([ref[...] for ref in dq_refs], 1)
    grad_normed = dot(grad_query, w_q_ref[...], NT)
    normal, inverse = normalize(after_ref[...].astype(f32))
    sums_ref[0:1, :] = column_sums(grad_normed * normal)
    sums_ref[1:2, :] = column_sums(grad_normed)
    grad = grad_after_ref[...].astype(f32) + normalize_back(grad_normed, normal, inverse, gain_ref[...])
    low = grad.astype(bf16)
    grad_ref[...] = low
    grad_heads_ref[...] = dot(low, w_out_ref[...], NT).astype(bf16)
    grad_w_ref[:, :features] = dot(normed_ref[...], grad_query, TN).astype(bf16)
    grad_w_ref[:, features:] = dot(attended_ref[...], low, TN).astype(bf16)


def summed_keyvals(refs):
    keys, values = [], []
    for call in refs:
        total = sum([ref[...].astype(f32) for ref in call[1:]], call[0][...].astype(f32)).astype(bf16)
        for pair in range(total.shape[1] // 256):
            keys.append(total[:, pair * 256 : pair * 256 + 128])
            values.append(total[:, pair * 256 + 128 : pair * 256 + 256])
    return keys + values


def memory_back_kernel(calls, parts, place_ref, *refs):
    *refs, sum_ref = refs
    grad_refs = [refs[call * parts : (call + 1) * parts] for call in range(calls)]
    memory_ref, w_ref, out_ref, pair_ref = refs[calls * parts : calls * parts + 4]
    grad_w_refs = refs[calls * parts + 4 : calls * parts + 4 + parts]
    row_refs = refs[calls * parts + 4 + parts :]
    features = out_ref.shape[1]
    grad = jnp.concatenate(summed_keyvals(grad_refs), 1)
    result = dot(grad, w_ref[...], NT).astype(bf16)
    length = row_refs[0].shape[0]
    for part, row_ref in enumerate(row_refs):
        row_ref[...] = result[part * length : (part + 1) * length, :]
    sum_ref[:, :features] = out_ref[...]
    sum_ref[:, features : 3 * features] = pair_ref[...]
    sum_ref[:, 3 * features :] = dot(memory_ref[...], grad, TN).astype(bf16)
    hand_out(place_ref[0], sum_ref, grad_w_refs)


def project_back_kernel(calls, parts, place_ref, *refs):
    *refs, sum_ref = refs
    dq_refs = refs[:calls]
    refs = refs[calls:]
    grad_refs = [refs[call * parts : (call + 1) * parts] for call in range(calls)]
    refs = refs[calls * parts :]
    x_ref, normed_ref, gain_ref, w_ref, grad_after_ref, second_ref, third_ref, b_up_ref = refs[:8]
    grad_w_refs, row_refs = refs[8 : 8 + parts], refs[8 + parts :]
    grad = jnp.concatenate([ref[...] for ref in dq_refs] + summed_keyvals(grad_refs), 1)
    features = x_ref.shape[1]
    sum_ref[:, : 3 * features] = dot(normed_ref[...], grad, TN).astype(bf16)
    grad_normed = dot(grad, w_ref[...], NT)
    normal, inverse = normalize(x_ref[...].astype(f32))
    result = grad_after_ref[...].astype(f32) + normalize_back(grad_normed, normal, inverse, gain_ref[...])
    length = row_refs[0].shape[0]
    for part, row_ref in enumerate(row_refs):
        row_ref[...] = result[part * length : (part + 1) * length, :].astype(bf16)
    pieces = [column_sums(grad_normed * normal), column_sums(grad_normed), second_ref[0:1, :], second_ref[1:2, :]]
    pieces += [third_ref[0:1, :], third_ref[1:2, :], third_ref[2:3, :]]
    pieces += [b_up_ref[:, i : i + features] for i in range(0, b_up_ref.shape[1], features)]
    lines = [piece[:, i : i + 128] for piece in pieces for i in range(0, features, 128)]
    lines.append(jnp.zeros((features - len(lines), 128), f32))
    sum_ref[:, 3 * features :] = jnp.concatenate(lines, 0).astype(bf16)
    hand_out(place_ref[0], sum_ref, grad_w_refs)


class Layout:
    def __init__(self, dp, rows, blocks):
        self.rows = rows
        self.share = share = blocks // rows
        self.blocks = blocks
        self.dp = dp
        place = lax.axis_index("blk")
        self.row = place // share
        self.place = lax.rem(place, share)
        self.device = lax.axis_index("dp") * blocks + place

    def shift_rows(self, step):
        rows, share = self.rows, self.share
        return [
            (a * share + b, ((a + step) % rows) * share + b) for a in range(rows) for b in range(share)
        ]

    def shift_share(self, step):
        rows, share = self.rows, self.share
        return [
            (a * share + b, a * share + (b + step) % share) for a in range(rows) for b in range(share)
        ]

    def bring_rows(self, parts):
        return (parts[0],) + tuple(
            lax.ppermute(parts[step], "blk", self.shift_rows(step)) for step in range(1, self.rows)
        )

    def return_row(self, parts, step):
        arrived = lax.ppermute(parts[step], "blk", self.shift_rows(self.rows - step))
        return (*parts[:step], arrived, *parts[step + 1 :])

    def gather_share(self, values):
        return (values,) + tuple(
            lax.ppermute(values, "blk", self.shift_share(step)) for step in range(1, self.share)
        )

    def return_share(self, parts):
        return (parts[0],) + tuple(
            lax.ppermute(parts[step], "blk", self.shift_share(self.share - step))
            for step in range(1, self.share)
        )


class Sum:
    def __init__(self, layout, values, halves=True):
        share, rows, dp, blocks = layout.share, layout.rows, layout.dp, layout.blocks
        self.layout = layout
        self.parts = values if isinstance(values, tuple) else None
        self.values = (values,)
        own = (share, layout.place, layout.shift_share)
        row = (rows, layout.row, layout.shift_rows)
        bits = [blocks << bit for bit in range((dp - 1).bit_length())]
        bits = list(zip(bits, bits[1:] + bits[:1]))
        self.left = [(self.scatter,) + own]
        self.left += [(self.halve,) + pair for pair in bits] if halves else [(self.scatter_far,)]
        self.left += [(self.scatter,) + row, (self.gather,) + row]
        self.left += [(self.double,) + pair for pair in reversed(bits)]
        self.left += [(self.gather,) + own]

    def part(self, start, size):
        items = [lax.dynamic_slice_in_dim(item, start, size, 0).astype(f32) for item in self.values]
        return sum(items[1:], items[0]).astype(bf16)

    def scatter(self, count, index, shift):
        parts = self.parts
        self.parts = None
        if parts is None:
            size = self.values[0].shape[0] // count
            parts = [self.part(lax.rem(index + step, count) * size, size) for step in range(count)]
        arrived = [lax.ppermute(parts[step], "blk", shift(step)) for step in range(1, count)]
        self.values = (parts[0], *arrived)

    def scatter_far(self):
        dp, device = self.layout.dp, self.layout.device
        count = (dp - 1).bit_length()
        size = self.values[0].shape[0] // dp
        place = device // self.layout.blocks

        def part(step):
            whose = lax.rem(place + step, dp)
            even = sum(((whose >> bit) & 1) << (count - 1 - bit) for bit in range(count))
            odd = sum(((whose >> ((bit + 1) % count)) & 1) << (count - 1 - bit) for bit in range(count))
            return self.part(jnp.where(device % 2 == 0, even, odd) * size, size)

        arrived = [
            lax.ppermute(part(step), "dp", [(d, (d + step) % dp) for d in range(dp)]) for step in range(1, dp)
        ]
        self.values = (part(0), *arrived)

    def gather(self, count, index, shift):
        mine = self.part(0, self.values[0].shape[0])
        part_rows = mine.shape[0]
        arrived = [lax.ppermute(mine, "blk", shift(step)) for step in range(1, count)]
        if not self.left:
            self.values = (mine, *arrived)
            return
        result = jnp.zeros((count * part_rows, mine.shape[1]), mine.dtype)
        result = lax.dynamic_update_slice_in_dim(result, mine, index * part_rows, 0)
        for step, item in enumerate(arrived, 1):
            source = lax.rem(index + count - step, count)
            result = lax.dynamic_update_slice_in_dim(result, item, source * part_rows, 0)
        self.values = (result,)

    def exchange(self, values, even, odd):
        pairs = [(d, d ^ (odd if d % 2 else even)) for d in range(self.layout.dp * self.layout.blocks)]
        return lax.ppermute(values, ("dp", "blk"), pairs)

    def upper(self, even, odd):
        device = self.layout.device
        return (device & jnp.where(device % 2 == 0, even, odd)) != 0

    def halve(self, even, odd):
        half = self.values[0].shape[0] // 2
        upper = self.upper(even, odd).astype(jnp.int32)
        send = self.part((1 - upper) * half, half)
        self.values = (self.part(upper * half, half), self.exchange(send, even, odd))

    def double(self, even, odd):
        (mine,) = self.values
        arrived = self.exchange(mine, even, odd)
        self.values = (
            jnp.where(
                self.upper(even, odd), jnp.concatenate([arrived, mine], 0), jnp.concatenate([mine, arrived], 0)
            ),
        )

    def step(self):
        if self.left:
            action = self.left.pop(0)
            action[0](*action[1:])


def beside(sums, kernel, operands, *others):
    for running in sums:
        running.step()
    result, operands, others, values = join(
        kernel(*operands), operands, others, [running.values for running in sums]
    )
    for running, value in zip(sums, values):
        running.values = value
    return result, operands, *others


def join(*values):
    return lax.optimization_barrier(values)


def body(
    dp,
    blocks,
    target,
    memory,
    target_seg,
    target_keep,
    memory_seg,
    memory_keep,
    cotangent,
    norm1_gain,
    norm1_bias,
    w_qkv,
    w_out,
    norm2_gain,
    norm2_bias,
    w_cross_q,
    w_cross_kv,
    w_cross_out,
    norm3_gain,
    norm3_bias,
    w_up,
    b_up,
    w_down,
    b_down,
):
    rows, length, features = target.shape
    tokens = rows * length
    layout = Layout(dp, rows, blocks)
    target_parts = pack_target(layout.row, target, (target_seg, target_keep, memory_seg, memory_keep))
    target_parts = layout.bring_rows(target_parts)
    memory_parts, cotangent_parts = pack_rows(layout.row, (memory, cotangent))
    norm1_gain, norm1_bias, norm2_gain, norm2_bias, norm3_gain, norm3_bias, b_up, b_down = (
        item.reshape(1, -1)
        for item in (norm1_gain, norm1_bias, norm2_gain, norm2_bias, norm3_gain, norm3_bias, b_up, b_down)
    )
    hidden = w_up.shape[1]
    row, wide_row = shaped((tokens, features)), shaped((tokens, 2 * features))
    row_parts = (shaped((length, features)),) * rows
    sums = shaped((8, features), f32)
    pairs = features // 128

    x, normed1, queries, keyvals, qmask = run(
        functools.partial(project_kernel, rows, length),
        "project",
        target_parts + (norm1_gain, norm1_bias, w_qkv),
        (row, row, row, shaped((tokens, 2 * features + 256)), shaped((tokens, 128))),
    )
    keyvals, memory_parts = join(keyvals, memory_parts)
    keyvals = layout.gather_share(keyvals)
    memory_parts = layout.bring_rows(memory_parts)
    self_masks = (keyvals, 2 * pairs)
    cross_masks = (keyvals, 2 * pairs + 1)
    self_low, self_lse = attend(queries, qmask, keyvals, *self_masks)
    self_low, memory_parts, cotangent_parts = join(self_low, memory_parts, cotangent_parts)
    memory_row, memory_keyvals = run(
        functools.partial(memory_kernel, rows), "memory", memory_parts + (w_cross_kv,), (row, wide_row)
    )
    memory_keyvals = layout.gather_share(memory_keyvals)
    after_self, normed2, cross_query = run(
        after_self_kernel,
        "after_self",
        (x, self_low, w_out, norm2_gain, norm2_bias, w_cross_q),
        (row, row, row),
    )
    cross_query, cotangent_parts, memory_keyvals = join(cross_query, cotangent_parts, memory_keyvals)
    cotangent_parts = layout.bring_rows(cotangent_parts)
    cross_low, cross_lse = attend(cross_query, qmask, memory_keyvals, *cross_masks)
    cross_low, cotangent_parts = join(cross_low, cotangent_parts)
    fed = feed_forward(
        layout.place,
        layout.share,
        after_self,
        cross_low,
        cotangent_parts,
        w_cross_out,
        norm3_gain,
        norm3_bias,
        w_up,
        b_up,
        w_down,
        b_down,
    )
    block_parts, grad_feed = tuple(fed[:rows]), tuple(fed[rows : rows + layout.share])
    grad_after_cross, grad_cross_heads, grad_w_cross_out, grad_b_up, sums3 = fed[rows + layout.share :]

    first = Sum(layout, grad_feed, halves=False)
    calls = 2

    def back(masks, call):
        count = pairs // calls
        return lambda *operands: attend_back(*operands, *masks, call * count, count)

    operands = (cross_query, qmask, grad_cross_heads, cross_low, cross_lse, memory_keyvals)
    for step in range(1, rows - 1):
        block_parts = layout.return_row(block_parts, step)
    grads, operands, block_parts = beside([first], back(cross_masks, 0), operands, block_parts)
    cross_grads, share = [grads[0]], layout.return_share(grads[1:])
    block_parts = layout.return_row(block_parts, rows - 1)
    grads, operands, share, block_parts = beside([first], back(cross_masks, 1), operands, share, block_parts)
    cross_grads.append(grads[0])
    cross_share = list(share) + list(layout.return_share(grads[1:]))
    (grad_after_self, grad_self_heads, grad_w_pair, sums2), _, cross_share = beside(
        [first],
        lambda *operands: run(
            functools.partial(after_self_back_kernel, calls),
            "after_self_back",
            operands,
            (row, row, shaped((features, 2 * features)), sums),
        ),
        tuple(cross_grads) + (after_self, normed2, self_low, grad_after_cross, norm2_gain, w_cross_q, w_out),
        cross_share,
    )
    share = layout.share
    part = shaped((features // share, 5 * features))
    outs, _, grad_self_heads = beside(
        [first],
        lambda *operands: run(
            functools.partial(memory_back_kernel, calls, share),
            "memory_back",
            operands,
            (part,) * share + row_parts,
            layout.place,
            [pltpu.VMEM((features, 5 * features), bf16)],
        ),
        tuple(cross_share) + (memory_row, w_cross_kv, grad_w_cross_out, grad_w_pair),
        grad_self_heads,
    )
    middle = Sum(layout, tuple(outs[:share]))

    calls = 4
    operands = (queries, qmask, grad_self_heads, self_low, self_lse, keyvals)
    memory_parts = tuple(outs[share:])
    self_grads, self_share, sent = [], [], ()
    for call in range(calls):
        if call + 1 < rows:
            memory_parts = layout.return_row(memory_parts, call + 1)
        if call == 1:
            first.step()
        grads, operands, sent, memory_parts, *late = beside(
            [middle] if call in (1, 2) else [first, middle],
            back(self_masks, call),
            operands,
            sent,
            memory_parts,
            *([first.values] if call == 2 else []),
        )
        if late:
            first.values = late[0]
        self_grads.append(grads[0])
        self_share += sent
        sent = layout.return_share(grads[1:])
    self_share += sent
    self_share = join(self_share, self_grads)[0]
    part = shaped((features // share, 3 * features + 128))
    outs, _ = beside(
        [first],
        lambda *operands: run(
            functools.partial(project_back_kernel, calls, share),
            "project_back",
            operands,
            (part,) * share + row_parts,
            layout.place,
            [pltpu.VMEM((features, 3 * features + 128), bf16)],
        ),
        tuple(self_grads)
        + tuple(self_share)
        + (x, normed1, norm1_gain, w_qkv, grad_after_self, sums2, sums3, grad_b_up),
    )
    last = Sum(layout, tuple(outs[:share]))
    target_parts = tuple(outs[share:])
    while first.left:
        first.step()
    far = rows // 2
    ready = []

    def placed(*parts):
        return place_rows(layout.row, parts)

    for steps in [(), (far,), [step for step in range(1, rows) if step != far]]:
        for step in steps:
            target_parts = layout.return_row(target_parts, step)
        taken = block_parts if steps == (far,) else memory_parts if steps else ()
        job = placed if taken else lambda: ()
        result, _, *late = beside([last, middle], job, taken, *([target_parts] if steps else []))
        target_parts = late[0] if steps else target_parts
        if taken:
            ready.append(result)

    block_out, memory_grad = ready
    target_grad, _ = beside([last, middle], placed, target_parts)
    while middle.left:
        middle.step()
    (grad_w_cross_out, grad_w_cross_q, grad_w_out, grad_w_cross_kv), _ = beside(
        [last],
        lambda *parts: unpack_columns(layout.place, parts, [features, features, features, 2 * features], []),
        middle.values,
    )
    last.step()
    (grad_w_up, grad_w_down), _ = beside(
        [last], lambda *parts: unpack_feed(layout.place, parts, hidden, features), first.values
    )
    while last.left:
        last.step()
    grad_w_qkv, *vectors = unpack_columns(layout.place, last.values, [3 * features], [features] * 7 + [hidden])
    (
        grad_norm1_gain,
        grad_norm1_bias,
        grad_norm2_gain,
        grad_norm2_bias,
        grad_norm3_gain,
        grad_norm3_bias,
        grad_b_down,
        grad_b_up,
    ) = [vector.reshape(-1) for vector in vectors]
    return (
        block_out,
        target_grad,
        memory_grad,
        grad_norm1_gain,
        grad_norm1_bias,
        grad_w_qkv,
        grad_w_out,
        grad_norm2_gain,
        grad_norm2_bias,
        grad_w_cross_q,
        grad_w_cross_kv,
        grad_w_cross_out,
        grad_norm3_gain,
        grad_norm3_bias,
        grad_w_up,
        grad_b_up,
        grad_w_down,
        grad_b_down,
    )


def solution(mesh):
    token = P("dp", "blk", None)
    code = P("dp", "blk")
    return jax.shard_map(
        functools.partial(body, mesh.shape["dp"], mesh.shape["blk"]),
        mesh=mesh,
        in_specs=(token, token, code, code, code, code, token) + (P(),) * 15,
        out_specs=(token, token, token) + (P(),) * 15,
        check_vma=False,
    )
```
